128 devices in a mesh: ep: 16 (over x, z), tp: 8 (over y, core).
Axes of the slice: x: 4, y: 4, z: 4, core: 2. Of those that a mesh axis runs over, the one named last changes fastest.
Arguments:
- layer_input: float32 [16384, 1024], P(('ep', 'tp')), may hold values from -6 to 6
- lengths: int32 [16], replicated, may hold values from 1024 to 1024, as said below
- routes: int32 [16384, 8], replicated, may hold values from 0 to 31, all different within a row; in each aligned block of 128 rows (0 to 127, 128 to 255, ...) at most 48 rows name the same one
- norm_gain: float32 [1024], replicated, may hold values from 0.5 to 1.5
- w_query: bfloat16 [1024, 1024], P(None, 'tp'), may hold values from -0.1875 to 0.1875
- w_keyval: bfloat16 [1024, 8, 128], P(None, 'tp'), may hold values from -0.1875 to 0.1875
- query_gain: float32 [1024], P('tp'), may hold values from 0.5 to 1.5
- key_gain: float32 [512], P('tp'), may hold values from 0.5 to 1.5
- w_out: bfloat16 [1024, 1024], P('tp'), may hold values from -3.5 to 3.5
- mlp_gain: float32 [1024], replicated, may hold values from 0.5 to 1.5
- w_router: float32 [1024, 32], replicated, may hold values from -0.09375 to 0.09375
- w_gate: bfloat16 [32, 1024, 512], P('ep', None, 'tp'), may hold values from -0.1875 to 0.1875
- w_up: bfloat16 [32, 1024, 512], P('ep', None, 'tp'), may hold values from -0.1875 to 0.1875
- w_down: bfloat16 [32, 512, 1024], P('ep', 'tp'), may hold values from -0.75 to 0.75
- cotangent: float32 [16384, 1024], P(('ep', 'tp')), may hold values from -6 to 6
Outputs:
- output: float32 [16384, 1024], P(('ep', 'tp'))
- grad_input: float32 [16384, 1024], P(('ep', 'tp'))
- loss: float32 [], replicated
- grad_norm_gain: float32 [1024], replicated
- grad_query: float32 [1024, 1024], P(None, 'tp')
- grad_keyval: float32 [1024, 8, 128], P(None, 'tp')
- grad_query_gain: float32 [1024], P('tp')
- grad_key_gain: float32 [512], P('tp')
- grad_out: float32 [1024, 1024], P('tp')
- grad_mlp_gain: float32 [1024], replicated
- grad_router: float32 [1024, 32], replicated
- grad_gate: float32 [32, 1024, 512], P('ep', None, 'tp')
- grad_up: float32 [32, 1024, 512], P('ep', None, 'tp')
- grad_down: float32 [32, 512, 1024], P('ep', 'tp')
The draws below stay inside these ranges and needn't reach their ends.
Inputs may be any that keep to these rules, and one draw needn't show every extreme that they name: `lengths`: each group's slots hold one sequence from place 0, of the given length; the rest are padding; some group is full. Each token names 8 different experts; among the routes of the 128 tokens of one device no expert is named more than 48 times, a bound that some block reaches.
All inputs are finite; a program needn't handle non-finite values.
Results may differ from the reference program's by a relative error of at most 0.028.
Values may be sent and summed in bfloat16 or wider, within the bound.
A program may use at most 128 MiB of HBM per device.

```python
import math
import jax
import jax.numpy as jnp
import numpy as np
from jax import lax

D = 1024
HEADS = 16
KV_HEADS = 8
HEAD_DIM = 64
FF = 512
TOP = 8
TOK_DEV = 128
LEN_MIN = 1024
EXPERTS = 32
GRP = 1024
TOKENS = 16384
CAP = 48
N_EP = 16
N_TP = 8


def draw_lengths(key, part):
    key = jax.random.fold_in(key, 7)
    pick_key, base_key = jax.random.split(key)
    shortest = min(LEN_MIN, GRP)
    drawn = jax.random.randint(base_key, (N_EP,), shortest, GRP + 1)
    full_one = jax.random.randint(pick_key, (), 0, N_EP)
    return jnp.where(jnp.arange(N_EP) == full_one, GRP, drawn).astype(jnp.int32)


def block_scale(stream_key, dims, pieces, least, top_value):
    def one(axis_at, shards_of):
        steps = jax.random.uniform(jax.random.fold_in(jax.random.fold_in(stream_key, 6), axis_at), (shards_of,), jnp.float32, least / len(pieces), top_value / len(pieces))
        return jnp.repeat(jnp.exp(steps), dims[axis_at] // shards_of).reshape((-1,) + (1,) * (len(dims) - axis_at - 1))

    factor_of = one(*pieces[0])
    for cut in pieces[1:]:
        factor_of = factor_of * one(*cut)
    return factor_of


def routed_block(stream_key, own, number, rows, count, top, bound, lean):
    sequence = jax.random.permutation(stream_key, count)
    packed, common = shares(count, rows * top, bound, lean, True), shares(count, rows * top, bound, lean, False)
    places = jnp.arange(count)

    def named(tallies, rotation):
        used = int((tallies > 0).sum())
        fixed = max(1, used // 4)
        shifted = fixed + (places - fixed + rotation * (used - fixed)) % max(1, count - fixed)
        return jnp.zeros((count,), jnp.int32).at[sequence[jnp.where(places < fixed, places, shifted)]].set(jnp.asarray(tallies, jnp.int32))

    tallies = jnp.where(number % 4 == 0, named(packed, number // 4), named(common, number - number // 4 - 1))
    mixed = jax.random.permutation(jax.random.fold_in(own, 3), count)
    source_of, taker = mixed[0:count // 2 * 2:2], mixed[1:count // 2 * 2:2]
    margin = jnp.minimum(tallies[source_of] - 1, bound - tallies[taker]) // 2
    margin = jnp.where((source_of == sequence[0]) | (taker == sequence[0]) | (tallies[taker] == 0), 0, jnp.maximum(margin, 0))
    shifted = jax.random.randint(jax.random.fold_in(own, 4), (count // 2,), 0, 1 << 20) % (margin + 1)
    tallies = tallies.at[source_of].add(-shifted).at[taker].add(shifted)
    items = jnp.searchsorted(jnp.cumsum(tallies), jnp.arange(rows * top), side="right").astype(jnp.int32)
    listing = items.reshape(top, rows).T
    listing = listing[jax.random.permutation(jax.random.fold_in(own, 1), rows)]
    rotation = jax.random.randint(jax.random.fold_in(own, 2), (rows, 1), 0, top)
    return jnp.take_along_axis(listing, (jnp.arange(top)[None, :] + rotation) % top, axis=1)


def shares(count, total, most, skew, full):
    weights = [(1 << 20) // math.isqrt(grade ** skew) + 1 for grade in range(1, count + 1)]
    largest = most if full else min(most, max(-(-total // count), total * weights[0] // sum(weights)))
    least = 1 if total - largest >= count - 1 else 0
    given, surplus = [largest] + [least] * (count - 1), total - largest - least * (count - 1)
    while surplus > 0:
        movable = [i for i in range(1, count) if given[i] < largest] or [i for i in range(1, count) if given[i] < most]
        whole, remaining = sum([weights[i] for i in movable]), surplus
        for i in movable:
            more = min(most - given[i], max(1, remaining * weights[i] // whole), surplus)
            given[i] = given[i] + more
            surplus = surplus - more
    return np.array(given)


def normal_values(rng, extent, width, most, pieces=(), kind=jnp.bfloat16):
    array = width * jax.random.normal(rng, extent, jnp.float32)
    if pieces:
        array = array * block_scale(rng, extent, pieces, -0.22, 0.18)
    return jnp.clip(array, -most, most).astype(kind)


def setup_inputs(seed: int = 0) -> dict:
    streams_of = jax.random.split(jax.random.key(seed), 16)
    layer_input = normal_values(streams_of[0], (TOKENS, D), 1.0, 6.0, ((0, 128),), jnp.float32)
    lengths = draw_lengths(jax.random.fold_in(streams_of[15], 71), 0)
    routes_keys = jax.random.split(jax.random.fold_in(streams_of[2], 1), TOKENS // TOK_DEV)
    routes_turns = jax.random.permutation(jax.random.fold_in(streams_of[2], 3), TOKENS // TOK_DEV)
    routes = jax.vmap(lambda own, number: routed_block(jax.random.fold_in(streams_of[2], 2), own, number, TOK_DEV, EXPERTS, TOP, CAP, 1))(routes_keys, routes_turns).reshape((TOKENS, TOP))
    norm_gain = jnp.clip(1.0 + 0.1 * jax.random.normal(streams_of[3], (D,), jnp.float32), 0.5, 1.5)
    w_query = normal_values(streams_of[4], (D, HEADS * HEAD_DIM), D ** -0.5, 0.1875, ((1, 8),))
    w_keyval = normal_values(streams_of[5], (D, KV_HEADS, 2 * HEAD_DIM), D ** -0.5, 0.1875, ((1, 8),))
    query_gain = jnp.clip(1.0 + 0.1 * jax.random.normal(streams_of[6], (HEADS * HEAD_DIM,), jnp.float32), 0.5, 1.5)
    key_gain = jnp.clip(1.0 + 0.1 * jax.random.normal(streams_of[7], (KV_HEADS * HEAD_DIM,), jnp.float32), 0.5, 1.5)
    w_out = normal_values(streams_of[8], (HEADS * HEAD_DIM, D), (max(1, 3 * HEADS * HEAD_DIM // GRP)) ** -0.5, 3.5, ((0, 8),))
    mlp_gain = jnp.clip(1.0 + 0.1 * jax.random.normal(streams_of[9], (D,), jnp.float32), 0.5, 1.5)
    w_router = normal_values(streams_of[10], (D, EXPERTS), (4 * D) ** -0.5, 0.09375, (), jnp.float32)
    w_gate = normal_values(streams_of[11], (EXPERTS, D, FF), D ** -0.5, 0.1875, ((0, 16), (2, 8)))
    w_up = normal_values(streams_of[12], (EXPERTS, D, FF), D ** -0.5, 0.1875, ((0, 16), (2, 8)))
    w_down = normal_values(streams_of[13], (EXPERTS, FF, D), (FF // 8) ** -0.5, 0.75, ((0, 16), (1, 8)))
    cotangent = normal_values(streams_of[14], (TOKENS, D), 1.0, 6.0, ((0, 128),), jnp.float32)
    return {"layer_input": layer_input, "lengths": lengths, "routes": routes, "norm_gain": norm_gain, "w_query": w_query, "w_keyval": w_keyval, "query_gain": query_gain, "key_gain": key_gain, "w_out": w_out, "mlp_gain": mlp_gain, "w_router": w_router, "w_gate": w_gate, "w_up": w_up, "w_down": w_down, "cotangent": cotangent}


epsilon = 1e-06
highest = lax.Precision.HIGHEST

@jax.custom_vjp
def low(v):
    return lax.optimization_barrier(v.astype(jnp.bfloat16)).astype(jnp.float32)

@jax.custom_vjp
def low_back(v):
    return v

def low_keep(v):
    return (low(v), None)

def low_pass(kept, grad):
    return (grad,)

def back_keep(v):
    return (v, None)

def back_low(kept, grad):
    return (low(grad),)
low.defvjp(low_keep, low_pass)
low_back.defvjp(back_keep, back_low)

def normed(inputs):
    return inputs * lax.rsqrt(lax.optimization_barrier(jnp.mean(inputs * inputs, -1, keepdims=True)) + epsilon)

def rotary(length):
    half_dim = HEAD_DIM // 2
    frequency = 10000.0 ** (-(jnp.arange(half_dim, dtype=jnp.float32) * 2.0 / HEAD_DIM))
    angles = jnp.arange(length, dtype=jnp.float32)[:, None] * frequency[None, :]
    return (jnp.cos(angles)[:, None, :], jnp.sin(angles)[:, None, :])

def rotate(inputs, cosine, sine_part):
    half_dim = HEAD_DIM // 2
    first = inputs[..., :half_dim]
    second = inputs[..., half_dim:]
    return jnp.concatenate([first * cosine - second * sine_part, second * cosine + first * sine_part], -1)

def attend_group(x_group, length, norm_gain, w_query, w_keyval, query_gain, key_gain, w_out):
    per_kv = HEADS // KV_HEADS
    h_one = low(normed(x_group) * norm_gain)
    q_raw = low_back(jnp.dot(h_one, w_query, precision=highest)).reshape(GRP, HEADS, HEAD_DIM)
    kv_raw = low_back(jnp.dot(h_one, w_keyval.reshape(D, -1), precision=highest)).reshape(GRP, KV_HEADS, 2 * HEAD_DIM)
    cosine, sine_part = rotary(GRP)
    query_rot = low_back(low(rotate(normed(q_raw) * query_gain.reshape(HEADS, HEAD_DIM), cosine, sine_part)))
    key_rot = low_back(low(rotate(normed(kv_raw[..., :HEAD_DIM]) * key_gain.reshape(KV_HEADS, HEAD_DIM), cosine, sine_part)))
    value_rows = low_back(low(kv_raw[..., HEAD_DIM:]))
    key_keep = jnp.arange(GRP) < length
    block_rows = min(512, GRP)

    def one_block(q_block):
        raw_scores = low_back(jnp.einsum('qcgd,kcd->cgqk', q_block, key_rot, precision=highest) * HEAD_DIM ** (-0.5))
        raw_scores = jnp.where(key_keep, raw_scores, -1e+30)
        probability = low(jax.nn.softmax(raw_scores, -1))
        return jnp.einsum('cgqk,kcd->qcgd', probability, value_rows, precision=highest)
    q_blocks = query_rot.reshape(GRP // block_rows, block_rows, KV_HEADS, per_kv, HEAD_DIM)
    attn_o = lax.map(jax.checkpoint(one_block), q_blocks)
    attn_o = low_back(low(attn_o.reshape(GRP, HEADS * HEAD_DIM)))
    return jnp.dot(attn_o, w_out, precision=highest)

def forward(layer_input, norm_gain, w_query, w_keyval, query_gain, key_gain, w_out, mlp_gain, w_router, w_gate, w_up, w_down, lengths, routes):

    def group_part(items):
        return attend_group(items[0], items[1], norm_gain, w_query, w_keyval, query_gain, key_gain, w_out)
    attn = lax.map(jax.checkpoint(group_part), (layer_input.reshape(N_EP, GRP, D), lengths)).reshape(TOKENS, D)
    valid = (jnp.arange(GRP)[None, :] < lengths[:, None]).reshape(TOKENS).astype(jnp.float32)
    h_mid = layer_input + low_back(attn)
    mlp_in = normed(h_mid) * mlp_gain
    logits = jnp.dot(mlp_in, w_router, precision=highest)
    probs = jax.nn.softmax(logits, -1)
    gates = jax.nn.softmax(jnp.take_along_axis(logits, routes, 1), -1) * valid[:, None]
    hit_count = lax.optimization_barrier(jnp.sum((routes[:, :, None] == jnp.arange(EXPERTS)[None, None, :]).astype(jnp.float32), 1))
    counts = lax.optimization_barrier(jnp.sum(hit_count * valid[:, None], 0))
    nvalid = jnp.sum(valid)
    loss = EXPERTS * jnp.sum(counts / (TOP * nvalid) * (lax.optimization_barrier(jnp.sum(probs * valid[:, None], 0)) / nvalid))
    rows_each = N_EP * N_TP * CAP
    flat_routes = routes.reshape(-1)
    one_hot = (flat_routes[:, None] == jnp.arange(EXPERTS)[None, :]).astype(jnp.int32)
    rank_in = lax.optimization_barrier(jnp.sum((jnp.cumsum(one_hot, 0) - one_hot) * one_hot, 1))
    place = (flat_routes * rows_each + rank_in).astype(jnp.int32)
    owner = jnp.zeros(EXPERTS * rows_each, jnp.int32).at[place].set((jnp.arange(TOKENS * TOP) // TOP).astype(jnp.int32))
    filled = jnp.zeros(EXPERTS * rows_each, jnp.float32).at[place].set(1.0)
    expert_in = low(mlp_in)

    def one_expert(items):
        gate_weight, up_weight, down_weight, token_of, slot_full = items
        row_copies = low_back(expert_in[token_of]) * slot_full[:, None]
        pre_gate = low_back(jnp.dot(row_copies, gate_weight, precision=highest))
        pre_up = low_back(jnp.dot(row_copies, up_weight, precision=highest))
        hidden = low(jax.nn.silu(pre_gate) * pre_up)
        return low_back(low(jnp.dot(hidden, down_weight, precision=highest)))
    expert_out = lax.map(jax.checkpoint(one_expert), (w_gate, w_up, w_down, owner.reshape(EXPERTS, rows_each), filled.reshape(EXPERTS, rows_each)))
    expert_out = expert_out.reshape(EXPERTS * rows_each, D)

    def combine(items):
        where_at, weight = items
        return lax.optimization_barrier(jnp.sum(weight[:, :, None] * expert_out[where_at], 1))
    mixture = lax.map(jax.checkpoint(combine), (place.reshape(N_EP, GRP, TOP), gates.reshape(N_EP, GRP, TOP))).reshape(TOKENS, D)
    return (valid[:, None] * (h_mid + mixture), loss)

def reference(layer_input, lengths, routes, norm_gain, w_query, w_keyval, query_gain, key_gain, w_out, mlp_gain, w_router, w_gate, w_up, w_down, cotangent):
    params = (layer_input, norm_gain, w_query.astype(jnp.float32), w_keyval.astype(jnp.float32), query_gain, key_gain, w_out.astype(jnp.float32), mlp_gain, w_router, w_gate.astype(jnp.float32), w_up.astype(jnp.float32), w_down.astype(jnp.float32))

    def run(*inputs):
        return forward(*inputs, lengths, routes)
    (output, loss), pull = jax.vjp(run, *params)
    grads = pull((cotangent, jnp.ones((), jnp.float32)))
    return (output, grads[0], loss, grads[1], grads[2], grads[3], grads[4], grads[5], grads[6], grads[7], grads[8], grads[9], grads[10], grads[11])
```

```python
import jax
import jax.numpy as jnp
import numpy as np
from jax import lax
from jax.experimental import pallas as pl
from jax.experimental.pallas import tpu as pltpu
from jax.sharding import PartitionSpec as P

MESH = pl.DeviceIdType.MESH
f32, bf16 = jnp.float32, jnp.bfloat16
HEAD_DIM = 64
epsilon = 1e-06
masked_score = -1e30
highest = lax.Precision.HIGHEST
MIB = 2**20

X, Y, Z, C = (1, 0, 0, 0), (0, 1, 0, 0), (0, 0, 1, 0), (0, 0, 0, 1)
XM, YM, ZM = (-1, 0, 0, 0), (0, -1, 0, 0), (0, 0, -1, 0)
X2, Z2 = (2, 0, 0, 0), (0, 0, 2, 0)
NEAR = (0, 1, -1, 2)


def times(d, k):
    return tuple(v * k for v in d)


class Net:
    def __init__(self, send_sems, recv_sems):
        self.ep, self.tp = lax.axis_index("ep"), lax.axis_index("tp")
        self.x, self.z = self.ep // 4, self.ep % 4
        self.y, self.c = self.tp // 2, self.tp % 2
        self.send_sems, self.recv_sems = send_sems, recv_sems
        self.count = 0
        self.unsent = []

    def device(self, d):
        x, y = (self.x + d[0]) % 4, (self.y + d[1]) % 4
        z, c = (self.z + d[2]) % 4, (self.c + d[3]) % 2
        return (x * 4 + z, y * 2 + c)

    def ep_at(self, dx, dz):
        return ((self.x + dx) % 4) * 4 + (self.z + dz) % 4

    def tp_at(self, dy, dc):
        return ((self.y + dy) % 4) * 2 + (self.c + dc) % 2

    def barrier(self, dirs):
        sem = pltpu.get_barrier_semaphore()
        for d in dirs:
            pl.semaphore_signal(sem, inc=1, device_id=self.device(d), device_id_type=MESH)
        pl.semaphore_wait(sem, len(dirs))

    def send(self, src, dst, d):
        i = self.count
        self.count += 1
        copy = pltpu.make_async_remote_copy(
            src_ref=src,
            dst_ref=dst,
            send_sem=self.send_sems.at[i],
            recv_sem=self.recv_sems.at[i],
            device_id=self.device(d),
            device_id_type=MESH,
        )
        copy.start()
        self.unsent.append(copy)
        return copy

    def keep(self, src, dst):
        i = self.count
        self.count += 1
        copy = pltpu.make_async_copy(src, dst, self.send_sems.at[i])
        copy.start()
        return copy

    def sent(self, copy):
        copy.wait_send()
        self.unsent = [c for c in self.unsent if c is not copy]

    def finish(self):
        for copy in self.unsent:
            copy.wait_send()
        self.unsent = []


class GatherTp:
    def __init__(self, net, ref, own=None):
        self.net, self.ref = net, ref
        self.own = own or (lambda half: ref(net.tp, half))
        self.copies = {}
        self.done = set()

    def wait(self, *key):
        if key not in self.done:
            self.done.add(key)
            self.copies[key].wait_recv()

    def along(self, dy, half, sign):
        src = self.own(half) if dy == 0 else self.ref(self.net.tp_at(dy, 0), half)
        to = (dy - sign + 1) % 4 - 1
        self.copies[("y", to, half)] = self.net.send(
            src, self.ref(self.net.tp_at(dy, 0), half), times(Y, sign)
        )

    def across(self, dy):
        for half in (0, 1):
            src = self.own(half) if dy == 0 else self.ref(self.net.tp_at(dy, 0), half)
            self.copies[("c", dy, half)] = self.net.send(
                src, self.ref(self.net.tp_at(dy, 0), half), C
            )

    def start(self):
        self.along(0, 0, 1)
        self.along(0, 1, -1)
        self.along(0, 1, 1)
        self.along(0, 0, -1)
        self.across(0)

    def relay(self):
        self.wait("y", -1, 0)
        self.along(-1, 0, 1)
        self.wait("y", 1, 1)
        self.along(1, 1, -1)
        for dy, half in ((-1, 1), (1, 0)):
            self.wait("y", dy, half)
            self.across(dy)

    def spread(self):
        for half in (0, 1):
            self.wait("y", 2, half)
        self.across(2)

    def need(self, dy, dc):
        if dc:
            for half in (0, 1):
                self.wait("c", dy, half)
        elif dy:
            for half in (0, 1):
                self.wait("y", dy, half)

    def finish(self):
        for key in list(self.copies):
            self.wait(*key)


class ScatterTp:
    def __init__(self, net, ref, sib, far, near):
        self.net, self.ref, self.sib, self.far_at, self.near_at = net, ref, sib, far, near
        self.copies = {}

    def across(self, dy):
        i = NEAR.index(dy)
        for half in (0, 1):
            self.copies[("c", dy, half)] = self.net.send(
                self.ref(self.net.tp_at(dy, 1), half), self.sib(i, half), C
            )

    def join(self, dy, half):
        self.copies[("c", dy, half)].wait_recv()
        return self.ref(self.net.tp_at(dy, 0), half)[...].astype(f32) + self.sib(
            NEAR.index(dy), half
        )[...].astype(f32)

    def far(self):
        for half, sign in ((0, 1), (1, -1)):
            ref = self.ref(self.net.tp_at(2, 0), half)
            ref[...] = self.join(2, half).astype(bf16)
            self.copies[("f", half)] = self.net.send(ref, self.far_at(half), times(Y, sign))

    def near(self):
        for part, sign in ((0, 1), (1, -1)):
            for half in (1 - part, part):
                ref = self.ref(self.net.tp_at(sign, 0), half)
                total = self.join(sign, half)
                if half == part:
                    self.copies[("f", part)].wait_recv()
                    total = total + self.far_at(part)[...].astype(f32)
                ref[...] = total.astype(bf16)
                self.copies[("n", part, half)] = self.net.send(
                    ref, self.near_at(part, half), times(Y, sign)
                )

    def last(self, half):
        total = self.join(0, half)
        for part in (0, 1):
            self.copies[("n", part, half)].wait_recv()
            total = total + self.near_at(part, half)[...].astype(f32)
        return total


class GatherEp:
    def __init__(self, net, buf, rows):
        self.net, self.buf, self.rows = net, buf, rows
        self.copies = {}
        self.done = set()

    def ref(self, h, j, k, part):
        half, quarter = self.rows // 2, self.rows // 4
        e = self.net.ep_at(j, k) if h == 0 else self.net.ep_at(k, j)
        if part is None:
            return self.buf.at[e, pl.ds(h * half, half)]
        return self.buf.at[e, pl.ds(h * half + part * quarter, quarter)]

    def send(self, h, j, k, part, along, sign):
        d = (X, Z)[along if h == 0 else 1 - along]
        r = self.ref(h, j, k, part)
        to = (j - sign, k) if along == 0 else (j, k - sign)
        to = tuple((v + 1) % 4 - 1 for v in to)
        self.copies[(h, *to, part)] = self.net.send(r, r, times(d, sign))

    def wait(self, *key):
        if key not in self.done:
            self.done.add(key)
            self.copies[key].wait_recv()

    def need(self, h, j, k):
        if (j, k) != (0, 0):
            for part in (None,) if (h, j, k, None) in self.copies else (0, 1):
                self.wait(h, j, k, part)

    def block(self, dx, dz):
        self.need(0, dx, dz)
        self.need(1, dz, dx)

    def start(self):
        for along in (0, 1):
            for h in (0, 1):
                for sign in (1, -1):
                    self.send(h, 0, 0, None, along, sign)

    def first(self):
        for part, sign in ((0, 1), (1, -1)):
            for h in (0, 1):
                self.wait(h, -sign, 0, None)
                self.send(h, -sign, 0, part, 0, sign)
        for sign in (1, -1):
            for h in (0, 1):
                for turn in (1, -1):
                    self.send(h, -sign, 0, None, 1, turn)

    def far(self):
        for h in (0, 1):
            self.need(h, 2, 0)
            for turn in (1, -1):
                self.send(h, 2, 0, None, 1, turn)

    def second(self, j):
        for part, sign in ((0, 1), (1, -1)):
            for h in (0, 1):
                self.wait(h, j, -sign, None)
                self.send(h, j, -sign, part, 1, sign)

    def finish(self):
        for key in list(self.copies):
            self.wait(*key)


class ScatterEp:
    def __init__(self, net, terms, landed, rows):
        self.net, self.terms, self.landed, self.rows = net, terms, landed, rows
        self.copies = {}

    def ref(self, h, g, j, part):
        j, k = (j, NEAR[g]) if g < 4 else (0, j)
        half, quarter = self.rows // 2, self.rows // 4
        e = self.net.ep_at(k, j) if h == 0 else self.net.ep_at(j, k)
        if part is None:
            return self.terms.at[e, pl.ds(h * half, half)]
        return self.terms.at[e, pl.ds(h * half + part * quarter, quarter)]

    def slot(self, g, h, which, part=None):
        quarter = self.rows // 4
        r = self.landed.at[g, h, which]
        return r if part is None else r.at[pl.ds(part * quarter, quarter)]

    def dir(self, h, g, sign):
        return times((Z, X)[(g == 4) if h == 0 else (g != 4)], sign)

    def far(self, g):
        for h in (0, 1):
            for part, sign in ((0, 1), (1, -1)):
                self.copies[(g, h, 2, part)] = self.net.send(
                    self.ref(h, g, 2, part), self.slot(g, h, 2, part), self.dir(h, g, sign)
                )

    def near(self, g):
        for h in (0, 1):
            for part, sign in ((0, 1), (1, -1)):
                self.copies[(g, h, 2, part)].wait_recv()
                r = self.ref(h, g, sign, part)
                r[...] = (r[...].astype(f32) + self.slot(g, h, 2, part)[...].astype(f32)).astype(bf16)
                self.copies[(g, h, part)] = self.net.send(
                    self.ref(h, g, sign, None), self.slot(g, h, part), self.dir(h, g, sign)
                )

    def last(self, g, h):
        for part in (0, 1):
            self.copies[(g, h, part)].wait_recv()
        r = self.ref(h, g, 0, None)
        total = r[...].astype(f32)
        for part in (0, 1):
            total = total + self.slot(g, h, part)[...].astype(f32)
        return total

    def turn(self, g):
        for h in (0, 1):
            self.ref(h, g, 0, None)[...] = self.last(g, h).astype(bf16)


def lanes(shape):
    return lax.broadcasted_iota(jnp.int32, shape, len(shape) - 1)


def low(shape):
    return lanes(shape) < HEAD_DIM


def normed(v):
    factor = lax.rsqrt(jnp.mean(v * v, -1, keepdims=True) + epsilon)
    return v * factor, factor


def norm_back(grad, hat, factor):
    return factor * (grad - hat * jnp.mean(grad * hat, -1, keepdims=True))


def pair_sums(v):
    first = low(v.shape)
    a = jnp.sum(jnp.where(first, v, 0.0), -1, keepdims=True)
    b = jnp.sum(jnp.where(first, 0.0, v), -1, keepdims=True)
    return jnp.where(first, a, b)


def pair_normed(v):
    factor = lax.rsqrt(pair_sums(v * v) / HEAD_DIM + epsilon)
    return v * factor, factor


def pair_norm_back(grad, hat, factor):
    return factor * (grad - hat * (pair_sums(grad * hat) / HEAD_DIM))


def partner(v):
    half = HEAD_DIM // 2
    return jnp.where(
        lanes(v.shape) % HEAD_DIM < half, pltpu.roll(v, 128 - half, 1), pltpu.roll(v, half, 1)
    )


def rotate(v, cosine, sine):
    return v * cosine + partner(v) * sine


def rotate_back(v, cosine, sine):
    return v * cosine - partner(v) * sine


def swap(v):
    return pltpu.roll(v, HEAD_DIM, v.ndim - 1)


def dot(a, b):
    return jnp.dot(a, b, preferred_element_type=f32)


def dot_nt(a, b):
    return lax.dot_general(a, b, (((1,), (1,)), ((), ())), preferred_element_type=f32)


def dot_tn(a, b):
    return lax.dot_general(a, b, (((0,), (0,)), ((), ())), preferred_element_type=f32)


def rotary(length):
    half = HEAD_DIM // 2
    frequency = 10000.0 ** (-(np.arange(half, dtype=np.float64) * 2.0 / HEAD_DIM))
    angles = np.arange(length, dtype=np.float64)[:, None] * frequency[None, :]
    cosine, sine = np.cos(angles), np.sin(angles)
    cosine = np.concatenate([cosine] * 4, -1).astype(np.float32)
    sine = np.concatenate([-sine, sine] * 2, -1).astype(np.float32)
    return cosine, sine


VM = pl.BlockSpec(memory_space=pltpu.VMEM)
SM = pl.BlockSpec(memory_space=pltpu.SMEM)
ANY = pl.BlockSpec(memory_space=pl.ANY)


def shaped(shape, dtype):
    return jax.ShapeDtypeStruct(shape, dtype)


def params(collective_id, vmem):
    return pltpu.CompilerParams(
        collective_id=collective_id, has_side_effects=True, vmem_limit_bytes=vmem * MIB
    )


def key_value(qkv, gains, cosine, sine):
    q_hat, q_scale = pair_normed(qkv[:, :128])
    kv = qkv[:, 128:]
    first = low(kv.shape)
    other = swap(kv)
    k_hat, k_scale = pair_normed(jnp.where(first, kv, other))
    query = rotate(q_hat * gains[0:1], cosine, sine).astype(bf16)
    key = rotate(k_hat * gains[1:2], cosine, sine).astype(bf16)
    value = jnp.where(first, other, kv).astype(bf16)
    return query, key, value, q_hat, q_scale, k_hat, k_scale


def attend_kernel(
    layer_input,
    lengths,
    norm_gain,
    w_query,
    w_keyval,
    gains,
    w_out,
    cosine,
    sine,
    cotangent,
    w_gu,
    w_down,
    h_mid_ref,
    h_out,
    attn_out,
    lse_out,
    cot_out,
    gu_out,
    down_out,
    h_all,
    w_qkv,
    query,
    key,
    value,
    attn_o,
    lse,
    terms,
    from_sib,
    from_far,
    from_near,
    cot,
    send_sems,
    recv_sems,
):
    net = Net(send_sems, recv_sems)
    rows = layer_input.shape[0]
    half_rows = rows // 2
    seq_len = lengths[net.ep]
    net.barrier([X, XM, Z, ZM, Y, YM, C])

    x_hat, _ = normed(layer_input[...])
    h_all[net.tp] = (x_hat * norm_gain[...]).astype(bf16)
    tokens = GatherTp(net, lambda t, half: h_all.at[t, pl.ds(half * half_rows, half_rows)])
    tokens.start()

    place = net.tp * rows + lax.broadcasted_iota(jnp.int32, (rows, 1), 0)
    cot[...] = jnp.where(place < seq_len, cotangent[...], 0.0).astype(bf16)
    cot_kept = net.keep(cot, cot_out.at[net.ep])
    units = w_down.shape[1]
    kept = [
        net.keep(w_gu.at[e], gu_out.at[e, :, pl.ds(pl.multiple_of(net.tp * 128, 128), 128)])
        for e in (0, 1)
    ] + [
        net.keep(w_down.at[e], down_out.at[e, pl.ds(pl.multiple_of(net.tp * units, units), units)])
        for e in (0, 1)
    ]
    w_qkv[:, :128] = w_query[...]
    w_qkv[:, 128:] = w_keyval[...]
    cot_kept.wait()
    cots = GatherEp(net, cot_out, rows)
    cots.start()

    tokens.relay()

    def project(dy):
        def one(i, _):
            t = net.tp_at(dy, i)
            at = pl.ds(pl.multiple_of(t * rows, rows), rows)
            qkv = dot(h_all[t], w_qkv[...])
            parts = key_value(qkv, gains, cosine[at, :], sine[at, :])
            query[at, :], key[at, :], value[at, :] = parts[:3]
            return 0

        lax.fori_loop(0, 2, one, 0)

    tokens.need(0, 1)
    project(0)
    cots.first()
    tokens.spread()
    tokens.need(-1, 1)
    project(-1)
    tokens.need(1, 1)
    project(1)
    cots.second(0)
    tokens.need(2, 1)
    project(2)
    tokens.finish()
    h_kept = net.keep(h_all, h_out)

    gu = GatherTp(
        net,
        lambda t, half: gu_out.at[half, :, pl.ds(pl.multiple_of(t * 128, 128), 128)],
        lambda half: w_gu.at[half],
    )
    down = GatherTp(
        net,
        lambda t, half: down_out.at[half, pl.ds(pl.multiple_of(t * units, units), units)],
        lambda half: w_down.at[half],
    )
    factor = HEAD_DIM**-0.5
    total_keys = key.shape[0]

    def attend(dy):
        def one(i, _):
            t = net.tp_at(dy, 1 - i)
            at = pl.ds(pl.multiple_of(t * rows, rows), rows)
            q = query[at, :]
            first = low(q.shape)
            mixed, logs = [], []
            for head in (0, 1):
                q_head = jnp.where(first == (head == 0), q, jnp.zeros_like(q))
                s = dot_nt(q_head, key[...]) * factor
                s = jnp.where(lanes(s.shape) < seq_len, s, masked_score)
                top = jnp.max(s, -1, keepdims=True)
                p = jnp.exp(s - top)
                total = jnp.sum(p, -1, keepdims=True)
                mixed.append(dot((p * (1.0 / total)).astype(bf16), value[...]))
                logs.append(top + jnp.log(total))
            o = jnp.where(first, mixed[0], mixed[1]).astype(bf16)
            attn_o[at, :] = o
            lse[at, :] = jnp.where(first, logs[0], logs[1])
            terms[t] = dot(o, w_out[...]).astype(bf16)
            return 0

        lax.fori_loop(0, 2, one, 0)

    sums = ScatterTp(
        net,
        lambda t, half: terms.at[t, pl.ds(half * half_rows, half_rows)],
        lambda i, half: from_sib.at[i, pl.ds(half * half_rows, half_rows)],
        lambda half: from_far.at[half],
        lambda part, half: from_near.at[part, pl.ds(half * half_rows, half_rows)],
    )
    attend(2)
    sums.across(2)
    cots.far()
    attend(1)
    sums.across(1)
    sums.far()
    cots.second(-1)
    attend(-1)
    sums.across(-1)
    sums.near()
    cots.second(1)
    attend(0)
    sums.across(0)
    cots.second(2)
    attn_kept = net.keep(attn_o, attn_out)
    lse_kept = net.keep(lse, lse_out)
    for half in (0, 1):
        at = pl.ds(half * half_rows, half_rows)
        h_mid_ref[at, :] = layer_input[at, :] + sums.last(half)
    gu.start()
    down.start()
    gu.relay()
    down.relay()
    gu.spread()
    down.spread()
    cots.finish()
    gu.finish()
    down.finish()
    for copy in kept + [h_kept, attn_kept, lse_kept]:
        copy.wait()
    net.finish()


def attend(layer_input, lengths, norm_gain, w_query, w_keyval, gains, w_out, cosine, sine, cotangent, w_gu, w_down):
    rows, width = layer_input.shape
    n_tp, n_ep = 8, 16
    group = rows * n_tp
    units = w_down.shape[1]
    return pl.pallas_call(
        attend_kernel,
        name="attend",
        out_shape=(
            shaped((rows, width), f32),
            shaped((n_tp, rows, width), bf16),
            shaped((group, 128), bf16),
            shaped((group, 128), f32),
            shaped((n_ep, rows, width), bf16),
            shaped((2, width, n_tp * 128), bf16),
            shaped((2, n_tp * units, width), bf16),
        ),
        in_specs=[VM, SM] + [VM] * 8 + [ANY, ANY],
        out_specs=(VM,) + (ANY,) * 6,
        scratch_shapes=[
            pltpu.VMEM((n_tp, rows, width), bf16),
            pltpu.VMEM((width, 256), bf16),
            pltpu.VMEM((group, 128), bf16),
            pltpu.VMEM((group, 128), bf16),
            pltpu.VMEM((group, 128), bf16),
            pltpu.VMEM((group, 128), bf16),
            pltpu.VMEM((group, 128), f32),
            pltpu.VMEM((n_tp, rows, width), bf16),
            pltpu.VMEM((4, rows, width), bf16),
            pltpu.VMEM((2, rows // 2, width), bf16),
            pltpu.VMEM((2, rows, width), bf16),
            pltpu.VMEM((rows, width), bf16),
            pltpu.SemaphoreType.DMA((128,)),
            pltpu.SemaphoreType.DMA((128,)),
        ],
        compiler_params=params(1, 40),
    )(layer_input, lengths, norm_gain.reshape(1, -1), w_query, w_keyval, gains, w_out, cosine, sine, cotangent, w_gu, w_down)


class Exchange:
    def __init__(self, net, out, half_way, got):
        self.net, self.out, self.half_way, self.got = net, out, half_way, got

    def start(self):
        net = self.net
        self.first = [
            net.send(self.out.at[(net.x + k) % 4], self.half_way.at[net.x], times(X, k))
            for k in (1, -1, 2)
        ]
        self.half_way[net.x] = self.out[net.x]

    def turn(self):
        net = self.net
        for copy in self.first:
            copy.wait_recv()
        self.second = [
            net.send(self.half_way.at[:, (net.z + k) % 4], self.got.at[:, net.z], times(Z, k))
            for k in (1, -1, 2)
        ]
        self.got[:, net.z] = self.half_way[:, net.z]

    def finish(self):
        for copy in self.second:
            copy.wait_recv()


def pick(v, t):
    return v[:, t * 128 : (t + 1) * 128]


ORDER = (
    (0, 0), (-1, 0), (1, 0), (0, -1),
    (0, 1), (2, 0), (0, 2), (-1, -1),
    (-1, 1), (1, -1), (1, 1), (2, -1),
    (2, 1), (-1, 2), (1, 2), (2, 2),
)
BATCH = 4


def experts_kernel(
    h_mid_ref,
    lengths,
    routes_t,
    mlp_gain,
    w_router_t,
    counts,
    cotangent,
    cot_hbm,
    gu_hbm,
    down_hbm,
    output,
    d_mid_ref,
    small,
    gu_grad_out,
    down_grad_out,
    tok,
    cot,
    gu,
    down,
    hits,
    places,
    picked,
    d_rows,
    hidden,
    d_pre,
    weighted,
    row_back,
    row_terms,
    mix_terms,
    row_landed,
    mix_landed,
    gate_out,
    gate_mid,
    gate_got,
    back_out,
    back_mid,
    back_got,
    d_gates_ref,
    gu_grad,
    down_grad,
    send_sems,
    recv_sems,
):
    net = Net(send_sems, recv_sems)
    rows, width = h_mid_ref.shape
    slots = places.shape[1] // 2
    n_exp = w_router_t.shape[0]
    seq_len = lengths[net.ep]
    loads = [
        net.keep(cot_hbm, cot),
        net.keep(gu_hbm, gu),
        net.keep(down_hbm, down),
    ]
    net.barrier([X, XM, X2, Z, ZM, Z2])

    h_hat, h_scale = normed(h_mid_ref[...])
    mlp_in = h_hat * mlp_gain[...]
    tok[net.ep] = mlp_in.astype(bf16)
    tokens = GatherEp(net, tok, rows)
    tokens.start()

    logits = lax.dot_general(
        w_router_t[...], mlp_in, (((1,), (1,)), ((), ())), precision=highest, preferred_element_type=f32
    )
    token_at = net.tp * rows + lanes((1, rows))
    valid = jnp.where(token_at < seq_len, 1.0, 0.0)
    expert = lax.broadcasted_iota(jnp.int32, (n_exp, rows), 0)
    mine = routes_t[:, pl.ds(pl.multiple_of((net.ep * 8 + net.tp) * rows, rows), rows)]
    chosen = jnp.zeros((n_exp, rows), jnp.bool_)
    for k in range(mine.shape[0]):
        chosen = jnp.logical_or(chosen, expert == mine[k : k + 1])
    top = jnp.max(logits, 0, keepdims=True)
    weights = jnp.exp(logits - top)
    probs = weights / jnp.sum(weights, 0, keepdims=True)
    top = jnp.max(jnp.where(chosen, logits, masked_score), 0, keepdims=True)
    weights = jnp.where(chosen, jnp.exp(jnp.where(chosen, logits - top, 0.0)), 0.0)
    soft = weights / jnp.sum(weights, 0, keepdims=True)
    gates = soft * valid
    for e in range(16):
        gate_out[e // 4, e % 4, 0:2, :] = gates[2 * e : 2 * e + 2]
    to_owners = Exchange(net, gate_out, gate_mid, gate_got)
    to_owners.start()

    for s in range(16):
        segment = routes_t[:, pl.ds(pl.multiple_of((s * 8 + net.tp) * rows, rows), rows)]
        for j in (0, 1):
            same = (segment == net.ep * 2 + j).astype(f32)
            hits[2 * s + j : 2 * s + j + 1, :] = jnp.max(same, 0, keepdims=True)
    before = lax.broadcasted_iota(jnp.int32, (rows, rows), 0) < lanes((rows, rows))
    rank = dot(hits[...].astype(bf16), before.astype(bf16))
    rank = jnp.where(hits[...] > 0.5, rank, -1.0)
    slot = lax.broadcasted_iota(jnp.int32, (slots, rows), 0).astype(f32)
    for s in range(16):
        for j in (0, 1):
            r = rank[2 * s + j : 2 * s + j + 1]
            places[s, j * slots : (j + 1) * slots, :] = (slot == r).astype(bf16)

    tokens.first()
    to_owners.turn()
    for copy in loads:
        copy.wait()
    to_owners.finish()

    n = BATCH * slots

    def batch(b):
        at = pl.ds(b * n, n)
        members = []
        for i, (dx, dz) in enumerate(ORDER[b * BATCH : (b + 1) * BATCH]):
            tokens.block(dx, dz)
            s = net.ep_at(dx, dz)
            members.append((s, (net.x + dx) % 4, (net.z + dz) % 4))
            here = places[s]
            taken = dot(here, tok[s]).astype(bf16)
            taken_d = dot(here, cot[s]).astype(bf16)
            for j in (0, 1):
                to = pl.ds(b * n + i * slots, slots)
                picked[j, to, :] = taken[j * slots : (j + 1) * slots]
                d_rows[j, to, :] = taken_d[j * slots : (j + 1) * slots]

        def one(j, _):
            gate_col = []
            for s, sx, sz in members:
                here = places[s, pl.ds(pl.multiple_of(j * slots, slots), slots), :].astype(f32)
                gate_col.append(jnp.sum(here * gate_got[sx, sz, pl.ds(j, 1), :], -1, keepdims=True))
            gate_col = jnp.concatenate(gate_col, 0)
            d_picked = d_rows[j, at, :].astype(f32)
            d_row = (gate_col * d_picked).astype(bf16)
            d_rows[j, at, :] = d_row
            pre = dot(picked[j, at, :], gu[j])
            d_hidden = dot_nt(d_row, down[j])
            for p in range(4):
                even, odd = pick(pre, 2 * p), pick(pre, 2 * p + 1)
                first = low(even.shape)
                g = jnp.where(first, even, swap(odd))
                u = jnp.where(first, swap(even), odd)
                sigma = 1.0 / (1.0 + jnp.exp(-g))
                act = g * sigma
                hidden[j, at, p * 128 : (p + 1) * 128] = (act * u).astype(bf16)
                dh = pick(d_hidden, p)
                dg = dh * u * sigma * (1.0 + g * (1.0 - sigma))
                du = dh * act
                d_pre[j, at, 2 * p * 128 : (2 * p + 1) * 128] = jnp.where(first, dg, swap(du)).astype(bf16)
                d_pre[j, at, (2 * p + 1) * 128 : (2 * p + 2) * 128] = jnp.where(first, swap(dg), du).astype(bf16)
            out = dot(hidden[j, at, :], down[j]).astype(bf16).astype(f32)
            d_gate = jnp.sum(out * d_picked, -1, keepdims=True)
            weighted[j] = (gate_col * out).astype(bf16)
            row_back[j] = dot_nt(d_pre[j, at, :], gu[j]).astype(bf16)
            for i, (s, sx, sz) in enumerate(members):
                here = places[s, pl.ds(pl.multiple_of(j * slots, slots), slots), :].astype(f32)
                d = jnp.sum(here * d_gate[i * slots : (i + 1) * slots], 0, keepdims=True)
                back_out[sx, sz, pl.ds(j, 1), :] = d
            return 0

        lax.fori_loop(0, 2, one, 0)
        for i, (s, _, _) in enumerate(members):
            here = places[s]
            to = slice(i * slots, (i + 1) * slots)
            mix_terms[s] = dot_tn(here, jnp.concatenate([weighted[0, to, :], weighted[1, to, :]], 0)).astype(bf16)
            row_terms[s] = dot_tn(here, jnp.concatenate([row_back[0, to, :], row_back[1, to, :]], 0)).astype(bf16)

    batch(0)
    tokens.second(0)
    tokens.far()
    batch(1)
    tokens.second(-1)
    tokens.second(1)
    batch(2)
    tokens.second(2)
    batch(3)
    tokens.finish()

    to_tokens = Exchange(net, back_out, back_mid, back_got)
    to_tokens.start()
    row_sums = ScatterEp(net, row_terms, row_landed, rows)
    mix_sums = ScatterEp(net, mix_terms, mix_landed, rows)
    for g in (3, 1, 2, 0):
        row_sums.far(g)
    to_tokens.turn()

    def grads(j, _):
        gu_grad[j] = dot_tn(picked[j], d_pre[j]).astype(bf16)
        down_grad[j] = dot_tn(hidden[j], d_rows[j]).astype(bf16)
        return 0

    for g in (3, 1, 2, 0):
        row_sums.near(g)
    lax.fori_loop(0, 2, grads, 0)
    grads_kept = [net.keep(gu_grad, gu_grad_out), net.keep(down_grad, down_grad_out)]
    row_sums.turn(3)
    row_sums.far(4)
    row_sums.turn(1)
    row_sums.turn(2)
    row_sums.near(4)
    row_sums.turn(0)
    to_tokens.finish()

    d_gates = []
    for e in range(16):
        d_gates_ref[2 * e : 2 * e + 2, :] = back_got[e // 4, e % 4, 0:2, :]
    d_gates = d_gates_ref[...] * valid
    d_chosen = soft * (d_gates - jnp.sum(soft * d_gates, 0, keepdims=True))
    nvalid = jnp.int32(0)
    for e in range(16):
        nvalid = nvalid + lengths[e]
    nvalid = nvalid.astype(f32)
    balance = n_exp * counts[...] / (8 * nvalid * nvalid)
    d_logits = d_chosen + valid * probs * (balance - jnp.sum(probs * balance, 0, keepdims=True))
    d_mlp_in = lax.dot_general(
        d_logits, w_router_t[...], (((0,), (0,)), ((), ())), precision=highest, preferred_element_type=f32
    )
    small[0:n_exp, :] = jnp.dot(d_logits, mlp_in, precision=highest, preferred_element_type=f32)
    small[n_exp + 8 :, :] = jnp.zeros((8, width), f32)
    small[n_exp + 8 :, 0:n_exp] = lax.dot_general(
        valid + jnp.zeros((8, rows), f32), probs, (((1,), (1,)), ((), ())), precision=highest, preferred_element_type=f32
    )
    total = jnp.concatenate([row_sums.last(4, 0), row_sums.last(4, 1)], 0)
    d_mlp_in = d_mlp_in + total
    gain_grad = jnp.sum(d_mlp_in * h_hat, 0, keepdims=True)
    small[n_exp : n_exp + 8, :] = gain_grad + jnp.zeros((8, width), f32)
    keep = net.tp * rows + lax.broadcasted_iota(jnp.int32, (rows, 1), 0) < seq_len
    d_out = jnp.where(keep, cotangent[...], 0.0)
    d_mid_ref[...] = d_out + norm_back(d_mlp_in * mlp_gain[...], h_hat, h_scale)

    for g in (3, 1, 2, 0):
        mix_sums.far(g)
    for g in (3, 1, 2, 0):
        mix_sums.near(g)
    mix_sums.turn(3)
    mix_sums.far(4)
    mix_sums.turn(1)
    mix_sums.turn(2)
    mix_sums.near(4)
    mix_sums.turn(0)
    mix = jnp.concatenate([mix_sums.last(4, 0), mix_sums.last(4, 1)], 0)
    output[...] = jnp.where(keep, h_mid_ref[...] + mix, 0.0)
    for copy in grads_kept:
        copy.wait()
    net.finish()


def experts(h_mid, lengths, routes_t, mlp_gain, w_router_t, counts, cotangent, cot_all, gu_all, down_all):
    rows, width = h_mid.shape
    n_exp = w_router_t.shape[0]
    slots = 3 * rows * routes_t.shape[0] // (2 * n_exp)
    units = down_all.shape[1]
    n = BATCH * slots
    small = pltpu.VMEM((4, 4, 8, rows), f32)
    return pl.pallas_call(
        experts_kernel,
        name="experts",
        out_shape=(
            shaped((rows, width), f32),
            shaped((rows, width), f32),
            shaped((n_exp + 16, width), f32),
            shaped((2, width, 2 * units), bf16),
            shaped((2, units, width), bf16),
        ),
        in_specs=[VM, SM] + [VM] * 5 + [ANY] * 3,
        out_specs=(VM, VM, VM, ANY, ANY),
        scratch_shapes=[
            pltpu.VMEM((16, rows, width), bf16),
            pltpu.VMEM((16, rows, width), bf16),
            pltpu.VMEM((2, width, 2 * units), bf16),
            pltpu.VMEM((2, units, width), bf16),
            pltpu.VMEM((n_exp, rows), f32),
            pltpu.VMEM((16, 2 * slots, rows), bf16),
            pltpu.VMEM((2, 16 * slots, width), bf16),
            pltpu.VMEM((2, 16 * slots, width), bf16),
            pltpu.VMEM((2, 16 * slots, units), bf16),
            pltpu.VMEM((2, 16 * slots, 2 * units), bf16),
            pltpu.VMEM((2, n, width), bf16),
            pltpu.VMEM((2, n, width), bf16),
            pltpu.VMEM((16, rows, width), bf16),
            pltpu.VMEM((16, rows, width), bf16),
            pltpu.VMEM((5, 2, 3, rows // 2, width), bf16),
            pltpu.VMEM((5, 2, 3, rows // 2, width), bf16),
            small, small, small, small, small, small,
            pltpu.VMEM((n_exp, rows), f32),
            pltpu.VMEM((2, width, 2 * units), bf16),
            pltpu.VMEM((2, units, width), bf16),
            pltpu.SemaphoreType.DMA((160,)),
            pltpu.SemaphoreType.DMA((160,)),
        ],
        compiler_params=params(2, 60),
    )(h_mid, lengths, routes_t, mlp_gain.reshape(1, -1), w_router_t, counts, cotangent, cot_all, gu_all, down_all)


class AxisSum:
    def __init__(self, net, term, slots, steps):
        self.net, self.term, self.slots = net, term, slots
        self.copies = [net.send(term, slots.at[i], d) for i, d in enumerate(steps)]

    def finish(self):
        total = self.term[...]
        for i, copy in enumerate(self.copies):
            copy.wait_recv()
            total = total + self.slots[i]
            self.net.sent(copy)
        return total


ALONG_X, ALONG_Y, ALONG_Z = ([times(d, k) for k in (1, -1, 2)] for d in (X, Y, Z))


def attend_back_kernel(
    layer_input,
    lengths,
    norm_gain,
    w_query,
    w_keyval,
    gains,
    w_out,
    cosine,
    sine,
    d_mid,
    attn_o,
    lse,
    small,
    h_hbm,
    gu_hbm,
    down_hbm,
    grad_input,
    grad_qkv_out,
    grad_out_out,
    gain_out,
    small_out,
    grad_gu_out,
    grad_down_out,
    h_all,
    d_all,
    w_qkv,
    query,
    key,
    value,
    q_hat,
    q_scale,
    k_hat,
    k_scale,
    soft,
    d_key_t,
    d_value_t,
    d_qkv,
    h_t,
    terms,
    from_sib,
    from_far,
    from_near,
    gu_terms,
    gu_sib,
    gu_far,
    gu_near,
    down_terms,
    down_sib,
    down_far,
    down_near,
    grad_terms,
    grad_landed,
    grad_all,
    small_term,
    small_sib,
    small_got,
    gain_term,
    gain_got,
    send_sems,
    recv_sems,
):
    net = Net(send_sems, recv_sems)
    rows, width = layer_input.shape
    half_rows = rows // 2
    units = grad_down_out.shape[1]
    seq_len = lengths[net.ep]
    loads = [net.keep(h_hbm, h_all), net.keep(gu_hbm, gu_terms), net.keep(down_hbm, down_terms)]
    net.barrier([X, XM, X2, Y, YM, times(Y, 2), Z, ZM, Z2, C])

    d_all[net.tp] = d_mid[...].astype(bf16)
    tokens = GatherTp(net, lambda t, half: d_all.at[t, pl.ds(half * half_rows, half_rows)])
    tokens.start()
    share = small.shape[0] // 2
    small_term[...] = small[...]
    small_first = net.send(small_term, small_sib, C)
    w_qkv[:, :128] = w_query[...]
    w_qkv[:, 128:] = w_keyval[...]
    d_key_t[...] = jnp.zeros_like(d_key_t)
    d_value_t[...] = jnp.zeros_like(d_value_t)
    factor = HEAD_DIM**-0.5
    group = query.shape[0]
    pair = 2 * rows
    loads[0].wait()

    def project(i, _):
        at = pl.ds(pl.multiple_of(i * rows, rows), rows)
        h = h_all[i]
        parts = key_value(dot(h, w_qkv[...]), gains, cosine[at, :], sine[at, :])
        for ref, part in zip((query, key, value, q_hat, q_scale, k_hat, k_scale), parts, strict=True):
            ref[at, :] = part
        h_t[:, at] = h.T
        return 0

    lax.fori_loop(0, 8, project, 0)
    tokens.relay()

    small_first.wait_recv()
    net.sent(small_first)
    mine = pl.ds(pl.multiple_of(net.c * share, 8), share)
    small_term[mine, :] = small_term[mine, :] + small_sib[mine, :]
    small_y = AxisSum(net, small_term.at[mine], small_got.at[0], ALONG_Y)

    def softmax_of(i, _):
        at = pl.ds(pl.multiple_of(i * rows, rows), rows)
        q = query[at, :]
        first = low(q.shape)
        for head in (0, 1):
            s = dot_nt(jnp.where(first == (head == 0), q, jnp.zeros_like(q)), key[...]) * factor
            s = jnp.where(lanes(s.shape) < seq_len, s, masked_score)
            log = lse[at, head * HEAD_DIM : head * HEAD_DIM + 1]
            soft[head, at, :] = jnp.exp(s - log).astype(bf16)
        return 0

    lax.fori_loop(0, 4, softmax_of, 0)
    tokens.spread()
    lax.fori_loop(4, 8, softmax_of, 0)
    tokens.finish()

    gu = ScatterTp(
        net,
        lambda t, half: gu_terms.at[half, :, pl.ds(pl.multiple_of(t * 128, 128), 128)],
        lambda i, half: gu_sib.at[i, half],
        lambda half: gu_far.at[half],
        lambda part, half: gu_near.at[part, half],
    )
    down = ScatterTp(
        net,
        lambda t, half: down_terms.at[half, pl.ds(pl.multiple_of(t * units, units), units)],
        lambda i, half: down_sib.at[i, half],
        lambda half: down_far.at[half],
        lambda part, half: down_near.at[part, half],
    )
    loads[1].wait()
    loads[2].wait()
    for dy in (2, 1, -1, 0):
        gu.across(dy)
        down.across(dy)

    def back(i, _):
        at = pl.ds(pl.multiple_of(i * pair, pair), pair)
        d_rows = jnp.concatenate([d_all[2 * i], d_all[2 * i + 1]], 0)
        d_o = dot_nt(d_rows, w_out[...]).astype(bf16)
        q = query[at, :]
        first = low(q.shape)
        d_q = []
        for head in (0, 1):
            own = first == (head == 0)
            d_o_head = jnp.where(own, d_o, jnp.zeros_like(d_o))
            q_head = jnp.where(own, q, jnp.zeros_like(q))
            p = soft[head, at, :]
            d_p = dot_nt(d_o_head, value[...])
            p32 = p.astype(f32)
            t = p32 * d_p
            d_s = (t - p32 * jnp.sum(t, -1, keepdims=True)).astype(bf16)
            d_q.append(dot(d_s, key[...]))
            d_key_t[...] += dot_tn(q_head, d_s)
            d_value_t[...] += dot_tn(d_o_head, p)
        d_query = (jnp.where(first, d_q[0], d_q[1]) * factor).astype(bf16).astype(f32)
        d_gained = rotate_back(d_query, cosine[at, :], sine[at, :])
        hat = q_hat[at, :]
        gain_term[8:9, :] += jnp.sum(d_gained * hat, 0, keepdims=True)
        d_raw = pair_norm_back(d_gained * gains[0:1], hat, q_scale[at, :])
        d_qkv[at, 0:128] = d_raw.astype(bf16)
        return 0

    gain_term[...] = jnp.zeros_like(gain_term)
    lax.fori_loop(0, 4, back, 0)

    gu.far()
    down.far()
    small_term[mine, :] = small_y.finish()
    small_x = AxisSum(net, small_term.at[mine], small_got.at[1], ALONG_X)

    half_dim = HEAD_DIM
    d_kv_t = jnp.concatenate(
        [
            d_key_t[:half_dim] + d_key_t[half_dim:],
            d_value_t[:half_dim] + d_value_t[half_dim:],
        ],
        0,
    )
    d_kv = d_kv_t.T
    first = low(d_kv.shape)
    d_key = (jnp.where(first, d_kv, swap(d_kv)) * factor).astype(bf16).astype(f32)
    d_gained = rotate_back(d_key, cosine[...], sine[...])
    hat = k_hat[...]
    gain_term[9:10, :] = jnp.sum(d_gained * hat, 0, keepdims=True)
    d_raw = pair_norm_back(d_gained * gains[1:2], hat, k_scale[...])
    d_qkv[:, 128:256] = jnp.where(first, d_raw, d_kv).astype(bf16)

    def spread(dy):
        def one(i, _):
            t = net.tp_at(dy, 1 - i)
            at = pl.ds(pl.multiple_of(t * rows, rows), rows)
            terms[t] = dot_nt(d_qkv[at, :], w_qkv[...]).astype(bf16)
            return 0

        lax.fori_loop(0, 2, one, 0)

    sums = ScatterTp(
        net,
        lambda t, half: terms.at[t, pl.ds(half * half_rows, half_rows)],
        lambda i, half: from_sib.at[i, pl.ds(half * half_rows, half_rows)],
        lambda half: from_far.at[half],
        lambda part, half: from_near.at[part, pl.ds(half * half_rows, half_rows)],
    )
    spread(2)
    sums.across(2)
    grad_qkv = dot(h_t[...], d_qkv[...])
    sums.far()
    spread(1)
    sums.across(1)
    spread(-1)
    sums.across(-1)
    blocks, block = grad_terms.shape[0], grad_terms.shape[1]
    for e in range(blocks):
        grad_terms[e, :, 0:256] = grad_qkv[e * block : (e + 1) * block].astype(bf16)
    products = grad_qkv * w_qkv[...].astype(f32)
    norm_sum = lax.dot_general(
        jnp.ones((8, 256), f32), products, (((1,), (1,)), ((), ())), precision=highest, preferred_element_type=f32
    )[0:1]
    norm_sum = norm_sum / norm_gain[...]
    for i in range(8):
        gain_term[i : i + 1, :] = norm_sum[:, i * 128 : (i + 1) * 128]
    gain_c = AxisSum(net, gain_term.at[0:8], gain_got.at[0, :, 0:8], [C])
    d_flat = d_all[...].reshape(group, width)
    grad_o = dot_tn(attn_o[...], d_flat).T
    for e in range(blocks):
        grad_terms[e, :, 256:384] = grad_o[e * block : (e + 1) * block].astype(bf16)
    grads = ScatterEp(net, grad_terms, grad_landed, block)
    for g in (3, 1, 2, 0):
        grads.far(g)
    sums.near()
    spread(0)
    sums.across(0)
    gain_term[0:8, :] = gain_c.finish()
    gain_y = AxisSum(net, gain_term.at[0:8], gain_got.at[1, :, 0:8], ALONG_Y)
    for g in (3, 1, 2, 0):
        grads.near(g)
    grads.turn(3)
    grads.far(4)
    grads.turn(1)
    grads.turn(2)
    grads.near(4)
    grads.turn(0)
    gain_term[0:8, :] = gain_y.finish()
    gain_x = AxisSum(net, gain_term, gain_got.at[2], ALONG_X)

    small_term[mine, :] = small_x.finish()
    small_z = AxisSum(net, small_term.at[mine], small_got.at[2], ALONG_Z)
    gu.near()
    down.near()
    x_hat, x_scale = normed(layer_input[...])
    total = jnp.concatenate([sums.last(0), sums.last(1)], 0)
    grad_input[...] = d_mid[...] + norm_back(total * norm_gain[...], x_hat, x_scale)

    for h in (0, 1):
        grad_all[net.ep, h * (block // 2) : (h + 1) * (block // 2), :] = grads.last(4, h).astype(bf16)
    spread_grads = GatherEp(net, grad_all, block)
    spread_grads.start()
    small_term[mine, :] = small_z.finish()
    small_last = net.send(small_term.at[mine], small_sib.at[mine], C)
    gain_term[...] = gain_x.finish()
    gain_z = AxisSum(net, gain_term, gain_got.at[3], ALONG_Z)
    for e in (0, 1):
        grad_gu_out[e] = gu.last(e)
        grad_down_out[e] = down.last(e)
    spread_grads.first()
    gain_out[...] = gain_z.finish()
    spread_grads.second(0)
    spread_grads.far()
    spread_grads.second(-1)
    spread_grads.second(1)
    spread_grads.second(2)
    small_last.wait_recv()
    other = pl.ds(pl.multiple_of((1 - net.c) * share, 8), share)
    small_out[mine, :] = small_term[mine, :]
    small_out[other, :] = small_sib[other, :]
    spread_grads.finish()
    for e in range(blocks):
        grad_qkv_out[e * block : (e + 1) * block, :] = grad_all[e, :, 0:256].astype(f32)
    grad_out_out[...] = grad_all[:, :, 256:384].astype(f32).reshape(blocks * block, 128).T
    net.finish()


def attend_back(layer_input, lengths, norm_gain, w_query, w_keyval, gains, w_out, cosine, sine, d_mid, attn_o, lse, small, h_all, gu_grad, down_grad):
    rows, width = layer_input.shape
    group = attn_o.shape[0]
    units = down_grad.shape[1] // 8
    n_small = small.shape[0]
    block = width // 16
    row_bf = pltpu.VMEM((group, 128), bf16)
    row_f = pltpu.VMEM((group, 128), f32)
    eight = pltpu.VMEM((8, rows, width), bf16)
    return pl.pallas_call(
        attend_back_kernel,
        name="attend_back",
        out_shape=(
            shaped((rows, width), f32),
            shaped((width, 256), f32),
            shaped((128, width), f32),
            shaped((16, 128), f32),
            shaped((n_small, width), f32),
            shaped((2, width, 128), f32),
            shaped((2, units, width), f32),
        ),
        in_specs=[VM, SM] + [VM] * 11 + [ANY] * 3,
        out_specs=(VM,) * 7,
        scratch_shapes=[
            eight,
            eight,
            pltpu.VMEM((width, 256), bf16),
            row_bf, row_bf, row_bf,
            row_f, row_f, row_f, row_f,
            pltpu.VMEM((2, group, group), bf16),
            pltpu.VMEM((128, group), f32),
            pltpu.VMEM((128, group), f32),
            pltpu.VMEM((group, 256), bf16),
            pltpu.VMEM((width, group), bf16),
            eight,
            pltpu.VMEM((4, rows, width), bf16),
            pltpu.VMEM((2, rows // 2, width), bf16),
            pltpu.VMEM((2, rows, width), bf16),
            pltpu.VMEM((2, width, width), bf16),
            pltpu.VMEM((4, 2, width, 128), bf16),
            pltpu.VMEM((2, width, 128), bf16),
            pltpu.VMEM((2, 2, width, 128), bf16),
            pltpu.VMEM((2, 8 * units, width), bf16),
            pltpu.VMEM((4, 2, units, width), bf16),
            pltpu.VMEM((2, units, width), bf16),
            pltpu.VMEM((2, 2, units, width), bf16),
            pltpu.VMEM((16, block, 384), bf16),
            pltpu.VMEM((5, 2, 3, block // 2, 384), bf16),
            pltpu.VMEM((16, block, 384), bf16),
            pltpu.VMEM((n_small, width), f32),
            pltpu.VMEM((n_small, width), f32),
            pltpu.VMEM((3, 3, n_small // 2, width), f32),
            pltpu.VMEM((16, 128), f32),
            pltpu.VMEM((4, 3, 16, 128), f32),
            pltpu.SemaphoreType.DMA((200,)),
            pltpu.SemaphoreType.DMA((200,)),
        ],
        compiler_params=params(3, 60),
    )(layer_input, lengths, norm_gain.reshape(1, -1), w_query, w_keyval, gains, w_out, cosine, sine, d_mid, attn_o, lse, small, h_all, gu_grad, down_grad)


def local(
    layer_input,
    lengths,
    routes,
    norm_gain,
    w_query,
    w_keyval,
    query_gain,
    key_gain,
    w_out,
    mlp_gain,
    w_router,
    w_gate,
    w_up,
    w_down,
    cotangent,
):
    rows, width = layer_input.shape
    group = rows * 8
    n_exp = w_router.shape[1]
    top_k = routes.shape[1]
    cosine, sine = rotary(group)
    gains = jnp.stack([query_gain, jnp.concatenate([key_gain, key_gain])])
    keyval = w_keyval.reshape(width, -1)
    w_gu = jnp.concatenate([w_gate, w_up], -1)
    routes_t = routes.T
    all_valid = (jnp.arange(group)[None, :] < lengths[:, None]).reshape(1, -1)
    hit = (routes_t[None] == jnp.arange(n_exp)[:, None, None]) & all_valid[None]
    counts = jnp.sum(hit.astype(f32), (1, 2)).reshape(n_exp, 1)
    nvalid = jnp.sum(lengths).astype(f32)
    h_mid, h_all, attn_o, lse, cot_all, gu_all, down_all = attend(
        layer_input, lengths, norm_gain, w_query, keyval, gains, w_out, cosine, sine, cotangent, w_gu, w_down
    )
    output, d_mid, small, gu_grad, down_grad = experts(
        h_mid, lengths, routes_t, mlp_gain, w_router.T, counts, cotangent, cot_all, gu_all, down_all
    )
    grad_input, grad_qkv, grad_out, gain_grads, small, grad_gu, grad_down = attend_back(
        layer_input, lengths, norm_gain, w_query, keyval, gains, w_out, cosine, sine, d_mid, attn_o, lse, small,
        h_all, gu_grad, down_grad,
    )
    prob_total = small[n_exp + 8, :n_exp]
    loss = n_exp * jnp.sum(counts[:, 0] / (top_k * nvalid) * (prob_total / nvalid))
    return (
        output,
        grad_input,
        loss,
        gain_grads[:8].reshape(-1),
        grad_qkv[:, :128],
        grad_qkv[:, 128:].reshape(w_keyval.shape),
        gain_grads[8],
        gain_grads[9, :HEAD_DIM],
        grad_out,
        small[n_exp],
        small[:n_exp].T,
        grad_gu[:, :, :HEAD_DIM],
        grad_gu[:, :, HEAD_DIM:],
        grad_down,
    )


def solution(mesh):
    in_specs = (
        P(("ep", "tp"), None),
        P(),
        P(),
        P(),
        P(None, "tp"),
        P(None, "tp", None),
        P("tp"),
        P("tp"),
        P("tp", None),
        P(),
        P(),
        P("ep", None, "tp"),
        P("ep", None, "tp"),
        P("ep", "tp", None),
        P(("ep", "tp"), None),
    )
    out_specs = (
        P(("ep", "tp"), None),
        P(("ep", "tp"), None),
        P(),
        P(),
        P(None, "tp"),
        P(None, "tp", None),
        P("tp"),
        P("tp"),
        P("tp", None),
        P(),
        P(),
        P("ep", None, "tp"),
        P("ep", None, "tp"),
        P("ep", "tp", None),
    )
    return jax.shard_map(local, mesh=mesh, in_specs=in_specs, out_specs=out_specs, check_vma=False)
```

```python
import jax
import jax.numpy as jnp
import numpy as np
from jax import lax
from jax.experimental import pallas as pl
from jax.experimental.pallas import tpu as pltpu
from jax.sharding import PartitionSpec as P

MESH = pl.DeviceIdType.MESH
f32, bf16 = jnp.float32, jnp.bfloat16
HEAD_DIM = 64
epsilon = 1e-06
masked_score = -1e30
highest = lax.Precision.HIGHEST
MIB = 2**20

X, Y, Z, C = (1, 0, 0, 0), (0, 1, 0, 0), (0, 0, 1, 0), (0, 0, 0, 1)
XM, YM, ZM = (-1, 0, 0, 0), (0, -1, 0, 0), (0, 0, -1, 0)
X2, Z2 = (2, 0, 0, 0), (0, 0, 2, 0)
NEAR = (0, 1, -1, 2)


def times(d, k):
    return tuple(v * k for v in d)


class Net:
    def __init__(self, send_sems, recv_sems):
        self.ep, self.tp = lax.axis_index("ep"), lax.axis_index("tp")
        self.x, self.z = self.ep // 4, self.ep % 4
        self.y, self.c = self.tp // 2, self.tp % 2
        self.send_sems, self.recv_sems = send_sems, recv_sems
        self.count = 0
        self.unsent = {}
        self.group = None

    def device(self, d):
        x, y = (self.x + d[0]) % 4, (self.y + d[1]) % 4
        z, c = (self.z + d[2]) % 4, (self.c + d[3]) % 2
        return (x * 4 + z, y * 2 + c)

    def ep_at(self, dx, dz):
        return ((self.x + dx) % 4) * 4 + (self.z + dz) % 4

    def tp_at(self, dy, dc):
        return ((self.y + dy) % 4) * 2 + (self.c + dc) % 2

    def barrier(self, dirs):
        sem = pltpu.get_barrier_semaphore()
        for d in dirs:
            pl.semaphore_signal(sem, inc=1, device_id=self.device(d), device_id_type=MESH)
        pl.semaphore_wait(sem, len(dirs))

    def send(self, src, dst, d):
        i = self.count
        self.count += 1
        copy = pltpu.make_async_remote_copy(
            src_ref=src,
            dst_ref=dst,
            send_sem=self.send_sems.at[i],
            recv_sem=self.recv_sems.at[i],
            device_id=self.device(d),
            device_id_type=MESH,
        )
        copy.start()
        self.unsent.setdefault(self.group, []).append(copy)
        return copy

    def keep(self, src, dst):
        i = self.count
        self.count += 1
        copy = pltpu.make_async_copy(src, dst, self.send_sems.at[i])
        copy.start()
        return copy

    def sent(self, copy):
        copy.wait_send()
        for group, copies in self.unsent.items():
            self.unsent[group] = [c for c in copies if c is not copy]

    def finish(self, *groups):
        for group in groups or tuple(self.unsent):
            for copy in self.unsent.pop(group, ()):
                copy.wait_send()


class GatherTp:
    def __init__(self, net, ref, own=None):
        self.net, self.ref = net, ref
        self.own = own or (lambda half: ref(net.tp, half))
        self.copies = {}
        self.done = set()

    def wait(self, *key):
        if key not in self.done:
            self.done.add(key)
            self.copies[key].wait_recv()

    def along(self, dy, half, sign):
        src = self.own(half) if dy == 0 else self.ref(self.net.tp_at(dy, 0), half)
        to = (dy - sign + 1) % 4 - 1
        self.copies[("y", to, half)] = self.net.send(
            src, self.ref(self.net.tp_at(dy, 0), half), times(Y, sign)
        )

    def across(self, dy):
        for half in (0, 1):
            src = self.own(half) if dy == 0 else self.ref(self.net.tp_at(dy, 0), half)
            self.copies[("c", dy, half)] = self.net.send(
                src, self.ref(self.net.tp_at(dy, 0), half), C
            )

    def start(self):
        self.along(0, 0, 1)
        self.along(0, 1, -1)
        self.along(0, 1, 1)
        self.along(0, 0, -1)
        self.across(0)

    def relay(self):
        self.wait("y", -1, 0)
        self.along(-1, 0, 1)
        self.wait("y", 1, 1)
        self.along(1, 1, -1)
        for dy, half in ((-1, 1), (1, 0)):
            self.wait("y", dy, half)
            self.across(dy)

    def spread(self):
        for half in (0, 1):
            self.wait("y", 2, half)
        self.across(2)

    def need(self, dy, dc):
        if dc:
            for half in (0, 1):
                self.wait("c", dy, half)
        elif dy:
            for half in (0, 1):
                self.wait("y", dy, half)

    def finish(self):
        for key in list(self.copies):
            self.wait(*key)


class ScatterTp:
    def __init__(self, net, ref, sib, far, near):
        self.net, self.ref, self.sib, self.far_at, self.near_at = net, ref, sib, far, near
        self.copies = {}

    def across(self, dy):
        i = NEAR.index(dy)
        for half in (0, 1):
            self.copies[("c", dy, half)] = self.net.send(
                self.ref(self.net.tp_at(dy, 1), half), self.sib(i, half), C
            )

    def join(self, dy, half):
        self.copies[("c", dy, half)].wait_recv()
        return self.ref(self.net.tp_at(dy, 0), half)[...].astype(f32) + self.sib(
            NEAR.index(dy), half
        )[...].astype(f32)

    def far(self):
        for half, sign in ((0, 1), (1, -1)):
            ref = self.ref(self.net.tp_at(2, 0), half)
            ref[...] = self.join(2, half).astype(bf16)
            self.copies[("f", half)] = self.net.send(ref, self.far_at(half), times(Y, sign))

    def near(self):
        for part, sign in ((0, 1), (1, -1)):
            for half in (1 - part, part):
                ref = self.ref(self.net.tp_at(sign, 0), half)
                total = self.join(sign, half)
                if half == part:
                    self.copies[("f", part)].wait_recv()
                    total = total + self.far_at(part)[...].astype(f32)
                ref[...] = total.astype(bf16)
                self.copies[("n", part, half)] = self.net.send(
                    ref, self.near_at(part, half), times(Y, sign)
                )

    def last(self, half):
        total = self.join(0, half)
        for part in (0, 1):
            self.copies[("n", part, half)].wait_recv()
            total = total + self.near_at(part, half)[...].astype(f32)
        return total


class GatherEp:
    def __init__(self, net, buf, rows):
        self.net, self.buf, self.rows = net, buf, rows
        self.copies = {}
        self.done = set()

    def ref(self, h, j, k, part):
        half, quarter = self.rows // 2, self.rows // 4
        e = self.net.ep_at(j, k) if h == 0 else self.net.ep_at(k, j)
        if part is None:
            return self.buf.at[e, pl.ds(h * half, half)]
        return self.buf.at[e, pl.ds(h * half + part * quarter, quarter)]

    def send(self, h, j, k, part, along, sign):
        d = (X, Z)[along if h == 0 else 1 - along]
        r = self.ref(h, j, k, part)
        to = (j - sign, k) if along == 0 else (j, k - sign)
        to = tuple((v + 1) % 4 - 1 for v in to)
        self.copies[(h, *to, part)] = self.net.send(r, r, times(d, sign))

    def wait(self, *key):
        if key not in self.done:
            self.done.add(key)
            self.copies[key].wait_recv()

    def need(self, h, j, k):
        if (j, k) != (0, 0):
            for part in (None,) if (h, j, k, None) in self.copies else (0, 1):
                self.wait(h, j, k, part)

    def block(self, dx, dz):
        self.need(0, dx, dz)
        self.need(1, dz, dx)

    def start(self):
        for along in (0, 1):
            for h in (0, 1):
                for sign in (1, -1):
                    self.send(h, 0, 0, None, along, sign)

    def first(self):
        for part, sign in ((0, 1), (1, -1)):
            for h in (0, 1):
                self.wait(h, -sign, 0, None)
                self.send(h, -sign, 0, part, 0, sign)
        for sign in (1, -1):
            for h in (0, 1):
                for turn in (1, -1):
                    self.send(h, -sign, 0, None, 1, turn)

    def far(self):
        for h in (0, 1):
            self.need(h, 2, 0)
            for turn in (1, -1):
                self.send(h, 2, 0, None, 1, turn)

    def second(self, j):
        for part, sign in ((0, 1), (1, -1)):
            for h in (0, 1):
                self.wait(h, j, -sign, None)
                self.send(h, j, -sign, part, 1, sign)

    def finish(self):
        for key in list(self.copies):
            self.wait(*key)


class ScatterEp:
    def __init__(self, net, term, landed, rows):
        self.net, self.term, self.landed, self.rows = net, term, landed, rows
        self.copies = {}

    def ref(self, h, g, j, part):
        j, k = (j, NEAR[g]) if g < 4 else (0, j)
        half, quarter = self.rows // 2, self.rows // 4
        e = self.net.ep_at(k, j) if h == 0 else self.net.ep_at(j, k)
        if part is None:
            return self.term(e, h * half, half)
        return self.term(e, h * half + part * quarter, quarter)

    def slot(self, g, h, which, part=None):
        half, quarter = self.rows // 2, self.rows // 4
        i = (g * 2 + h) * 3 + which
        return self.landed(i, 0, half) if part is None else self.landed(i, part * quarter, quarter)

    def dir(self, h, g, sign):
        return times((Z, X)[(g == 4) if h == 0 else (g != 4)], sign)

    def far(self, g):
        for h in (0, 1):
            for part, sign in ((0, 1), (1, -1)):
                self.copies[(g, h, 2, part)] = self.net.send(
                    self.ref(h, g, 2, part), self.slot(g, h, 2, part), self.dir(h, g, sign)
                )

    def near(self, g):
        for h in (0, 1):
            for part, sign in ((0, 1), (1, -1)):
                self.copies[(g, h, 2, part)].wait_recv()
                r = self.ref(h, g, sign, part)
                r[...] = (r[...].astype(f32) + self.slot(g, h, 2, part)[...].astype(f32)).astype(bf16)
                self.copies[(g, h, part)] = self.net.send(
                    self.ref(h, g, sign, None), self.slot(g, h, part), self.dir(h, g, sign)
                )

    def last(self, g, h):
        for part in (0, 1):
            self.copies[(g, h, part)].wait_recv()
        total = self.ref(h, g, 0, None)[...].astype(f32)
        for part in (0, 1):
            total = total + self.slot(g, h, part)[...].astype(f32)
        return total

    def turn(self, g):
        for h in (0, 1):
            self.ref(h, g, 0, None)[...] = self.last(g, h).astype(bf16)


def lanes(shape):
    return lax.broadcasted_iota(jnp.int32, shape, len(shape) - 1)


def low(shape):
    return lanes(shape) < HEAD_DIM


def normed(v):
    factor = lax.rsqrt(jnp.mean(v * v, -1, keepdims=True) + epsilon)
    return v * factor, factor


def norm_back(grad, hat, factor):
    return factor * (grad - hat * jnp.mean(grad * hat, -1, keepdims=True))


def pair_sums(v):
    first = low(v.shape)
    a = jnp.sum(jnp.where(first, v, 0.0), -1, keepdims=True)
    b = jnp.sum(jnp.where(first, 0.0, v), -1, keepdims=True)
    return jnp.where(first, a, b)


def pair_normed(v):
    factor = lax.rsqrt(pair_sums(v * v) / HEAD_DIM + epsilon)
    return v * factor, factor


def pair_norm_back(grad, hat, factor):
    return factor * (grad - hat * (pair_sums(grad * hat) / HEAD_DIM))


def partner(v):
    half = HEAD_DIM // 2
    return jnp.where(
        lanes(v.shape) % HEAD_DIM < half, pltpu.roll(v, 128 - half, 1), pltpu.roll(v, half, 1)
    )


def rotate(v, cosine, sine):
    return v * cosine + partner(v) * sine


def rotate_back(v, cosine, sine):
    return v * cosine - partner(v) * sine


def swap(v):
    return pltpu.roll(v, HEAD_DIM, v.ndim - 1)


def dot(a, b):
    return jnp.dot(a, b, preferred_element_type=f32)


def dot_nt(a, b):
    return lax.dot_general(a, b, (((1,), (1,)), ((), ())), preferred_element_type=f32)


def dot_tn(a, b):
    return lax.dot_general(a, b, (((0,), (0,)), ((), ())), preferred_element_type=f32)


def rotary(length):
    half = HEAD_DIM // 2
    frequency = 10000.0 ** (-(np.arange(half, dtype=np.float64) * 2.0 / HEAD_DIM))
    angles = np.arange(length, dtype=np.float64)[:, None] * frequency[None, :]
    cosine, sine = np.cos(angles), np.sin(angles)
    cosine = np.concatenate([cosine] * 4, -1).astype(np.float32)
    sine = np.concatenate([-sine, sine] * 2, -1).astype(np.float32)
    return cosine, sine


VM = pl.BlockSpec(memory_space=pltpu.VMEM)
SM = pl.BlockSpec(memory_space=pltpu.SMEM)
ANY = pl.BlockSpec(memory_space=pl.ANY)


def shaped(shape, dtype):
    return jax.ShapeDtypeStruct(shape, dtype)


def params(collective_id, vmem):
    return pltpu.CompilerParams(
        collective_id=collective_id, has_side_effects=True, vmem_limit_bytes=int(vmem * MIB)
    )


def key_value(qkv, q_gain, k_gain, cosine, sine):
    q_hat, _ = pair_normed(qkv[:, :128])
    kv = qkv[:, 128:]
    first = low(kv.shape)
    other = swap(kv)
    k_raw = jnp.where(first, kv, other)
    k_hat, _ = pair_normed(k_raw)
    query = rotate(q_hat * q_gain, cosine, sine).astype(bf16)
    key = rotate(k_hat * k_gain, cosine, sine).astype(bf16)
    value = jnp.where(first, other, kv).astype(bf16)
    return query, key, value, qkv[:, :128], k_raw


class Exchange:
    def __init__(self, net, out, half_way, got):
        self.net, self.out, self.half_way, self.got = net, out, half_way, got

    def start(self):
        net = self.net
        self.first = [
            net.send(self.out.at[(net.x + k) % 4], self.half_way.at[net.x], times(X, k))
            for k in (1, -1, 2)
        ]
        self.half_way[net.x] = self.out[net.x]

    def turn(self):
        net = self.net
        for copy in self.first:
            copy.wait_recv()
        self.second = [
            net.send(self.half_way.at[:, (net.z + k) % 4], self.got.at[:, net.z], times(Z, k))
            for k in (1, -1, 2)
        ]
        self.got[:, net.z] = self.half_way[:, net.z]

    def finish(self):
        for copy in self.second:
            copy.wait_recv()


class AxisSum:
    def __init__(self, net, term, slots, steps):
        self.net, self.term, self.slots = net, term, slots
        self.copies = [net.send(term, slots.at[i], d) for i, d in enumerate(steps)]

    def finish(self):
        total = self.term[...]
        for i, copy in enumerate(self.copies):
            copy.wait_recv()
            total = total + self.slots[i]
            self.net.sent(copy)
        return total


ALONG_X, ALONG_Y, ALONG_Z = ([times(d, k) for k in (1, -1, 2)] for d in (X, Y, Z))
Y2 = times(Y, 2)

ORDER = (
    (0, 0), (-1, 0), (1, 0), (0, -1),
    (0, 1), (2, 0), (0, 2), (-1, -1),
    (-1, 1), (1, -1), (1, 1), (2, -1),
    (2, 1), (-1, 2), (1, 2), (2, 2),
)
BATCH = 4


def layer_kernel(*refs, inputs, outputs, scratch):
    names = inputs + outputs + scratch
    r = dict(zip(names, refs, strict=True))

    class R:
        pass

    v = R()
    for name, ref in r.items():
        setattr(v, name, ref)
    v.lse, v.q_raw, v.d_key_t = v.grad_query, v.grad_keyval, v.grad_out
    v.d_value_t, v.x, v.cot_f = v.grad_gate, v.grad_up, v.grad_down
    net = Net(v.send_sems, v.recv_sems)
    rows, width = v.output.shape
    half_rows = rows // 2
    group = rows * 8
    units = v.w_down.shape[1]
    ff = units * 8
    n_exp = v.w_router_t.shape[0]
    slots = v.places.shape[1] // 2
    full = 16 * slots
    seq_len = v.lengths[net.ep]
    factor = HEAD_DIM**-0.5

    def weight(a, j, t):
        return v.w.at[j, pl.ds(pl.multiple_of(a * ff + t * units, units), units)]

    def rows_of(i, count=1):
        return pl.ds(pl.multiple_of(i * rows, rows), rows * count)

    def half_of(t, half):
        return pl.ds(pl.multiple_of(t * rows + half * half_rows, half_rows), half_rows)

    x_load = [net.keep(v.layer_input.at[pl.ds(i * half_rows, half_rows)], v.x.at[i]) for i in (0, 1)]
    early = [
        net.keep(v.w_query, v.w_qkv.at[:, pl.ds(0, 128)]),
        net.keep(v.w_keyval, v.w_qkv.at[:, pl.ds(128, 128)]),
        net.keep(v.cosine_in, v.cosine),
        net.keep(v.sine_in, v.sine),
    ]
    cot_load = [net.keep(v.cotangent.at[pl.ds(i * half_rows, half_rows)], v.cot_f.at[i]) for i in (0, 1)]
    weight_loads = [
        net.keep(source.at[j], weight(a, j, net.tp))
        for a, source in enumerate((v.w_gate, v.w_up, v.w_down))
        for j in (0, 1)
    ]
    late = [net.keep(v.routes_in, v.routes), net.keep(v.w_out_in, v.w_out)]
    net.barrier([X, XM, X2, Y, YM, Y2, Z, ZM, Z2, C])

    for copy in x_load:
        copy.wait()
    x_hat, _ = normed(v.x[...].reshape(rows, width))
    v.spare[rows_of(net.tp), :] = (x_hat * v.norm_gain[...]).astype(bf16)
    tokens = GatherTp(net, lambda t, half: v.spare.at[half_of(t, half)])
    tokens.start()
    place = net.tp * rows + lax.broadcasted_iota(jnp.int32, (rows, 1), 0)
    for copy in cot_load:
        copy.wait()
    v.cot[net.ep] = jnp.where(place < seq_len, v.cot_f[...].reshape(rows, width), 0.0).astype(bf16)
    cots = GatherEp(net, v.cot, rows)
    net.group = "cot"
    cots.start()
    net.group = None

    for copy in early + late:
        copy.wait()
    v.k_gain[:, 0:HEAD_DIM] = v.key_gain[...]
    k_gain = v.k_gain[...]
    k_gain = jnp.where(low(k_gain.shape), k_gain, swap(k_gain))
    q_gain = v.query_gain[...]

    def project(dy):
        def one(i, _):
            t = net.tp_at(dy, i)
            at = rows_of(t)
            h = v.spare[at, :]
            parts = key_value(dot(h, v.w_qkv[...]), q_gain, k_gain, v.cosine[at, :], v.sine[at, :])
            for ref, part in zip((v.query, v.key, v.value, v.q_raw, v.k_raw), parts, strict=True):
                ref[at, :] = part
            v.h_t[:, at] = h.T
            return 0

        lax.fori_loop(0, 2, one, 0)

    def routing():
        for s in range(16):
            segment = v.routes[:, rows_of(s * 8 + net.tp)]
            for j in (0, 1):
                same = (segment == net.ep * 2 + j).astype(f32)
                v.hits[2 * s + j : 2 * s + j + 1, :] = jnp.max(same, 0, keepdims=True)
        before = lax.broadcasted_iota(jnp.int32, (rows, rows), 0) < lanes((rows, rows))
        rank = dot(v.hits[...].astype(bf16), before.astype(bf16))
        rank = jnp.where(v.hits[...] > 0.5, rank, -1.0)
        slot = lax.broadcasted_iota(jnp.int32, (slots, rows), 0).astype(f32)
        for s in range(16):
            for j in (0, 1):
                mine = rank[2 * s + j : 2 * s + j + 1]
                v.places[s, j * slots : (j + 1) * slots, :] = (slot == mine).astype(bf16)

    def count():
        v.counted[...] = jnp.zeros_like(v.counted)

        def one(g, _):
            segment = v.routes[:, pl.ds(pl.multiple_of(g * group, group), group)]
            segment = jnp.where(lanes(segment.shape) < v.lengths[g], segment, -1)
            for e in range(n_exp):
                hit = (segment == e).astype(f32)
                total = hit[:, 0:128]
                for i in range(1, group // 128):
                    total = total + hit[:, i * 128 : (i + 1) * 128]
                v.counted[e] += total
            return 0

        lax.fori_loop(0, 16, one, 0)

    routing()
    tokens.relay()
    tokens.need(0, 1)
    project(0)
    cots_step = lambda step, *a: (setattr(net, "group", "cot"), step(*a), setattr(net, "group", None))
    cots_step(cots.first)
    tokens.spread()
    tokens.need(-1, 1)
    project(-1)
    tokens.need(1, 1)
    project(1)
    cots_step(cots.second, 0)
    for copy in weight_loads:
        copy.wait()
    net.group = "w"
    gate, up, down = (
        GatherTp(net, lambda t, half, a=a: weight(a, half, t)) for a in range(3)
    )
    gate.start()
    net.group = None
    tokens.need(2, 1)
    project(2)
    tokens.finish()

    def attend(dy):
        def one(i, _):
            t = net.tp_at(dy, 1 - i)
            at = rows_of(t)
            q = v.query[at, :]
            first = low(q.shape)
            mixed, logs = [], []
            for head in (0, 1):
                q_head = jnp.where(first == (head == 0), q, jnp.zeros_like(q))
                s = dot_nt(q_head, v.key[...]) * factor
                s = jnp.where(lanes(s.shape) < seq_len, s, masked_score)
                top = jnp.max(s, -1, keepdims=True)
                p = jnp.exp(s - top)
                total = jnp.sum(p, -1, keepdims=True)
                mixed.append(dot((p * (1.0 / total)).astype(bf16), v.value[...]))
                logs.append(top + jnp.log(total))
            o = jnp.where(first, mixed[0], mixed[1]).astype(bf16)
            v.attn_o[at, :] = o
            v.lse[at, :] = jnp.where(first, logs[0], logs[1])
            v.spare[rows_of(8 + t), :] = dot(o, v.w_out[...]).astype(bf16)
            return 0

        lax.fori_loop(0, 2, one, 0)

    def token_sums():
        return ScatterTp(
            net,
            lambda t, half: v.spare.at[half_of(8 + t, half)],
            lambda i, half: v.from_sib.at[i, pl.ds(half * half_rows, half_rows)],
            lambda half: v.from_far.at[half],
            lambda part, half: v.from_near.at[part, pl.ds(half * half_rows, half_rows)],
        )

    w_step = lambda step, *a: (setattr(net, "group", "w"), step(*a), setattr(net, "group", None))
    sums = token_sums()
    attend(2)
    sums.across(2)
    cots_step(cots.far)
    w_step(gate.relay)
    attend(1)
    sums.across(1)
    sums.far()
    w_step(up.start)
    cots_step(cots.second, -1)
    attend(-1)
    sums.across(-1)
    sums.near()
    w_step(gate.spread)
    cots_step(cots.second, 1)
    attend(0)
    sums.across(0)
    cots_step(cots.second, 2)
    w_step(up.relay)
    count()
    h_mid = v.output
    for half in (0, 1):
        at = pl.ds(half * half_rows, half_rows)
        h_mid[at, :] = v.x[half] + sums.last(half)
    net.finish(None)

    h_hat, h_scale = normed(h_mid[...])
    mlp_in = h_hat * v.mlp_gain[...]
    v.tok[net.ep] = mlp_in.astype(bf16)
    tokens = GatherEp(net, v.tok, rows)
    tokens.start()
    w_step(down.start)

    w_router_t = v.w_router_t
    logits = lax.dot_general(
        w_router_t[...], mlp_in, (((1,), (1,)), ((), ())), precision=highest, preferred_element_type=f32
    )
    token_at = net.tp * rows + lanes((1, rows))
    valid = jnp.where(token_at < seq_len, 1.0, 0.0)
    expert = lax.broadcasted_iota(jnp.int32, (n_exp, rows), 0)
    mine = v.routes[:, rows_of(net.ep * 8 + net.tp)]
    chosen = expert == mine[0:1]
    for k in range(1, mine.shape[0]):
        chosen = jnp.logical_or(chosen, expert == mine[k : k + 1])
    top = jnp.max(logits, 0, keepdims=True)
    weights = jnp.exp(logits - top)
    probs = weights / jnp.sum(weights, 0, keepdims=True)
    top = jnp.max(jnp.where(chosen, logits, masked_score), 0, keepdims=True)
    weights = jnp.where(chosen, jnp.exp(jnp.where(chosen, logits - top, 0.0)), 0.0)
    soft = weights / jnp.sum(weights, 0, keepdims=True)
    v.probs[...] = probs
    v.soft[...] = soft
    gates = soft * valid
    for e in range(16):
        v.gate_out[e // 4, e % 4, 0:2, :] = gates[2 * e : 2 * e + 2]
    to_owners = Exchange(net, v.gate_out, v.gate_mid, v.gate_got)
    to_owners.start()

    w_step(up.spread)
    tokens.first()
    to_owners.turn()
    cots.finish()
    net.finish("cot")
    gate.finish()
    up.finish()
    w_step(down.relay)
    to_owners.finish()

    n = BATCH * slots

    def picked(j, at, count):
        return pl.ds(pl.multiple_of(j * full + at, slots), count)

    def d_picked(j, at, count):
        return pl.ds(pl.multiple_of((2 + j) * full + at, slots), count)

    def batch(b):
        members = []
        for i, (dx, dz) in enumerate(ORDER[b * BATCH : (b + 1) * BATCH]):
            tokens.block(dx, dz)
            s = net.ep_at(dx, dz)
            members.append((s, (net.x + dx) % 4, (net.z + dz) % 4))
            here = v.places[s]
            taken = dot(here, v.tok[s]).astype(bf16)
            taken_d = dot(here, v.cot[s]).astype(bf16)
            for j in (0, 1):
                v.big[picked(j, b * n + i * slots, slots), :] = taken[j * slots : (j + 1) * slots]
                v.big[d_picked(j, b * n + i * slots, slots), :] = taken_d[j * slots : (j + 1) * slots]

        def one(j, _):
            at, at_d = picked(j, b * n, n), d_picked(j, b * n, n)
            gate_col = []
            for s, sx, sz in members:
                here = v.places[s, pl.ds(pl.multiple_of(j * slots, slots), slots), :].astype(f32)
                gate_col.append(jnp.sum(here * v.gate_got[sx, sz, pl.ds(j, 1), :], -1, keepdims=True))
            gate_col = jnp.concatenate(gate_col, 0)
            d_rows = v.big[at_d, :].astype(f32)
            d_row = (gate_col * d_rows).astype(bf16)
            v.big[at_d, :] = d_row
            pre = dot_nt(v.big[at, :], v.w[j, 0 : 2 * ff])
            d_hidden = dot_nt(d_row, v.w[j, 2 * ff :])
            g, u = pre[:, :ff], pre[:, ff:]
            sigma = 1.0 / (1.0 + jnp.exp(-g))
            act = g * sigma
            hid = (act * u).astype(bf16)
            v.deep[pl.ds(2 * full + b * n, n), pl.ds(pl.multiple_of(j * ff, ff), ff)] = hid
            d_g = d_hidden * u * sigma * (1.0 + g * (1.0 - sigma))
            v.deep[at, 0:ff] = d_g.astype(bf16)
            v.deep[at, ff:] = (d_hidden * act).astype(bf16)
            out = dot(hid, v.w[j, 2 * ff :]).astype(bf16).astype(f32)
            d_gate = jnp.sum(out * d_rows, -1, keepdims=True)
            v.spare[picked(j, b * n, n), :] = (gate_col * out).astype(bf16)
            v.row_back[j] = dot(v.deep[at, :], v.w[j, 0 : 2 * ff]).astype(bf16)
            for i, (s, sx, sz) in enumerate(members):
                here = v.places[s, pl.ds(pl.multiple_of(j * slots, slots), slots), :].astype(f32)
                d = jnp.sum(here * d_gate[i * slots : (i + 1) * slots], 0, keepdims=True)
                v.back_out[sx, sz, pl.ds(j, 1), :] = d
            return 0

        lax.fori_loop(0, 2, one, 0)
        for i, (s, _, _) in enumerate(members):
            at = pl.ds(i * slots, slots)
            both = jnp.concatenate([v.row_back[0, at, :], v.row_back[1, at, :]], 0)
            v.cot[s] = dot_tn(v.places[s], both).astype(bf16)

    tokens.second(0)
    tokens.far()
    w_step(down.spread)
    down.finish()
    net.finish("w")
    batch(0)
    tokens.second(-1)
    batch(1)
    tokens.second(1)
    tokens.second(2)
    batch(2)
    tokens.finish()
    net.finish(None)
    batch(3)

    to_tokens = Exchange(net, v.back_out, v.back_mid, v.back_got)
    to_tokens.start()
    row_sums = ScatterEp(
        net,
        lambda e, start, count: v.cot.at[e, pl.ds(start, count)],
        lambda i, start, count: v.landed.at[i, pl.ds(start, count)],
        rows,
    )
    mix_sums = ScatterEp(
        net,
        lambda e, start, count: v.big.at[pl.ds(pl.multiple_of(e * rows + start, 16), count)],
        lambda i, start, count: v.tok.at[i // 2, pl.ds(i % 2 * half_rows + start, count)],
        rows,
    )
    for g in (3, 1, 2, 0):
        row_sums.far(g)
    to_tokens.turn()

    def grads(j, _):
        v.w[j, 0 : 2 * ff] = dot_tn(
            v.deep[picked(j, 0, full), :], v.big[picked(j, 0, full), :]
        ).astype(bf16)
        hidden = v.deep[2 * full : 3 * full, pl.ds(pl.multiple_of(j * ff, ff), ff)]
        v.w[j, 2 * ff :] = dot_tn(hidden, v.big[d_picked(j, 0, full), :]).astype(bf16)
        return 0

    for g in (3, 1, 2, 0):
        row_sums.near(g)
    lax.fori_loop(0, 2, grads, 0)
    gate, up, down = (
        ScatterTp(
            net,
            lambda t, half, a=a: weight(a, half, t),
            lambda i, half, a=a: v.w_sib.at[i, a, half],
            lambda half, a=a: v.w_far.at[a, half],
            lambda part, half, a=a: v.w_near.at[part, a, half],
        )
        for a in range(3)
    )
    for dy in (2, 1, -1, 0):
        for sum_ in (gate, up, down):
            sum_.across(dy)
    row_sums.turn(3)
    row_sums.far(4)
    row_sums.turn(1)
    row_sums.turn(2)
    row_sums.near(4)
    row_sums.turn(0)
    for sum_ in (gate, up, down):
        sum_.far()
    for s in range(16):
        i = [(net.ep_at(dx, dz)) for dx, dz in ORDER][s]
        both = jnp.concatenate([v.spare[picked(j, s * slots, slots), :] for j in (0, 1)], 0)
        v.big[rows_of(i), :] = dot_tn(v.places[i], both).astype(bf16)
    to_tokens.finish()

    for e in range(16):
        v.d_gates[2 * e : 2 * e + 2, :] = v.back_got[e // 4, e % 4, 0:2, :]
    probs, soft = v.probs[...], v.soft[...]
    d_gates = v.d_gates[...] * valid
    d_chosen = soft * (d_gates - jnp.sum(soft * d_gates, 0, keepdims=True))
    nvalid = jnp.int32(0)
    for e in range(16):
        nvalid = nvalid + v.lengths[e]
    nvalid = nvalid.astype(f32)
    counts = jnp.sum(jnp.sum(v.counted[...], 1), -1, keepdims=True)
    balance = n_exp * counts / (8 * nvalid * nvalid)
    d_logits = d_chosen + valid * probs * (balance - jnp.sum(probs * balance, 0, keepdims=True))
    d_mlp_in = lax.dot_general(
        d_logits, w_router_t[...], (((0,), (0,)), ((), ())), precision=highest, preferred_element_type=f32
    )
    h_hat, h_scale = normed(h_mid[...])
    mlp_in = h_hat * v.mlp_gain[...]
    small = v.small
    small[0:n_exp, :] = jnp.dot(d_logits, mlp_in, precision=highest, preferred_element_type=f32)
    small[n_exp + 8 :, :] = jnp.zeros((8, width), f32)
    small[n_exp + 8 :, 0:n_exp] = lax.dot_general(
        valid + jnp.zeros((8, rows), f32), probs, (((1,), (1,)), ((), ())), precision=highest, preferred_element_type=f32
    )
    total = jnp.concatenate([row_sums.last(4, 0), row_sums.last(4, 1)], 0)
    d_mlp_in = d_mlp_in + total
    gain_grad = jnp.sum(d_mlp_in * h_hat, 0, keepdims=True)
    small[n_exp : n_exp + 8, :] = gain_grad + jnp.zeros((8, width), f32)
    d_mid = v.grad_input
    d_out = jnp.where(place < seq_len, v.cot_f[...].reshape(rows, width), 0.0)
    d_mid[...] = d_out + norm_back(d_mlp_in * v.mlp_gain[...], h_hat, h_scale)

    v.d_all[net.tp] = d_mid[...].astype(bf16)
    tokens = GatherTp(net, lambda t, half: v.d_all.at[t, pl.ds(half * half_rows, half_rows)])
    tokens.start()
    for g in (3, 1, 2, 0):
        mix_sums.far(g)
    share = small.shape[0] // 2
    small_first = net.send(small, v.small_sib, C)
    v.d_key_t[...] = jnp.zeros_like(v.d_key_t)
    v.d_value_t[...] = jnp.zeros_like(v.d_value_t)

    def softmax_of(i, _):
        at = rows_of(i)
        q = v.query[at, :]
        first = low(q.shape)
        for head in (0, 1):
            s = dot_nt(jnp.where(first == (head == 0), q, jnp.zeros_like(q)), v.key[...]) * factor
            s = jnp.where(lanes(s.shape) < seq_len, s, masked_score)
            log = v.lse[at, head * HEAD_DIM : head * HEAD_DIM + 1]
            v.deep[rows_of(head * 8 + i), :] = jnp.exp(s - log).astype(bf16)
        return 0

    lax.fori_loop(0, 3, softmax_of, 0)
    tokens.relay()
    small_first.wait_recv()
    net.sent(small_first)
    mine = pl.ds(pl.multiple_of(net.c * share, 8), share)
    small[mine, :] = small[mine, :] + v.small_sib[mine, :]
    small_y = AxisSum(net, small.at[mine], v.small_got.at[0], ALONG_Y)
    lax.fori_loop(3, 6, softmax_of, 0)
    tokens.spread()
    for g in (3, 1, 2, 0):
        mix_sums.near(g)
    lax.fori_loop(6, 8, softmax_of, 0)
    tokens.finish()

    def back(i, _):
        at = rows_of(2 * i, 2)
        d_rows = jnp.concatenate([v.d_all[2 * i], v.d_all[2 * i + 1]], 0)
        d_o = dot_nt(d_rows, v.w_out[...]).astype(bf16)
        q = v.query[at, :]
        first = low(q.shape)
        d_q = []
        for head in (0, 1):
            own = first == (head == 0)
            d_o_head = jnp.where(own, d_o, jnp.zeros_like(d_o))
            q_head = jnp.where(own, q, jnp.zeros_like(q))
            p = v.deep[rows_of(head * 8 + 2 * i, 2), :]
            d_p = dot_nt(d_o_head, v.value[...])
            p32 = p.astype(f32)
            t = p32 * d_p
            d_s = (t - p32 * jnp.sum(t, -1, keepdims=True)).astype(bf16)
            d_q.append(dot(d_s, v.key[...]))
            v.d_key_t[...] += dot_tn(q_head, d_s)
            v.d_value_t[...] += dot_tn(d_o_head, p).reshape(v.d_value_t.shape)
        d_query = (jnp.where(first, d_q[0], d_q[1]) * factor).astype(bf16).astype(f32)
        d_gained = rotate_back(d_query, v.cosine[at, :], v.sine[at, :])
        hat, scale = pair_normed(v.q_raw[at, :])
        v.gain[8:9, :] += jnp.sum(d_gained * hat, 0, keepdims=True)
        v.d_qkv[at, 0:128] = pair_norm_back(d_gained * q_gain, hat, scale).astype(bf16)
        return 0

    v.gain[...] = jnp.zeros_like(v.gain)
    lax.fori_loop(0, 2, back, 0)
    mix_sums.turn(3)
    mix_sums.far(4)
    for sum_ in (gate, up, down):
        sum_.near()
    lax.fori_loop(2, 4, back, 0)
    mix_sums.turn(1)
    mix_sums.turn(2)
    mix_sums.near(4)
    small[mine, :] = small_y.finish()
    small_x = AxisSum(net, small.at[mine], v.small_got.at[1], ALONG_X)

    d_kv = jnp.concatenate(
        [
            v.d_key_t[:HEAD_DIM] + v.d_key_t[HEAD_DIM:],
            v.d_value_t[0] + v.d_value_t[1],
        ],
        0,
    ).T
    first = low(d_kv.shape)
    d_key = (jnp.where(first, d_kv, swap(d_kv)) * factor).astype(bf16).astype(f32)
    d_gained = rotate_back(d_key, v.cosine[...], v.sine[...])
    hat, scale = pair_normed(v.k_raw[...])
    v.gain[9:10, :] = jnp.sum(d_gained * hat, 0, keepdims=True)
    d_raw = pair_norm_back(d_gained * k_gain, hat, scale)
    v.d_qkv[:, 128:256] = jnp.where(first, d_raw, d_kv).astype(bf16)

    def spread(dy):
        def one(i, _):
            t = net.tp_at(dy, 1 - i)
            v.spare[rows_of(8 + t), :] = dot_nt(v.d_qkv[rows_of(t), :], v.w_qkv[...]).astype(bf16)
            return 0

        lax.fori_loop(0, 2, one, 0)

    sums = token_sums()
    spread(2)
    sums.across(2)
    grad_qkv = dot(v.h_t[...], v.d_qkv[...])
    sums.far()
    spread(1)
    sums.across(1)
    spread(-1)
    sums.across(-1)
    blocks, block = v.grad_terms.shape[0], v.grad_terms.shape[1]
    for e in range(blocks):
        v.grad_terms[e, :, 0:256] = grad_qkv[e * block : (e + 1) * block].astype(bf16)
    products = grad_qkv * v.w_qkv[...].astype(f32)
    norm_sum = lax.dot_general(
        jnp.ones((8, 256), f32), products, (((1,), (1,)), ((), ())), precision=highest, preferred_element_type=f32
    )[0:1]
    norm_sum = norm_sum / v.norm_gain[...]
    for i in range(8):
        v.gain[i : i + 1, :] = norm_sum[:, i * 128 : (i + 1) * 128]
    gain_c = AxisSum(net, v.gain.at[0:8], v.gain_got.at[0, :, 0:8], [C])
    grad_o = dot_tn(v.attn_o[...], v.d_all[...].reshape(group, width)).T
    for e in range(blocks):
        v.grad_terms[e, :, 256:384] = grad_o[e * block : (e + 1) * block].astype(bf16)
    grad_sums = ScatterEp(
        net,
        lambda e, start, count: v.grad_terms.at[e, pl.ds(start, count)],
        lambda i, start, count: v.grad_landed.at[i, pl.ds(start, count)],
        block,
    )
    for g in (3, 1, 2, 0):
        grad_sums.far(g)
    sums.near()
    spread(0)
    sums.across(0)
    v.gain[0:8, :] = gain_c.finish()
    gain_y = AxisSum(net, v.gain.at[0:8], v.gain_got.at[1, :, 0:8], ALONG_Y)
    for g in (3, 1, 2, 0):
        grad_sums.near(g)
    grad_sums.turn(3)
    grad_sums.far(4)
    grad_sums.turn(1)
    grad_sums.turn(2)
    grad_sums.near(4)
    grad_sums.turn(0)
    v.gain[0:8, :] = gain_y.finish()
    gain_x = AxisSum(net, v.gain, v.gain_got.at[2], ALONG_X)
    small[mine, :] = small_x.finish()
    small_z = AxisSum(net, small.at[mine], v.small_got.at[2], ALONG_Z)

    for h in (0, 1):
        part = grad_sums.last(4, h).astype(bf16)
        v.grad_all[net.ep, h * (block // 2) : (h + 1) * (block // 2), :] = part
    spread_grads = GatherEp(net, v.grad_all, block)
    spread_grads.start()

    x_hat, x_scale = normed(v.x[...].reshape(rows, width))
    total = jnp.concatenate([sums.last(0), sums.last(1)], 0)
    v.grad_input[...] = d_mid[...] + norm_back(total * v.norm_gain[...], x_hat, x_scale)

    mix_sums.turn(0)
    mix = jnp.concatenate([mix_sums.last(4, 0), mix_sums.last(4, 1)], 0)
    v.output[...] = jnp.where(place < seq_len, h_mid[...] + mix, 0.0)

    small[mine, :] = small_z.finish()
    small_last = net.send(small.at[mine], v.small_sib.at[mine], C)
    v.gain[...] = gain_x.finish()
    gain_z = AxisSum(net, v.gain, v.gain_got.at[3], ALONG_Z)
    spread_grads.first()
    for out, sum_ in ((v.grad_gate, gate), (v.grad_up, up), (v.grad_down, down)):
        for j in (0, 1):
            out[j] = sum_.last(j)
    v.gain_out[...] = gain_z.finish()
    spread_grads.second(0)
    spread_grads.far()
    spread_grads.second(-1)
    spread_grads.second(1)
    spread_grads.second(2)
    small_last.wait_recv()
    other = pl.ds(pl.multiple_of((1 - net.c) * share, 8), share)
    v.small_out[mine, :] = small[mine, :]
    v.small_out[other, :] = v.small_sib[other, :]
    prob_total = v.small_out[n_exp + 8 :, 0:n_exp]
    loss = jnp.dot(prob_total, counts, precision=highest, preferred_element_type=f32)
    v.loss[...] = loss * (n_exp / (8.0 * nvalid * nvalid)) + jnp.zeros((8, 128), f32)
    spread_grads.finish()
    for e in range(blocks):
        at = slice(e * block, (e + 1) * block)
        v.grad_query[at, :] = v.grad_all[e, :, 0:128].astype(f32)
        v.grad_keyval[at, :] = v.grad_all[e, :, 128:256].astype(f32)
    v.grad_out[...] = v.grad_all[:, :, 256:384].astype(f32).reshape(blocks * block, 128).T
    net.finish()


def local(
    layer_input,
    lengths,
    routes,
    norm_gain,
    w_query,
    w_keyval,
    query_gain,
    key_gain,
    w_out,
    mlp_gain,
    w_router,
    w_gate,
    w_up,
    w_down,
    cotangent,
):
    rows, width = layer_input.shape
    group = rows * 8
    n_exp = w_router.shape[1]
    top_k = routes.shape[1]
    units = w_down.shape[1]
    ff = units * 8
    slots = 3 * rows * top_k // (2 * n_exp)
    full = 16 * slots
    n = BATCH * slots
    block = width // 16
    n_small = n_exp + 16
    cosine, sine = rotary(group)
    inputs = {
        "layer_input": (layer_input, ANY),
        "lengths": (lengths, SM),
        "routes_in": (routes.T, ANY),
        "norm_gain": (norm_gain.reshape(1, -1), VM),
        "w_query": (w_query, ANY),
        "w_keyval": (w_keyval.reshape(width, -1), ANY),
        "query_gain": (query_gain.reshape(1, -1), VM),
        "key_gain": (key_gain.reshape(1, -1), VM),
        "w_out_in": (w_out, ANY),
        "mlp_gain": (mlp_gain.reshape(1, -1), VM),
        "w_router_t": (w_router.T, VM),
        "w_gate": (w_gate.transpose(0, 2, 1), ANY),
        "w_up": (w_up.transpose(0, 2, 1), ANY),
        "w_down": (w_down, ANY),
        "cotangent": (cotangent, ANY),
        "cosine_in": (jnp.asarray(cosine), ANY),
        "sine_in": (jnp.asarray(sine), ANY),
    }
    outputs = {
        "output": (rows, width),
        "grad_input": (rows, width),
        "loss": (8, 128),
        "grad_query": (width, 128),
        "grad_keyval": (width, 128),
        "gain_out": (16, 128),
        "grad_out": (128, width),
        "small_out": (n_small, width),
        "grad_gate": (2, units, width),
        "grad_up": (2, units, width),
        "grad_down": (2, units, width),
    }
    eight = pltpu.VMEM((8, rows, width), bf16)
    sixteen = pltpu.VMEM((16, rows, width), bf16)
    row_bf = pltpu.VMEM((group, 128), bf16)
    row_f = pltpu.VMEM((group, 128), f32)
    piece = pltpu.VMEM((4, 4, 8, rows), f32)
    by_expert = pltpu.VMEM((n_exp, rows), f32)
    scratch = {
        "w_qkv": pltpu.VMEM((width, 256), bf16),
        "w_out": pltpu.VMEM((128, width), bf16),
        "cosine": row_f,
        "sine": row_f,
        "routes": pltpu.VMEM((top_k, 16 * group), jnp.int32),
        "w": pltpu.VMEM((2, 3 * ff, width), bf16),
        "k_gain": pltpu.VMEM((1, 128), f32),
        "h_t": pltpu.VMEM((width, group), bf16),
        "spare": pltpu.VMEM((16 * rows, width), bf16),
        "d_all": eight,
        "query": row_bf,
        "key": row_bf,
        "value": row_bf,
        "k_raw": row_f,
        "attn_o": row_bf,
        "from_sib": pltpu.VMEM((4, rows, width), bf16),
        "from_far": pltpu.VMEM((2, rows // 2, width), bf16),
        "from_near": pltpu.VMEM((2, rows, width), bf16),
        "tok": sixteen,
        "cot": sixteen,
        "hits": by_expert,
        "probs": by_expert,
        "soft": by_expert,
        "d_gates": by_expert,
        "places": pltpu.VMEM((16, 2 * slots, rows), bf16),
        "counted": pltpu.VMEM((n_exp, 8, 128), f32),
        "gate_out": piece,
        "gate_mid": piece,
        "gate_got": piece,
        "back_out": piece,
        "back_mid": piece,
        "back_got": piece,
        "big": pltpu.VMEM((4 * full, width), bf16),
        "deep": pltpu.VMEM((max(3 * full, 2 * group), 2 * ff), bf16),
        "row_back": pltpu.VMEM((2, n, width), bf16),
        "landed": pltpu.VMEM((30, rows // 2, width), bf16),
        "w_sib": pltpu.VMEM((4, 3, 2, units, width), bf16),
        "w_far": pltpu.VMEM((3, 2, units, width), bf16),
        "w_near": pltpu.VMEM((2, 3, 2, units, width), bf16),
        "small": pltpu.VMEM((n_small, width), f32),
        "small_sib": pltpu.VMEM((n_small, width), f32),
        "small_got": pltpu.VMEM((3, 3, n_small // 2, width), f32),
        "d_qkv": pltpu.VMEM((group, 256), bf16),
        "grad_terms": pltpu.VMEM((16, block, 384), bf16),
        "grad_landed": pltpu.VMEM((30, block // 2, 384), bf16),
        "grad_all": pltpu.VMEM((16, block, 384), bf16),
        "gain": pltpu.VMEM((16, 128), f32),
        "gain_got": pltpu.VMEM((4, 3, 16, 128), f32),
        "send_sems": pltpu.SemaphoreType.DMA((512,)),
        "recv_sems": pltpu.SemaphoreType.DMA((512,)),
    }
    got = pl.pallas_call(
        lambda *refs: layer_kernel(*refs, inputs=tuple(inputs), outputs=tuple(outputs), scratch=tuple(scratch)),
        name="layer",
        out_shape=tuple(shaped(shape, f32) for shape in outputs.values()),
        in_specs=[spec for _, spec in inputs.values()],
        out_specs=(VM,) * len(outputs),
        scratch_shapes=list(scratch.values()),
        compiler_params=params(1, 63.9),
    )(*[array for array, _ in inputs.values()])
    got = dict(zip(outputs, got, strict=True))
    gains, small = got["gain_out"], got["small_out"]
    return (
        got["output"],
        got["grad_input"],
        got["loss"][0, 0],
        gains[:8].reshape(-1),
        got["grad_query"],
        got["grad_keyval"].reshape(w_keyval.shape),
        gains[8],
        gains[9, :HEAD_DIM],
        got["grad_out"],
        small[n_exp],
        small[:n_exp].T,
        got["grad_gate"].transpose(0, 2, 1),
        got["grad_up"].transpose(0, 2, 1),
        got["grad_down"],
    )


def solution(mesh):
    in_specs = (
        P(("ep", "tp"), None),
        P(),
        P(),
        P(),
        P(None, "tp"),
        P(None, "tp", None),
        P("tp"),
        P("tp"),
        P("tp", None),
        P(),
        P(),
        P("ep", None, "tp"),
        P("ep", None, "tp"),
        P("ep", "tp", None),
        P(("ep", "tp"), None),
    )
    out_specs = (
        P(("ep", "tp"), None),
        P(("ep", "tp"), None),
        P(),
        P(),
        P(None, "tp"),
        P(None, "tp", None),
        P("tp"),
        P("tp"),
        P("tp", None),
        P(),
        P(),
        P("ep", None, "tp"),
        P("ep", None, "tp"),
        P("ep", "tp", None),
    )
    return jax.shard_map(local, mesh=mesh, in_specs=in_specs, out_specs=out_specs, check_vma=False)
```

```python
import jax
import jax.numpy as jnp
import numpy as np
from jax import lax
from jax.experimental import pallas as pl
from jax.experimental.pallas import tpu as pltpu
from jax.sharding import PartitionSpec as P

MESH = pl.DeviceIdType.MESH
f32, bf16 = jnp.float32, jnp.bfloat16
HEAD_DIM = 64
epsilon = 1e-06
masked_score = -1e30
highest = lax.Precision.HIGHEST
MIB = 2**20

X, Y, Z, C = (1, 0, 0, 0), (0, 1, 0, 0), (0, 0, 1, 0), (0, 0, 0, 1)
XM, YM, ZM = (-1, 0, 0, 0), (0, -1, 0, 0), (0, 0, -1, 0)
X2, Z2 = (2, 0, 0, 0), (0, 0, 2, 0)
NEAR = (0, 1, -1, 2)


def times(d, k):
    return tuple(v * k for v in d)


class Bank:
    def __init__(self, first, size):
        self.first, self.size, self.used = first, size, 0

    def restart(self):
        self.used = 0
        return self

    def take(self):
        assert self.used < self.size
        self.used += 1
        return self.first + self.used - 1


class Net:
    def __init__(self, send_sems, recv_sems):
        self.ep, self.tp = lax.axis_index("ep"), lax.axis_index("tp")
        self.x, self.z = self.ep // 4, self.ep % 4
        self.y, self.c = self.tp // 2, self.tp % 2
        self.send_sems, self.recv_sems = send_sems, recv_sems
        self.free = list(range(SENDS))
        self.unsent = {}
        self.group = None

    def device(self, d):
        x, y = (self.x + d[0]) % 4, (self.y + d[1]) % 4
        z, c = (self.z + d[2]) % 4, (self.c + d[3]) % 2
        return (x * 4 + z, y * 2 + c)

    def ep_at(self, dx, dz):
        return ((self.x + dx) % 4) * 4 + (self.z + dz) % 4

    def tp_at(self, dy, dc):
        return ((self.y + dy) % 4) * 2 + (self.c + dc) % 2

    def barrier(self, dirs):
        sem = pltpu.get_barrier_semaphore()
        for d in dirs:
            pl.semaphore_signal(sem, inc=1, device_id=self.device(d), device_id_type=MESH)
        pl.semaphore_wait(sem, len(dirs))

    def send(self, src, dst, d, bank):
        i = self.free.pop(0)
        copy = pltpu.make_async_remote_copy(
            src_ref=src,
            dst_ref=dst,
            send_sem=self.send_sems.at[i],
            recv_sem=self.recv_sems.at[bank.take()],
            device_id=self.device(d),
            device_id_type=MESH,
        )
        copy.start()
        self.unsent.setdefault(self.group, []).append((copy, i))
        return copy

    def keep(self, src, dst):
        i = self.free.pop(0)
        copy = pltpu.make_async_copy(src, dst, self.send_sems.at[i])
        copy.start()
        return copy, i

    def kept(self, pair):
        pair[0].wait()
        self.free.append(pair[1])

    def sent(self, copy):
        for group, pairs in self.unsent.items():
            for _, i in [pair for pair in pairs if pair[0] is copy]:
                copy.wait_send()
                self.free.append(i)
            self.unsent[group] = [pair for pair in pairs if pair[0] is not copy]

    def finish(self, *groups):
        for group in groups or tuple(self.unsent):
            for copy, i in self.unsent.pop(group, ()):
                copy.wait_send()
                self.free.append(i)


class GatherTp:
    def __init__(self, net, bank, ref, own=None):
        self.net, self.bank, self.ref = net, bank.restart(), ref
        self.own = own or (lambda half: ref(net.tp, half))
        self.copies = {}
        self.done = set()

    def wait(self, *key):
        if key not in self.done:
            self.done.add(key)
            self.copies[key].wait_recv()

    def along(self, dy, half, sign):
        src = self.own(half) if dy == 0 else self.ref(self.net.tp_at(dy, 0), half)
        to = (dy - sign + 1) % 4 - 1
        self.copies[("y", to, half)] = self.net.send(
            src, self.ref(self.net.tp_at(dy, 0), half), times(Y, sign), self.bank
        )

    def across(self, dy):
        for half in (0, 1):
            src = self.own(half) if dy == 0 else self.ref(self.net.tp_at(dy, 0), half)
            self.copies[("c", dy, half)] = self.net.send(
                src, self.ref(self.net.tp_at(dy, 0), half), C, self.bank
            )

    def start(self):
        self.along(0, 0, 1)
        self.along(0, 1, -1)
        self.along(0, 1, 1)
        self.along(0, 0, -1)
        self.across(0)

    def relay(self):
        self.wait("y", -1, 0)
        self.along(-1, 0, 1)
        self.wait("y", 1, 1)
        self.along(1, 1, -1)

    def share(self):
        for dy, half in ((-1, 1), (1, 0)):
            self.wait("y", dy, half)
            self.across(dy)

    def spread(self):
        for half in (0, 1):
            self.wait("y", 2, half)
        self.across(2)

    def need(self, dy, dc):
        if dc:
            for half in (0, 1):
                self.wait("c", dy, half)
        elif dy:
            for half in (0, 1):
                self.wait("y", dy, half)

    def finish(self):
        for key in list(self.copies):
            self.wait(*key)


class ScatterTp:
    def __init__(self, net, bank, ref, sib, far, near):
        self.bank = bank.restart()
        self.net, self.ref, self.sib, self.far_at, self.near_at = net, ref, sib, far, near
        self.copies = {}

    def across(self, dy):
        i = NEAR.index(dy)
        for half in (0, 1):
            self.copies[("c", dy, half)] = self.net.send(
                self.ref(self.net.tp_at(dy, 1), half), self.sib(i, half), C, self.bank
            )

    def join(self, dy, half):
        self.copies[("c", dy, half)].wait_recv()
        return self.ref(self.net.tp_at(dy, 0), half)[...] + self.sib(NEAR.index(dy), half)[...]

    def far(self):
        for half, sign in ((0, 1), (1, -1)):
            ref = self.ref(self.net.tp_at(2, 0), half)
            ref[...] = self.join(2, half)
            self.copies[("f", half)] = self.net.send(ref, self.far_at(half), times(Y, sign), self.bank)

    def towards(self, part, half):
        sign = (1, -1)[part]
        ref = self.ref(self.net.tp_at(sign, 0), half)
        total = self.join(sign, half)
        if half == part:
            self.copies[("f", part)].wait_recv()
            total = total + self.far_at(part)[...]
        ref[...] = total
        self.copies[("n", part, half)] = self.net.send(
            ref, self.near_at(part, half), times(Y, sign), self.bank
        )

    def near_first(self):
        for part in (0, 1):
            self.towards(part, 1 - part)

    def near_second(self):
        for part in (0, 1):
            self.towards(part, part)

    def last(self, half):
        total = self.join(0, half).astype(f32)
        for part in (0, 1):
            self.copies[("n", part, half)].wait_recv()
            total = total + self.near_at(part, half)[...].astype(f32)
        return total


class GatherEp:
    def __init__(self, net, bank, buf, rows):
        self.bank = bank.restart()
        self.net, self.buf, self.rows = net, buf, rows
        self.copies = {}
        self.done = set()

    def ref(self, h, j, k, part):
        half, quarter = self.rows // 2, self.rows // 4
        e = self.net.ep_at(j, k) if h == 0 else self.net.ep_at(k, j)
        if part is None:
            return self.buf.at[e, pl.ds(h * half, half)]
        return self.buf.at[e, pl.ds(h * half + part * quarter, quarter)]

    def send(self, h, j, k, part, along, sign):
        d = (X, Z)[along if h == 0 else 1 - along]
        r = self.ref(h, j, k, part)
        to = (j - sign, k) if along == 0 else (j, k - sign)
        to = tuple((v + 1) % 4 - 1 for v in to)
        self.copies[(h, *to, part)] = self.net.send(r, r, times(d, sign), self.bank)

    def wait(self, *key):
        if key not in self.done:
            self.done.add(key)
            self.copies[key].wait_recv()

    def need(self, h, j, k):
        if (j, k) != (0, 0):
            for part in (None,) if (h, j, k, None) in self.copies else (0, 1):
                self.wait(h, j, k, part)

    def block(self, dx, dz):
        self.need(0, dx, dz)
        self.need(1, dz, dx)

    def start(self):
        for along in (0, 1):
            for h in (0, 1):
                for sign in (1, -1):
                    self.send(h, 0, 0, None, along, sign)

    def first(self):
        for part, sign in ((0, 1), (1, -1)):
            for h in (0, 1):
                self.wait(h, -sign, 0, None)
                self.send(h, -sign, 0, part, 0, sign)
        for sign in (1, -1):
            for h in (0, 1):
                for turn in (1, -1):
                    self.send(h, -sign, 0, None, 1, turn)

    def far(self):
        for h in (0, 1):
            self.need(h, 2, 0)
            for turn in (1, -1):
                self.send(h, 2, 0, None, 1, turn)

    def second(self, j):
        for part, sign in ((0, 1), (1, -1)):
            for h in (0, 1):
                self.wait(h, j, -sign, None)
                self.send(h, j, -sign, part, 1, sign)

    def finish(self):
        for key in list(self.copies):
            self.wait(*key)


class ScatterEp:
    def __init__(self, net, bank, term, landed, rows):
        self.bank = bank.restart()
        self.net, self.term, self.landed, self.rows = net, term, landed, rows
        self.copies = {}

    def ref(self, h, g, j, part):
        j, k = (j, NEAR[g]) if g < 4 else (0, j)
        half, quarter = self.rows // 2, self.rows // 4
        e = self.net.ep_at(k, j) if h == 0 else self.net.ep_at(j, k)
        if part is None:
            return self.term(e, h * half, half)
        return self.term(e, h * half + part * quarter, quarter)

    def slot(self, g, h, which, part=None):
        half, quarter = self.rows // 2, self.rows // 4
        i = (g * 2 + h) * 3 + which
        return self.landed(i, 0, half) if part is None else self.landed(i, part * quarter, quarter)

    def dir(self, h, g, sign):
        return times((Z, X)[(g == 4) if h == 0 else (g != 4)], sign)

    def far(self, g):
        for h in (0, 1):
            for part, sign in ((0, 1), (1, -1)):
                self.copies[(g, h, 2, part)] = self.net.send(
                    self.ref(h, g, 2, part), self.slot(g, h, 2, part), self.dir(h, g, sign), self.bank
                )

    def near(self, g):
        for h in (0, 1):
            for part, sign in ((0, 1), (1, -1)):
                self.copies[(g, h, 2, part)].wait_recv()
                r = self.ref(h, g, sign, part)
                r[...] = r[...] + self.slot(g, h, 2, part)[...]
                self.copies[(g, h, part)] = self.net.send(
                    self.ref(h, g, sign, None), self.slot(g, h, part), self.dir(h, g, sign), self.bank
                )

    def last(self, g, h):
        for part in (0, 1):
            self.copies[(g, h, part)].wait_recv()
        total = self.ref(h, g, 0, None)[...].astype(f32)
        for part in (0, 1):
            total = total + self.slot(g, h, part)[...].astype(f32)
        return total

    def turn(self, g):
        for h in (0, 1):
            self.ref(h, g, 0, None)[...] = self.last(g, h).astype(bf16)


def lanes(shape):
    return lax.broadcasted_iota(jnp.int32, shape, len(shape) - 1)


def low(shape):
    return lanes(shape) < HEAD_DIM


def normed(v):
    factor = lax.rsqrt(jnp.mean(v * v, -1, keepdims=True) + epsilon)
    return v * factor, factor


def norm_back(grad, hat, factor):
    return factor * (grad - hat * jnp.mean(grad * hat, -1, keepdims=True))


def pair_sums(v):
    first = low(v.shape)
    a = jnp.sum(jnp.where(first, v, 0.0), -1, keepdims=True)
    b = jnp.sum(jnp.where(first, 0.0, v), -1, keepdims=True)
    return jnp.where(first, a, b)


def pair_normed(v):
    factor = lax.rsqrt(pair_sums(v * v) / HEAD_DIM + epsilon)
    return v * factor, factor


def pair_norm_back(grad, hat, factor):
    return factor * (grad - hat * (pair_sums(grad * hat) / HEAD_DIM))


def partner(v):
    half = HEAD_DIM // 2
    return jnp.where(
        lanes(v.shape) % HEAD_DIM < half, pltpu.roll(v, 128 - half, 1), pltpu.roll(v, half, 1)
    )


def rotate(v, cosine, sine):
    return v * cosine + partner(v) * sine


def rotate_back(v, cosine, sine):
    return v * cosine - partner(v) * sine


def swap(v):
    return pltpu.roll(v, HEAD_DIM, v.ndim - 1)


def dot(a, b):
    return jnp.dot(a, b, preferred_element_type=f32)


def dot_nt(a, b):
    return lax.dot_general(a, b, (((1,), (1,)), ((), ())), preferred_element_type=f32)


def dot_tn(a, b):
    return lax.dot_general(a, b, (((0,), (0,)), ((), ())), preferred_element_type=f32)


def rotary(length):
    half = HEAD_DIM // 2
    frequency = 10000.0 ** (-(np.arange(half, dtype=np.float64) * 2.0 / HEAD_DIM))
    angles = np.arange(length, dtype=np.float64)[:, None] * frequency[None, :]
    cosine, sine = np.cos(angles), np.sin(angles)
    cosine = np.concatenate([cosine] * 4, -1).astype(np.float32)
    sine = np.concatenate([-sine, sine] * 2, -1).astype(np.float32)
    return cosine, sine


VM = pl.BlockSpec(memory_space=pltpu.VMEM)
SM = pl.BlockSpec(memory_space=pltpu.SMEM)
ANY = pl.BlockSpec(memory_space=pl.ANY)


def shaped(shape, dtype):
    return jax.ShapeDtypeStruct(shape, dtype)


def params(collective_id, vmem):
    return pltpu.CompilerParams(
        collective_id=collective_id, has_side_effects=True, vmem_limit_bytes=int(vmem * MIB)
    )


def key_value(qkv, q_gain, k_gain, cosine, sine):
    q_hat, _ = pair_normed(qkv[:, :128])
    kv = qkv[:, 128:]
    first = low(kv.shape)
    other = swap(kv)
    k_raw = jnp.where(first, kv, other)
    k_hat, _ = pair_normed(k_raw)
    query = (rotate(q_hat * q_gain, cosine, sine).astype(bf16).astype(f32) * HEAD_DIM**-0.5).astype(bf16)
    key = rotate(k_hat * k_gain, cosine, sine).astype(bf16)
    value = jnp.where(first, other, kv).astype(bf16)
    value = jnp.concatenate([value, jnp.ones_like(value)], -1)
    return query, key, value, qkv[:, :128], k_raw


class Exchange:
    def __init__(self, net, bank, out, half_way, got):
        self.bank = bank.restart()
        self.net, self.out, self.half_way, self.got = net, out, half_way, got

    def start(self):
        net = self.net
        self.first = [
            net.send(self.out.at[(net.x + k) % 4], self.half_way.at[net.x], times(X, k), self.bank)
            for k in (1, -1, 2)
        ]
        self.half_way[net.x] = self.out[net.x]

    def turn(self):
        net = self.net
        for copy in self.first:
            copy.wait_recv()
        self.second = [
            net.send(self.half_way.at[:, (net.z + k) % 4], self.got.at[:, net.z], times(Z, k), self.bank)
            for k in (1, -1, 2)
        ]
        self.got[:, net.z] = self.half_way[:, net.z]

    def finish(self):
        for copy in self.second:
            copy.wait_recv()


class AxisSum:
    def __init__(self, net, bank, term, slots, steps):
        self.net, self.term, self.slots = net, term, slots
        self.copies = [net.send(term, slots.at[i], d, bank) for i, d in enumerate(steps)]

    def finish(self):
        total = self.term[...]
        for i, copy in enumerate(self.copies):
            copy.wait_recv()
            total = total + self.slots[i]
            self.net.sent(copy)
        return total


ALONG_X, ALONG_Y, ALONG_Z = ([times(d, k) for k in (1, -1, 2)] for d in (X, Y, Z))
Y2 = times(Y, 2)

SENDS = 232
BANKS = {"ep0": 40, "ep1": 40, "ep2": 40, "tp0": 14, "tp1": 14}
BANKS |= {name + str(a): 14 for name in ("gather", "scatter") for a in range(3)}
BANKS |= {"gates": 6, "back": 6, "small": 11, "gains": 10}

ORDER = (
    (0, 0), (-1, 0), (1, 0), (0, -1),
    (0, 1), (2, 0), (0, 2), (-1, -1),
    (-1, 1), (1, -1), (1, 1), (2, -1),
    (2, 1), (-1, 2), (1, 2), (2, 2),
)
BATCH = 8


def layer_kernel(*refs, inputs, outputs, scratch):
    names = inputs + outputs + scratch
    r = dict(zip(names, refs, strict=True))

    class R:
        pass

    v = R()
    for name, ref in r.items():
        setattr(v, name, ref)
    v.totals, v.q_raw, v.d_key_t = v.grad_query, v.grad_keyval, v.grad_out
    v.d_value_t, v.x, v.cot_f = v.grad_gate, v.grad_up, v.grad_down
    net = Net(v.send_sems, v.recv_sems)
    banks, first = {}, 0
    for name, size in BANKS.items():
        banks[name] = Bank(first, size)
        first += size
    rows, width = v.output.shape
    half_rows = rows // 2
    group = rows * 8
    units = v.w_down.shape[1]
    ff = units * 8
    n_exp = v.w_router_t.shape[0]
    slots = v.places.shape[1] // 2
    full = 16 * slots
    seq_len = v.lengths[net.ep]
    factor = HEAD_DIM**-0.5

    def weight(a, j, t):
        return v.w.at[j, pl.ds(pl.multiple_of(a * ff + t * units, units), units)]

    def rows_of(i, count=1):
        return pl.ds(pl.multiple_of(i * rows, rows), rows * count)

    def half_of(t, half):
        return pl.ds(pl.multiple_of(t * rows + half * half_rows, half_rows), half_rows)

    x_load = [net.keep(v.layer_input.at[pl.ds(i * half_rows, half_rows)], v.x.at[i]) for i in (0, 1)]
    early = [
        net.keep(v.w_query, v.w_qkv.at[:, pl.ds(0, 128)]),
        net.keep(v.w_keyval, v.w_qkv.at[:, pl.ds(128, 128)]),
        net.keep(v.cosine_in, v.cosine),
        net.keep(v.sine_in, v.sine),
    ]
    cot_load = [net.keep(v.cotangent.at[pl.ds(i * half_rows, half_rows)], v.cot_f.at[i]) for i in (0, 1)]
    weight_loads = [
        net.keep(source.at[j], weight(a, j, net.tp))
        for a, source in enumerate((v.w_gate, v.w_up, v.w_down))
        for j in (0, 1)
    ]
    late = [net.keep(v.routes_in, v.routes), net.keep(v.w_out_in, v.w_out)]
    net.barrier([X, XM, X2, Y, YM, Y2, Z, ZM, Z2, C])

    for copy in x_load:
        net.kept(copy)
    x_hat, _ = normed(v.x[...].reshape(rows, width))
    v.spare[rows_of(net.tp), :] = (x_hat * v.norm_gain[...]).astype(bf16)
    tokens = GatherTp(net, banks["tp0"], lambda t, half: v.spare.at[half_of(t, half)])
    tokens.start()
    place = net.tp * rows + lax.broadcasted_iota(jnp.int32, (rows, 1), 0)
    for copy in cot_load:
        net.kept(copy)
    v.cot[net.ep] = jnp.where(place < seq_len, v.cot_f[...].reshape(rows, width), 0.0).astype(bf16)
    cots = GatherEp(net, banks["ep0"], v.cot, rows)
    net.group = "cot"
    cots.start()
    net.group = None

    for copy in early + late:
        net.kept(copy)
    v.k_gain[:, 0:HEAD_DIM] = v.key_gain[...]
    k_gain = v.k_gain[...]
    k_gain = jnp.where(low(k_gain.shape), k_gain, swap(k_gain))
    q_gain = v.query_gain[...]

    def project(dy):
        at = rows_of(net.tp_at(dy, 0) - net.c, 2)
        h = v.spare[at, :]
        parts = key_value(dot(h, v.w_qkv[...]), q_gain, k_gain, v.cosine[at, :], v.sine[at, :])
        for ref, part in zip((v.query, v.key, v.value, v.q_raw, v.k_raw), parts, strict=True):
            ref[at, :] = part
        v.h_t[:, at] = h.T

    def routing():
        for s in range(16):
            segment = v.routes[:, rows_of(s * 8 + net.tp)]
            for j in (0, 1):
                same = (segment == net.ep * 2 + j).astype(f32)
                v.hits[2 * s + j : 2 * s + j + 1, :] = jnp.max(same, 0, keepdims=True)
        before = lax.broadcasted_iota(jnp.int32, (rows, rows), 0) < lanes((rows, rows))
        rank = dot(v.hits[...].astype(bf16), before.astype(bf16))
        rank = jnp.where(v.hits[...] > 0.5, rank, -1.0)
        slot = lax.broadcasted_iota(jnp.int32, (slots, rows), 0).astype(f32)
        for s in range(16):
            for j in (0, 1):
                mine = rank[2 * s + j : 2 * s + j + 1]
                v.places[s, j * slots : (j + 1) * slots, :] = (slot == mine).astype(bf16)

    def count():
        v.counted[...] = jnp.zeros_like(v.counted)

        def one(g, _):
            segment = v.routes[:, pl.ds(pl.multiple_of(g * group, group), group)]
            segment = jnp.where(lanes(segment.shape) < v.lengths[g], segment, -1)
            for e in range(n_exp):
                hit = (segment == e).astype(f32)
                total = hit[:, 0:128]
                for i in range(1, group // 128):
                    total = total + hit[:, i * 128 : (i + 1) * 128]
                v.counted[e] += total
            return 0

        lax.fori_loop(0, 16, one, 0)

    routing()
    count()
    tokens.need(0, 1)
    project(0)
    tokens.relay()
    cots_step = lambda step, *a: (setattr(net, "group", "cot"), step(*a), setattr(net, "group", None))
    cots_step(cots.first)
    tokens.share()
    cots_step(cots.second, 0)
    tokens.need(-1, 1)
    project(-1)
    tokens.need(1, 1)
    project(1)
    cots_step(cots.far)
    tokens.spread()
    for copy in weight_loads:
        net.kept(copy)
    w_step = lambda step, *a: (setattr(net, "group", "w"), step(*a), setattr(net, "group", None))
    gate, up, down = (
        GatherTp(net, banks[f"gather{a}"], lambda t, half, a=a: weight(a, half, t)) for a in range(3)
    )
    w_step(gate.start)
    w_step(up.start)
    tokens.need(2, 1)
    project(2)
    tokens.finish()

    bias = jnp.where(lanes((1, group)) < seq_len, 0.0, masked_score)

    def weights_of(q, head):
        q_head = jnp.where(low(q.shape) == (head == 0), q, jnp.zeros_like(q))
        return jnp.exp(dot_nt(q_head, v.key[...]) + bias).astype(bf16)

    def attend(dy):
        def one(i, _):
            t = net.tp_at(dy, 1 - i)
            at = rows_of(t)
            q = v.query[at, :]
            first = low(q.shape)
            mixed = [dot(weights_of(q, head), v.value[...]) for head in (0, 1)]
            total = jnp.where(first, mixed[0][:, 128:], mixed[1][:, 128:])
            o = (jnp.where(first, mixed[0][:, :128], mixed[1][:, :128]) / total).astype(bf16)
            v.attn_o[at, :] = o
            v.totals[at, :] = total
            v.spare[rows_of(8 + t), :] = dot(o, v.w_out[...]).astype(bf16)
            return 0

        lax.fori_loop(0, 2, one, 0)

    def token_sums():
        return ScatterTp(
            net,
            banks["tp1"],
            lambda t, half: v.spare.at[half_of(8 + t, half)],
            lambda i, half: v.from_sib.at[i, pl.ds(half * half_rows, half_rows)],
            lambda half: v.from_far.at[half],
            lambda part, half: v.from_near.at[part, pl.ds(half * half_rows, half_rows)],
        )

    sums = token_sums()
    attend(2)
    sums.across(2)
    attend(1)
    sums.across(1)
    sums.far()
    attend(-1)
    sums.across(-1)
    cots_step(cots.second, -1)
    sums.near_first()
    attend(0)
    sums.across(0)
    w_step(gate.relay)
    sums.near_second()
    cots_step(cots.second, 1)
    cots_step(cots.second, 2)
    h_mid = v.output
    for half in (0, 1):
        at = pl.ds(half * half_rows, half_rows)
        h_mid[at, :] = v.x[half] + sums.last(half)
    net.finish(None)

    h_hat, h_scale = normed(h_mid[...])
    mlp_in = h_hat * v.mlp_gain[...]
    v.tok[net.ep] = mlp_in.astype(bf16)
    tokens = GatherEp(net, banks["ep1"], v.tok, rows)
    tokens.start()
    w_step(down.start)
    w_step(gate.share)
    w_step(up.relay)

    w_router_t = v.w_router_t
    logits = lax.dot_general(
        w_router_t[...], mlp_in, (((1,), (1,)), ((), ())), precision=highest, preferred_element_type=f32
    )
    token_at = net.tp * rows + lanes((1, rows))
    valid = jnp.where(token_at < seq_len, 1.0, 0.0)
    expert = lax.broadcasted_iota(jnp.int32, (n_exp, rows), 0)
    mine = v.routes[:, rows_of(net.ep * 8 + net.tp)]
    chosen = expert == mine[0:1]
    for k in range(1, mine.shape[0]):
        chosen = jnp.logical_or(chosen, expert == mine[k : k + 1])
    top = jnp.max(logits, 0, keepdims=True)
    weights = jnp.exp(logits - top)
    probs = weights / jnp.sum(weights, 0, keepdims=True)
    top = jnp.max(jnp.where(chosen, logits, masked_score), 0, keepdims=True)
    weights = jnp.where(chosen, jnp.exp(jnp.where(chosen, logits - top, 0.0)), 0.0)
    soft = weights / jnp.sum(weights, 0, keepdims=True)
    v.probs[...] = probs
    v.soft[...] = soft
    gates = soft * valid
    for e in range(16):
        v.gate_out[e // 4, e % 4, 0:2, :] = gates[2 * e : 2 * e + 2]
    to_owners = Exchange(net, banks["gates"], v.gate_out, v.gate_mid, v.gate_got)
    to_owners.start()

    cots.finish()
    net.finish("cot")
    tokens.first()
    w_step(up.share)
    w_step(gate.spread)
    to_owners.turn()
    tokens.second(0)
    w_step(down.relay)
    w_step(up.spread)
    tokens.far()
    w_step(down.share)
    to_owners.finish()
    tokens.second(-1)
    tokens.second(1)
    w_step(down.spread)
    tokens.second(2)
    for gather in (gate, up, down):
        gather.finish()
    net.finish("w")

    n = BATCH * slots

    def picked(j, at, count):
        return pl.ds(pl.multiple_of(j * full + at, slots), count)

    def d_picked(j, at, count):
        return pl.ds(pl.multiple_of((2 + j) * full + at, slots), count)

    def batch(b):
        members = []
        for i, (dx, dz) in enumerate(ORDER[b * BATCH : (b + 1) * BATCH]):
            tokens.block(dx, dz)
            s = net.ep_at(dx, dz)
            members.append((s, (net.x + dx) % 4, (net.z + dz) % 4))
            here = v.places[s]
            taken = dot(here, v.tok[s]).astype(bf16)
            taken_d = dot(here, v.cot[s]).astype(bf16)
            for j in (0, 1):
                v.big[picked(j, b * n + i * slots, slots), :] = taken[j * slots : (j + 1) * slots]
                v.big[d_picked(j, b * n + i * slots, slots), :] = taken_d[j * slots : (j + 1) * slots]

        def one(j, _):
            at, at_d = picked(j, b * n, n), d_picked(j, b * n, n)
            gate_col = []
            for s, sx, sz in members:
                here = v.places[s, pl.ds(pl.multiple_of(j * slots, slots), slots), :].astype(f32)
                gate_col.append(jnp.sum(here * v.gate_got[sx, sz, pl.ds(j, 1), :], -1, keepdims=True))
            gate_col = jnp.concatenate(gate_col, 0)
            pre = dot_nt(v.big[at, :], v.w[j, 0 : 2 * ff])
            d_hidden = dot_nt(v.big[at_d, :], v.w[j, 2 * ff :])
            g, u = pre[:, :ff], pre[:, ff:]
            sigma = 0.5 * jnp.tanh(0.5 * g) + 0.5
            act = g * sigma
            hid = act * u
            d_gate = jnp.sum(d_hidden * hid, -1, keepdims=True)
            hid = (gate_col * hid).astype(bf16)
            v.deep[pl.ds(2 * full + b * n, n), pl.ds(pl.multiple_of(j * ff, ff), ff)] = hid
            d_hidden = d_hidden * gate_col
            v.deep[at, 0:ff] = (d_hidden * u * (sigma * (1.0 + g - act))).astype(bf16)
            v.deep[at, ff:] = (d_hidden * act).astype(bf16)
            v.spare[picked(j, b * n, n), :] = dot(hid, v.w[j, 2 * ff :]).astype(bf16)
            v.row_back[j] = dot(v.deep[at, :], v.w[j, 0 : 2 * ff]).astype(bf16)
            for i, (s, sx, sz) in enumerate(members):
                here = v.places[s, pl.ds(pl.multiple_of(j * slots, slots), slots), :].astype(f32)
                d = jnp.sum(here * d_gate[i * slots : (i + 1) * slots], 0, keepdims=True)
                v.back_out[sx, sz, pl.ds(j, 1), :] = d
            return 0

        lax.fori_loop(0, 2, one, 0)
        for i, (s, _, _) in enumerate(members):
            at = pl.ds(i * slots, slots)
            both = jnp.concatenate([v.row_back[0, at, :], v.row_back[1, at, :]], 0)
            v.cot[s] = dot_tn(v.places[s], both).astype(bf16)

    row_sums = ScatterEp(
        net,
        banks["ep0"],
        lambda e, start, count: v.cot.at[e, pl.ds(start, count)],
        lambda i, start, count: v.landed.at[i, pl.ds(start, count)],
        rows,
    )
    batch(0)
    tokens.finish()
    net.finish(None)
    row_sums.far(0)
    batch(1)

    to_tokens = Exchange(net, banks["back"], v.back_out, v.back_mid, v.back_got)
    to_tokens.start()
    mix_sums = ScatterEp(
        net,
        banks["ep1"],
        lambda e, start, count: v.big.at[pl.ds(pl.multiple_of(e * rows + start, 16), count)],
        lambda i, start, count: v.tok.at[i // 2, pl.ds(i % 2 * half_rows + start, count)],
        rows,
    )
    for g in (3, 1, 2):
        row_sums.far(g)
    row_sums.near(0)

    def grads(j, _):
        v.w[j, 0 : 2 * ff] = dot_tn(
            v.deep[picked(j, 0, full), :], v.big[picked(j, 0, full), :]
        ).astype(bf16)
        hidden = v.deep[2 * full : 3 * full, pl.ds(pl.multiple_of(j * ff, ff), ff)]
        v.w[j, 2 * ff :] = dot_tn(hidden, v.big[d_picked(j, 0, full), :]).astype(bf16)
        return 0

    lax.fori_loop(0, 2, grads, 0)
    to_tokens.turn()
    for g in (3, 1, 2):
        row_sums.near(g)
    gate, up, down = (
        ScatterTp(
            net,
            banks[f"scatter{a}"],
            lambda t, half, a=a: weight(a, half, t),
            lambda i, half, a=a: v.w_sib.at[i, a, half],
            lambda half, a=a: v.w_far.at[a, half],
            lambda part, half, a=a: v.w_near.at[part, a, half],
        )
        for a in range(3)
    )
    for dy in (2, 1, -1, 0):
        for sum_ in (gate, up, down):
            w_step(sum_.across, dy)
    for s in range(16):
        i = net.ep_at(*ORDER[s])
        both = jnp.concatenate([v.spare[picked(j, s * slots, slots), :] for j in (0, 1)], 0)
        v.big[rows_of(i), :] = dot_tn(v.places[i], both).astype(bf16)
    row_sums.turn(3)
    row_sums.far(4)
    for sum_ in (gate, up, down):
        w_step(sum_.far)
    to_tokens.finish()

    for e in range(16):
        v.d_gates[2 * e : 2 * e + 2, :] = v.back_got[e // 4, e % 4, 0:2, :]
    probs, soft = v.probs[...], v.soft[...]
    d_gates = v.d_gates[...] * valid
    d_chosen = soft * (d_gates - jnp.sum(soft * d_gates, 0, keepdims=True))
    nvalid = jnp.int32(0)
    for e in range(16):
        nvalid = nvalid + v.lengths[e]
    nvalid = nvalid.astype(f32)
    counts = jnp.sum(jnp.sum(v.counted[...], 1), -1, keepdims=True)
    balance = n_exp * counts / (8 * nvalid * nvalid)
    d_logits = d_chosen + valid * probs * (balance - jnp.sum(probs * balance, 0, keepdims=True))
    d_mlp_in = lax.dot_general(
        d_logits, w_router_t[...], (((0,), (0,)), ((), ())), precision=highest, preferred_element_type=f32
    )
    h_hat, h_scale = normed(h_mid[...])
    mlp_in = h_hat * v.mlp_gain[...]
    small = v.small
    small[0:n_exp, :] = jnp.dot(d_logits, mlp_in, precision=highest, preferred_element_type=f32)
    small[n_exp + 8 :, :] = jnp.zeros((8, width), f32)
    small[n_exp + 8 :, 0:n_exp] = lax.dot_general(
        valid + jnp.zeros((8, rows), f32), probs, (((1,), (1,)), ((), ())), precision=highest, preferred_element_type=f32
    )
    row_sums.turn(1)
    row_sums.turn(2)
    row_sums.near(4)
    row_sums.turn(0)
    d_out = jnp.where(place < seq_len, v.cot_f[...].reshape(rows, width), 0.0)
    total = jnp.concatenate([row_sums.last(4, 0), row_sums.last(4, 1)], 0)
    d_mlp_in = d_mlp_in + total
    gain_grad = jnp.sum(d_mlp_in * h_hat, 0, keepdims=True)
    small[n_exp : n_exp + 8, :] = gain_grad + jnp.zeros((8, width), f32)
    d_mid = v.grad_input
    d_mid[...] = d_out + norm_back(d_mlp_in * v.mlp_gain[...], h_hat, h_scale)

    net.finish(None)

    v.d_all[net.tp] = d_mid[...].astype(bf16)
    tokens = GatherTp(net, banks["tp0"], lambda t, half: v.d_all.at[t, pl.ds(half * half_rows, half_rows)])
    tokens.start()
    net.group = "mix"
    for g in (3, 1, 2, 0):
        mix_sums.far(g)
    net.group = None
    share = small.shape[0] // 2
    small_first = net.send(small, v.small_sib, C, banks["small"])
    v.d_key_t[...] = jnp.zeros_like(v.d_key_t)
    v.d_value_t[...] = jnp.zeros_like(v.d_value_t)

    def softmax_of(i, _):
        q = v.query[rows_of(i), :]
        for head in (0, 1):
            v.deep[rows_of(head * 8 + i), :] = weights_of(q, head)
        return 0

    lax.fori_loop(0, 8, softmax_of, 0)
    tokens.relay()
    small_first.wait_recv()
    net.sent(small_first)
    mine = pl.ds(pl.multiple_of(net.c * share, 8), share)
    small[mine, :] = small[mine, :] + v.small_sib[mine, :]
    net.group = "mix"
    for g in (3, 1, 2, 0):
        mix_sums.near(g)
    net.group = None
    tokens.share()
    tokens.spread()
    for sum_ in (gate, up, down):
        w_step(sum_.near_first)
        w_step(sum_.near_second)
    small_y = AxisSum(net, banks["small"], small.at[mine], v.small_got.at[0], ALONG_Y)
    tokens.finish()

    def back(i, _):
        at = rows_of(2 * i, 2)
        d_rows = jnp.concatenate([v.d_all[2 * i], v.d_all[2 * i + 1]], 0)
        d_o = dot_nt(d_rows, v.w_out[...]).astype(bf16).astype(f32) / v.totals[at, :]
        shift = pair_sums(d_o * v.attn_o[at, :].astype(f32))
        d_o = d_o.astype(bf16)
        q = v.query[at, :]
        first = low(q.shape)
        d_q = []
        for head in (0, 1):
            own = first == (head == 0)
            d_o_head = jnp.where(own, d_o, jnp.zeros_like(d_o))
            q_head = jnp.where(own, q, jnp.zeros_like(q))
            p = v.deep[rows_of(head * 8 + 2 * i, 2), :]
            d_p = dot_nt(d_o_head, v.value[:, 0:128]) - shift[:, head * HEAD_DIM : head * HEAD_DIM + 1]
            d_s = (p.astype(f32) * d_p).astype(bf16)
            d_q.append(dot(d_s, v.key[...]))
            v.d_key_t[...] += dot_tn(q_head, d_s)
            v.d_value_t[...] += dot_tn(d_o_head, p).reshape(v.d_value_t.shape)
        d_query = (jnp.where(first, d_q[0], d_q[1]) * factor).astype(bf16).astype(f32)
        d_gained = rotate_back(d_query, v.cosine[at, :], v.sine[at, :])
        hat, scale = pair_normed(v.q_raw[at, :])
        v.gain[8:9, :] += jnp.sum(d_gained * hat, 0, keepdims=True)
        v.d_qkv[at, 0:128] = pair_norm_back(d_gained * q_gain, hat, scale).astype(bf16)
        return 0

    v.gain[...] = jnp.zeros_like(v.gain)
    lax.fori_loop(0, 2, back, 0)
    blocks, block = v.grad_terms.shape[0], v.grad_terms.shape[1]
    grad_o = dot_tn(v.attn_o[...], v.d_all[...].reshape(group, width)).T
    for e in range(blocks):
        v.grad_terms[e, :, 256:384] = grad_o[e * block : (e + 1) * block].astype(bf16)
    mix_sums.turn(3)
    mix_sums.far(4)
    lax.fori_loop(2, 4, back, 0)

    d_kv = jnp.concatenate(
        [
            v.d_key_t[:HEAD_DIM] + v.d_key_t[HEAD_DIM:],
            v.d_value_t[0] + v.d_value_t[1],
        ],
        0,
    ).T
    first = low(d_kv.shape)
    d_key = jnp.where(first, d_kv, swap(d_kv)).astype(bf16).astype(f32)
    d_gained = rotate_back(d_key, v.cosine[...], v.sine[...])
    hat, scale = pair_normed(v.k_raw[...])
    v.gain[9:10, :] = jnp.sum(d_gained * hat, 0, keepdims=True)
    d_raw = pair_norm_back(d_gained * k_gain, hat, scale)
    v.d_qkv[:, 128:256] = jnp.where(first, d_raw, d_kv).astype(bf16)

    def spread(dy):
        def one(i, _):
            t = net.tp_at(dy, 1 - i)
            v.spare[rows_of(8 + t), :] = dot_nt(v.d_qkv[rows_of(t), :], v.w_qkv[...]).astype(bf16)
            return 0

        lax.fori_loop(0, 2, one, 0)

    grad_qkv = dot(v.h_t[...], v.d_qkv[...])
    for e in range(blocks):
        v.grad_terms[e, :, 0:256] = grad_qkv[e * block : (e + 1) * block].astype(bf16)
    grad_sums = ScatterEp(
        net,
        banks["ep0"],
        lambda e, start, count: v.grad_terms.at[e, pl.ds(start, count)],
        lambda i, start, count: v.grad_landed.at[i, pl.ds(start, count)],
        block,
    )
    for g in (3, 1, 2, 0):
        grad_sums.far(g)
    sums = token_sums()
    spread(2)
    sums.across(2)
    spread(1)
    sums.across(1)
    sums.far()
    spread(-1)
    sums.across(-1)
    for g in (3, 1, 2, 0):
        grad_sums.near(g)
    sums.near_first()
    spread(0)
    sums.across(0)
    products = grad_qkv * v.w_qkv[...].astype(f32)
    norm_sum = lax.dot_general(
        jnp.ones((8, 256), f32), products, (((1,), (1,)), ((), ())), precision=highest, preferred_element_type=f32
    )[0:1]
    norm_sum = norm_sum / v.norm_gain[...]
    for i in range(8):
        v.gain[i : i + 1, :] = norm_sum[:, i * 128 : (i + 1) * 128]
    gain_c = AxisSum(net, banks["gains"], v.gain.at[0:8], v.gain_got.at[0, :, 0:8], [C])
    sums.near_second()
    grad_sums.turn(3)
    grad_sums.far(4)
    small[mine, :] = small_y.finish()
    small_x = AxisSum(net, banks["small"], small.at[mine], v.small_got.at[1], ALONG_X)
    v.gain[0:8, :] = gain_c.finish()
    gain_y = AxisSum(net, banks["gains"], v.gain.at[0:8], v.gain_got.at[1, :, 0:8], ALONG_Y)
    grad_sums.turn(1)
    grad_sums.turn(2)
    grad_sums.near(4)
    grad_sums.turn(0)
    mix_sums.turn(1)
    mix_sums.turn(2)
    mix_sums.near(4)
    mix_sums.turn(0)
    for h in (0, 1):
        part = grad_sums.last(4, h).astype(bf16)
        v.grad_all[net.ep, h * (block // 2) : (h + 1) * (block // 2), :] = part
    spread_grads = GatherEp(net, banks["ep2"], v.grad_all, block)
    spread_grads.start()
    v.gain[0:8, :] = gain_y.finish()
    gain_x = AxisSum(net, banks["gains"], v.gain, v.gain_got.at[2], ALONG_X)
    small[mine, :] = small_x.finish()
    small_z = AxisSum(net, banks["small"], small.at[mine], v.small_got.at[2], ALONG_Z)

    x_hat, x_scale = normed(v.x[...].reshape(rows, width))
    total = jnp.concatenate([sums.last(0), sums.last(1)], 0)
    v.grad_input[...] = d_mid[...] + norm_back(total * v.norm_gain[...], x_hat, x_scale)

    spread_grads.first()
    spread_grads.second(0)
    spread_grads.far()
    v.gain[...] = gain_x.finish()
    gain_z = AxisSum(net, banks["gains"], v.gain, v.gain_got.at[3], ALONG_Z)
    spread_grads.second(-1)
    spread_grads.second(1)
    spread_grads.second(2)
    small[mine, :] = small_z.finish()
    small_last = net.send(small.at[mine], v.small_sib.at[mine], C, banks["small"])
    mix = jnp.concatenate([mix_sums.last(4, 0), mix_sums.last(4, 1)], 0)
    v.output[...] = jnp.where(place < seq_len, h_mid[...] + mix, 0.0)
    for out, sum_ in ((v.grad_gate, gate), (v.grad_up, up), (v.grad_down, down)):
        for j in (0, 1):
            out[j] = sum_.last(j)
    v.gain_out[...] = gain_z.finish()
    small_last.wait_recv()
    other = pl.ds(pl.multiple_of((1 - net.c) * share, 8), share)
    v.small_out[mine, :] = small[mine, :]
    v.small_out[other, :] = v.small_sib[other, :]
    prob_total = v.small_out[n_exp + 8 :, 0:n_exp]
    loss = jnp.dot(prob_total, counts, precision=highest, preferred_element_type=f32)
    v.loss[...] = loss * (n_exp / (8.0 * nvalid * nvalid)) + jnp.zeros((8, 128), f32)
    spread_grads.finish()
    for e in range(blocks):
        at = slice(e * block, (e + 1) * block)
        v.grad_query[at, :] = v.grad_all[e, :, 0:128].astype(f32)
        v.grad_keyval[at, :] = v.grad_all[e, :, 128:256].astype(f32)
    v.grad_out[...] = v.grad_all[:, :, 256:384].astype(f32).reshape(blocks * block, 128).T
    net.finish()


LARGE = ("output", "grad_input", "grad_query", "grad_keyval", "grad_out", "grad_gate", "grad_up", "grad_down")


def results_kernel(*refs):
    n = len(LARGE)
    large, (loss_in, gains, small), refs = refs[:n], refs[n : n + 3], refs[n + 3 :]
    out, (loss, norm_gain, query_gain, key_gain, mlp_gain, router), refs = refs[:n], refs[n : n + 6], refs[n + 6 :]
    held, sems = refs[:n], refs[n]
    reads = [pltpu.make_async_copy(large[i], held[i], sems.at[0, i]) for i in range(n)]
    for copy in reads:
        copy.start()
    n_exp = router.shape[0]
    loss[...] = loss_in[0:1, 0:1]
    for i in range(8):
        norm_gain[:, i * 128 : (i + 1) * 128] = gains[i : i + 1, :]
    query_gain[...] = gains[8:9, :]
    key_gain[...] = gains[9:10, 0:HEAD_DIM]
    mlp_gain[...] = small[n_exp : n_exp + 1, :]
    router[...] = small[0:n_exp, :]
    writes = []
    for i in range(n):
        reads[i].wait()
        writes.append(pltpu.make_async_copy(held[i], out[i], sems.at[1, i]))
        writes[i].start()
    for copy in writes:
        copy.wait()


def local(
    layer_input,
    lengths,
    routes,
    norm_gain,
    w_query,
    w_keyval,
    query_gain,
    key_gain,
    w_out,
    mlp_gain,
    w_router,
    w_gate,
    w_up,
    w_down,
    cotangent,
):
    rows, width = layer_input.shape
    group = rows * 8
    n_exp = w_router.shape[1]
    top_k = routes.shape[1]
    units = w_down.shape[1]
    ff = units * 8
    slots = 3 * rows * top_k // (2 * n_exp)
    full = 16 * slots
    n = BATCH * slots
    block = width // 16
    n_small = n_exp + 16
    cosine, sine = rotary(group)
    inputs = {
        "layer_input": (layer_input, ANY),
        "lengths": (lengths, SM),
        "routes_in": (routes.T, ANY),
        "norm_gain": (norm_gain.reshape(1, -1), VM),
        "w_query": (w_query, ANY),
        "w_keyval": (w_keyval.reshape(width, -1), ANY),
        "query_gain": (query_gain.reshape(1, -1), VM),
        "key_gain": (key_gain.reshape(1, -1), VM),
        "w_out_in": (w_out, ANY),
        "mlp_gain": (mlp_gain.reshape(1, -1), VM),
        "w_router_t": (w_router.T, VM),
        "w_gate": (w_gate.transpose(0, 2, 1), ANY),
        "w_up": (w_up.transpose(0, 2, 1), ANY),
        "w_down": (w_down, ANY),
        "cotangent": (cotangent, ANY),
        "cosine_in": (jnp.asarray(cosine), ANY),
        "sine_in": (jnp.asarray(sine), ANY),
    }
    outputs = {
        "output": (rows, width),
        "grad_input": (rows, width),
        "loss": (8, 128),
        "grad_query": (width, 128),
        "grad_keyval": (width, 128),
        "gain_out": (16, 128),
        "grad_out": (128, width),
        "small_out": (n_small, width),
        "grad_gate": (2, units, width),
        "grad_up": (2, units, width),
        "grad_down": (2, units, width),
    }
    eight = pltpu.VMEM((8, rows, width), bf16)
    sixteen = pltpu.VMEM((16, rows, width), bf16)
    row_bf = pltpu.VMEM((group, 128), bf16)
    row_f = pltpu.VMEM((group, 128), f32)
    piece = pltpu.VMEM((4, 4, 8, rows), f32)
    by_expert = pltpu.VMEM((n_exp, rows), f32)
    scratch = {
        "w_qkv": pltpu.VMEM((width, 256), bf16),
        "w_out": pltpu.VMEM((128, width), bf16),
        "cosine": row_f,
        "sine": row_f,
        "routes": pltpu.VMEM((top_k, 16 * group), jnp.int32),
        "w": pltpu.VMEM((2, 3 * ff, width), bf16),
        "k_gain": pltpu.VMEM((1, 128), f32),
        "h_t": pltpu.VMEM((width, group), bf16),
        "spare": pltpu.VMEM((16 * rows, width), bf16),
        "d_all": eight,
        "query": row_bf,
        "key": row_bf,
        "value": pltpu.VMEM((group, 256), bf16),
        "k_raw": row_f,
        "attn_o": row_bf,
        "from_sib": pltpu.VMEM((4, rows, width), bf16),
        "from_far": pltpu.VMEM((2, rows // 2, width), bf16),
        "from_near": pltpu.VMEM((2, rows, width), bf16),
        "tok": sixteen,
        "cot": sixteen,
        "hits": by_expert,
        "probs": by_expert,
        "soft": by_expert,
        "d_gates": by_expert,
        "places": pltpu.VMEM((16, 2 * slots, rows), bf16),
        "counted": pltpu.VMEM((n_exp, 8, 128), f32),
        "gate_out": piece,
        "gate_mid": piece,
        "gate_got": piece,
        "back_out": piece,
        "back_mid": piece,
        "back_got": piece,
        "big": pltpu.VMEM((4 * full, width), bf16),
        "deep": pltpu.VMEM((max(3 * full, 2 * group), 2 * ff), bf16),
        "row_back": pltpu.VMEM((2, n, width), bf16),
        "landed": pltpu.VMEM((30, rows // 2, width), bf16),
        "w_sib": pltpu.VMEM((4, 3, 2, units, width), bf16),
        "w_far": pltpu.VMEM((3, 2, units, width), bf16),
        "w_near": pltpu.VMEM((2, 3, 2, units, width), bf16),
        "small": pltpu.VMEM((n_small, width), f32),
        "small_sib": pltpu.VMEM((n_small, width), f32),
        "small_got": pltpu.VMEM((3, 3, n_small // 2, width), f32),
        "d_qkv": pltpu.VMEM((group, 256), bf16),
        "grad_terms": pltpu.VMEM((16, block, 384), bf16),
        "grad_landed": pltpu.VMEM((30, block // 2, 384), bf16),
        "grad_all": pltpu.VMEM((16, block, 384), bf16),
        "gain": pltpu.VMEM((16, 128), f32),
        "gain_got": pltpu.VMEM((4, 3, 16, 128), f32),
        "send_sems": pltpu.SemaphoreType.DMA((SENDS,)),
        "recv_sems": pltpu.SemaphoreType.DMA((sum(BANKS.values()),)),
    }
    got = pl.pallas_call(
        lambda *refs: layer_kernel(*refs, inputs=tuple(inputs), outputs=tuple(outputs), scratch=tuple(scratch)),
        name="layer",
        out_shape=tuple(shaped(shape, f32) for shape in outputs.values()),
        in_specs=[spec for _, spec in inputs.values()],
        out_specs=(VM,) * len(outputs),
        scratch_shapes=list(scratch.values()),
        compiler_params=params(1, 63.9),
    )(*[array for array, _ in inputs.values()])
    got = dict(zip(outputs, got, strict=True))
    large = [got[name] for name in LARGE]
    pieces = [got[name] for name in ("loss", "gain_out", "small_out")]
    sizes = [(1, 1), (1, width), (1, 128), (1, HEAD_DIM), (1, width), (n_exp, width)]
    got = pl.pallas_call(
        results_kernel,
        name="results",
        out_shape=tuple(shaped(a.shape, f32) for a in large) + tuple(shaped(size, f32) for size in sizes),
        in_specs=[pl.BlockSpec(memory_space=pltpu.HBM)] * len(large) + [VM] * len(pieces),
        out_specs=(ANY,) * len(large) + (VM,) * len(sizes),
        scratch_shapes=[pltpu.VMEM(a.shape, f32) for a in large] + [pltpu.SemaphoreType.DMA((2, len(large)))],
        compiler_params=pltpu.CompilerParams(vmem_limit_bytes=62 * MIB),
    )(*large, *pieces)
    large = dict(zip(LARGE, got, strict=False))
    loss, grad_norm_gain, grad_query_gain, grad_key_gain, grad_mlp_gain, grad_router = got[len(LARGE) :]
    return (
        large["output"],
        large["grad_input"],
        loss.reshape(()),
        grad_norm_gain.reshape(-1),
        large["grad_query"],
        large["grad_keyval"].reshape(w_keyval.shape),
        grad_query_gain.reshape(-1),
        grad_key_gain.reshape(-1),
        large["grad_out"],
        grad_mlp_gain.reshape(-1),
        grad_router.T,
        large["grad_gate"].transpose(0, 2, 1),
        large["grad_up"].transpose(0, 2, 1),
        large["grad_down"],
    )


def solution(mesh):
    in_specs = (
        P(("ep", "tp"), None),
        P(),
        P(),
        P(),
        P(None, "tp"),
        P(None, "tp", None),
        P("tp"),
        P("tp"),
        P("tp", None),
        P(),
        P(),
        P("ep", None, "tp"),
        P("ep", None, "tp"),
        P("ep", "tp", None),
        P(("ep", "tp"), None),
    )
    out_specs = (
        P(("ep", "tp"), None),
        P(("ep", "tp"), None),
        P(),
        P(),
        P(None, "tp"),
        P(None, "tp", None),
        P("tp"),
        P("tp"),
        P("tp", None),
        P(),
        P(),
        P("ep", None, "tp"),
        P("ep", None, "tp"),
        P("ep", "tp", None),
    )
    return jax.shard_map(local, mesh=mesh, in_specs=in_specs, out_specs=out_specs, check_vma=False)
```

```python
import jax
import jax.numpy as jnp
import numpy as np
from jax import lax
from jax.experimental import pallas as pl
from jax.experimental.pallas import tpu as pltpu
from jax.sharding import PartitionSpec as P

MESH = pl.DeviceIdType.MESH
f32, bf16 = jnp.float32, jnp.bfloat16
HEAD_DIM = 64
epsilon = 1e-06
masked_score = -1e30
highest = lax.Precision.HIGHEST
MIB = 2**20

X, Y, Z, C = (1, 0, 0, 0), (0, 1, 0, 0), (0, 0, 1, 0), (0, 0, 0, 1)
XM, YM, ZM = (-1, 0, 0, 0), (0, -1, 0, 0), (0, 0, -1, 0)
X2, Z2 = (2, 0, 0, 0), (0, 0, 2, 0)
NEAR = (0, 1, -1, 2)


def times(d, k):
    return tuple(v * k for v in d)


class Bank:
    def __init__(self, first, size):
        self.first, self.size, self.used = first, size, 0

    def restart(self):
        self.used = 0
        return self

    def take(self):
        assert self.used < self.size
        self.used += 1
        return self.first + self.used - 1


class Net:
    def __init__(self, send_sems, recv_sems):
        self.ep, self.tp = lax.axis_index("ep"), lax.axis_index("tp")
        self.x, self.z = self.ep // 4, self.ep % 4
        self.y, self.c = self.tp // 2, self.tp % 2
        self.send_sems, self.recv_sems = send_sems, recv_sems
        self.free = list(range(SENDS))
        self.unsent = {}
        self.group = None

    def device(self, d):
        x, y = (self.x + d[0]) % 4, (self.y + d[1]) % 4
        z, c = (self.z + d[2]) % 4, (self.c + d[3]) % 2
        return (x * 4 + z, y * 2 + c)

    def ep_at(self, dx, dz):
        return ((self.x + dx) % 4) * 4 + (self.z + dz) % 4

    def tp_at(self, dy, dc):
        return ((self.y + dy) % 4) * 2 + (self.c + dc) % 2

    def barrier(self, dirs):
        sem = pltpu.get_barrier_semaphore()
        for d in dirs:
            pl.semaphore_signal(sem, inc=1, device_id=self.device(d), device_id_type=MESH)
        pl.semaphore_wait(sem, len(dirs))

    def send(self, src, dst, d, bank):
        i = self.free.pop(0)
        copy = pltpu.make_async_remote_copy(
            src_ref=src,
            dst_ref=dst,
            send_sem=self.send_sems.at[i],
            recv_sem=self.recv_sems.at[bank.take()],
            device_id=self.device(d),
            device_id_type=MESH,
        )
        copy.start()
        self.unsent.setdefault(self.group, []).append((copy, i))
        return copy

    def keep(self, src, dst):
        i = self.free.pop(0)
        copy = pltpu.make_async_copy(src, dst, self.send_sems.at[i])
        copy.start()
        return copy, i

    def kept(self, pair):
        pair[0].wait()
        self.free.append(pair[1])

    def sent(self, copy):
        for group, pairs in self.unsent.items():
            for _, i in [pair for pair in pairs if pair[0] is copy]:
                copy.wait_send()
                self.free.append(i)
            self.unsent[group] = [pair for pair in pairs if pair[0] is not copy]

    def finish(self, *groups):
        for group in groups or tuple(self.unsent):
            for copy, i in self.unsent.pop(group, ()):
                copy.wait_send()
                self.free.append(i)


class GatherTp:
    def __init__(self, net, bank, ref, own=None):
        self.net, self.bank, self.ref = net, bank.restart(), ref
        self.own = own or (lambda half: ref(net.tp, half))
        self.copies = {}
        self.done = set()

    def wait(self, *key):
        if key not in self.done:
            self.done.add(key)
            self.copies[key].wait_recv()

    def along(self, dy, half, sign):
        src = self.own(half) if dy == 0 else self.ref(self.net.tp_at(dy, 0), half)
        to = (dy - sign + 1) % 4 - 1
        self.copies[("y", to, half)] = self.net.send(
            src, self.ref(self.net.tp_at(dy, 0), half), times(Y, sign), self.bank
        )

    def across(self, dy):
        for half in (0, 1):
            src = self.own(half) if dy == 0 else self.ref(self.net.tp_at(dy, 0), half)
            self.copies[("c", dy, half)] = self.net.send(
                src, self.ref(self.net.tp_at(dy, 0), half), C, self.bank
            )

    def start(self):
        self.along(0, 0, 1)
        self.along(0, 1, -1)
        self.along(0, 1, 1)
        self.along(0, 0, -1)
        self.across(0)

    def relay(self):
        self.wait("y", -1, 0)
        self.along(-1, 0, 1)
        self.wait("y", 1, 1)
        self.along(1, 1, -1)

    def share(self):
        for dy, half in ((-1, 1), (1, 0)):
            self.wait("y", dy, half)
            self.across(dy)

    def spread(self):
        for half in (0, 1):
            self.wait("y", 2, half)
        self.across(2)

    def need(self, dy, dc):
        if dc:
            for half in (0, 1):
                self.wait("c", dy, half)
        elif dy:
            for half in (0, 1):
                self.wait("y", dy, half)

    def finish(self):
        for key in list(self.copies):
            self.wait(*key)


class ScatterTp:
    def __init__(self, net, bank, ref, sib, far, near):
        self.bank = bank.restart()
        self.net, self.ref, self.sib, self.far_at, self.near_at = net, ref, sib, far, near
        self.copies = {}

    def across(self, dy):
        i = NEAR.index(dy)
        for half in (0, 1):
            self.copies[("c", dy, half)] = self.net.send(
                self.ref(self.net.tp_at(dy, 1), half), self.sib(i, half), C, self.bank
            )

    def join(self, dy, half):
        self.copies[("c", dy, half)].wait_recv()
        return self.ref(self.net.tp_at(dy, 0), half)[...] + self.sib(NEAR.index(dy), half)[...]

    def far(self):
        for half, sign in ((0, 1), (1, -1)):
            ref = self.ref(self.net.tp_at(2, 0), half)
            ref[...] = self.join(2, half)
            self.copies[("f", half)] = self.net.send(ref, self.far_at(half), times(Y, sign), self.bank)

    def towards(self, part, half):
        sign = (1, -1)[part]
        ref = self.ref(self.net.tp_at(sign, 0), half)
        total = self.join(sign, half)
        if half == part:
            self.copies[("f", part)].wait_recv()
            total = total + self.far_at(part)[...]
        ref[...] = total
        self.copies[("n", part, half)] = self.net.send(
            ref, self.near_at(part, half), times(Y, sign), self.bank
        )

    def near_first(self):
        for part in (0, 1):
            self.towards(part, 1 - part)

    def near_second(self):
        for part in (0, 1):
            self.towards(part, part)

    def last(self, half):
        total = self.join(0, half).astype(f32)
        for part in (0, 1):
            self.copies[("n", part, half)].wait_recv()
            total = total + self.near_at(part, half)[...].astype(f32)
        return total


class GatherEp:
    def __init__(self, net, bank, buf, rows):
        self.bank = bank.restart()
        self.net, self.buf, self.rows = net, buf, rows
        self.copies = {}
        self.done = set()

    def ref(self, h, j, k, part):
        half, quarter = self.rows // 2, self.rows // 4
        e = self.net.ep_at(j, k) if h == 0 else self.net.ep_at(k, j)
        if part is None:
            return self.buf.at[e, pl.ds(h * half, half)]
        return self.buf.at[e, pl.ds(h * half + part * quarter, quarter)]

    def send(self, h, j, k, part, along, sign):
        d = (X, Z)[along if h == 0 else 1 - along]
        r = self.ref(h, j, k, part)
        to = (j - sign, k) if along == 0 else (j, k - sign)
        to = tuple((v + 1) % 4 - 1 for v in to)
        self.copies[(h, *to, part)] = self.net.send(r, r, times(d, sign), self.bank)

    def wait(self, *key):
        if key not in self.done:
            self.done.add(key)
            self.copies[key].wait_recv()

    def need(self, h, j, k):
        if (j, k) != (0, 0):
            for part in (None,) if (h, j, k, None) in self.copies else (0, 1):
                self.wait(h, j, k, part)

    def block(self, dx, dz):
        self.need(0, dx, dz)
        self.need(1, dz, dx)

    def start(self):
        for along in (0, 1):
            for h in (0, 1):
                for sign in (1, -1):
                    self.send(h, 0, 0, None, along, sign)

    def first(self):
        for part, sign in ((0, 1), (1, -1)):
            for h in (0, 1):
                self.wait(h, -sign, 0, None)
                self.send(h, -sign, 0, part, 0, sign)
        for sign in (1, -1):
            for h in (0, 1):
                for turn in (1, -1):
                    self.send(h, -sign, 0, None, 1, turn)

    def far(self):
        for h in (0, 1):
            self.need(h, 2, 0)
            for turn in (1, -1):
                self.send(h, 2, 0, None, 1, turn)

    def second(self, j):
        for part, sign in ((0, 1), (1, -1)):
            for h in (0, 1):
                self.wait(h, j, -sign, None)
                self.send(h, j, -sign, part, 1, sign)

    def finish(self):
        for key in list(self.copies):
            self.wait(*key)


class ScatterEp:
    def __init__(self, net, bank, term, landed, rows):
        self.bank = bank.restart()
        self.net, self.term, self.landed, self.rows = net, term, landed, rows
        self.copies = {}

    def ref(self, h, g, j, part):
        j, k = (j, NEAR[g]) if g < 4 else (0, j)
        half, quarter = self.rows // 2, self.rows // 4
        e = self.net.ep_at(k, j) if h == 0 else self.net.ep_at(j, k)
        if part is None:
            return self.term(e, h * half, half)
        return self.term(e, h * half + part * quarter, quarter)

    def slot(self, g, h, which, part=None):
        half, quarter = self.rows // 2, self.rows // 4
        i = (g * 2 + h) * 3 + which
        return self.landed(i, 0, half) if part is None else self.landed(i, part * quarter, quarter)

    def dir(self, h, g, sign):
        return times((Z, X)[(g == 4) if h == 0 else (g != 4)], sign)

    def far(self, g):
        for h in (0, 1):
            for part, sign in ((0, 1), (1, -1)):
                self.copies[(g, h, 2, part)] = self.net.send(
                    self.ref(h, g, 2, part), self.slot(g, h, 2, part), self.dir(h, g, sign), self.bank
                )

    def near(self, g):
        for h in (0, 1):
            for part, sign in ((0, 1), (1, -1)):
                self.copies[(g, h, 2, part)].wait_recv()
                r = self.ref(h, g, sign, part)
                r[...] = r[...] + self.slot(g, h, 2, part)[...]
                self.copies[(g, h, part)] = self.net.send(
                    self.ref(h, g, sign, None), self.slot(g, h, part), self.dir(h, g, sign), self.bank
                )

    def last(self, g, h):
        for part in (0, 1):
            self.copies[(g, h, part)].wait_recv()
        total = self.ref(h, g, 0, None)[...].astype(f32)
        for part in (0, 1):
            total = total + self.slot(g, h, part)[...].astype(f32)
        return total

    def turn(self, g):
        for h in (0, 1):
            self.ref(h, g, 0, None)[...] = self.last(g, h).astype(bf16)


def lanes(shape):
    return lax.broadcasted_iota(jnp.int32, shape, len(shape) - 1)


def low(shape):
    return lanes(shape) < HEAD_DIM


def normed(v):
    factor = lax.rsqrt(jnp.mean(v * v, -1, keepdims=True) + epsilon)
    return v * factor, factor


def norm_back(grad, hat, factor):
    return factor * (grad - hat * jnp.mean(grad * hat, -1, keepdims=True))


def pair_sums(v):
    first = low(v.shape)
    a = jnp.sum(jnp.where(first, v, 0.0), -1, keepdims=True)
    b = jnp.sum(jnp.where(first, 0.0, v), -1, keepdims=True)
    return jnp.where(first, a, b)


def pair_normed(v):
    factor = lax.rsqrt(pair_sums(v * v) / HEAD_DIM + epsilon)
    return v * factor, factor


def pair_norm_back(grad, hat, factor):
    return factor * (grad - hat * (pair_sums(grad * hat) / HEAD_DIM))


def partner(v):
    half = HEAD_DIM // 2
    return jnp.where(
        lanes(v.shape) % HEAD_DIM < half, pltpu.roll(v, 128 - half, 1), pltpu.roll(v, half, 1)
    )


def rotate(v, cosine, sine):
    return v * cosine + partner(v) * sine


def rotate_back(v, cosine, sine):
    return v * cosine - partner(v) * sine


def swap(v):
    return pltpu.roll(v, HEAD_DIM, v.ndim - 1)


def dot(a, b):
    return jnp.dot(a, b, preferred_element_type=f32)


def dot_nt(a, b):
    return lax.dot_general(a, b, (((1,), (1,)), ((), ())), preferred_element_type=f32)


def dot_tn(a, b):
    return lax.dot_general(a, b, (((0,), (0,)), ((), ())), preferred_element_type=f32)


def rotary(length):
    half = HEAD_DIM // 2
    frequency = 10000.0 ** (-(np.arange(half, dtype=np.float64) * 2.0 / HEAD_DIM))
    angles = np.arange(length, dtype=np.float64)[:, None] * frequency[None, :]
    cosine, sine = np.cos(angles), np.sin(angles)
    cosine = np.concatenate([cosine] * 4, -1).astype(np.float32)
    sine = np.concatenate([-sine, sine] * 2, -1).astype(np.float32)
    return cosine, sine


VM = pl.BlockSpec(memory_space=pltpu.VMEM)
SM = pl.BlockSpec(memory_space=pltpu.SMEM)
ANY = pl.BlockSpec(memory_space=pl.ANY)


def shaped(shape, dtype):
    return jax.ShapeDtypeStruct(shape, dtype)


def params(collective_id, vmem):
    return pltpu.CompilerParams(
        collective_id=collective_id, has_side_effects=True, vmem_limit_bytes=int(vmem * MIB)
    )


def key_value(qkv, q_gain, k_gain, cosine, sine):
    q_hat, _ = pair_normed(qkv[:, :128])
    kv = qkv[:, 128:]
    first = low(kv.shape)
    other = swap(kv)
    k_raw = jnp.where(first, kv, other)
    k_hat, _ = pair_normed(k_raw)
    query = (rotate(q_hat * q_gain, cosine, sine).astype(bf16).astype(f32) * HEAD_DIM**-0.5).astype(bf16)
    key = rotate(k_hat * k_gain, cosine, sine).astype(bf16)
    value = jnp.where(first, other, kv).astype(bf16)
    value = jnp.concatenate([value, jnp.ones_like(value)], -1)
    return query, key, value, qkv[:, :128], k_raw


class Exchange:
    def __init__(self, net, bank, out, half_way, got):
        self.bank = bank.restart()
        self.net, self.out, self.half_way, self.got = net, out, half_way, got

    def start(self):
        net = self.net
        self.first = [
            net.send(self.out.at[(net.x + k) % 4], self.half_way.at[net.x], times(X, k), self.bank)
            for k in (1, -1, 2)
        ]
        self.half_way[net.x] = self.out[net.x]

    def turn(self):
        net = self.net
        for copy in self.first:
            copy.wait_recv()
        self.second = [
            net.send(self.half_way.at[:, (net.z + k) % 4], self.got.at[:, net.z], times(Z, k), self.bank)
            for k in (1, -1, 2)
        ]
        self.got[:, net.z] = self.half_way[:, net.z]

    def finish(self):
        for copy in self.second:
            copy.wait_recv()


class AxisSum:
    def __init__(self, net, bank, term, slots, steps):
        self.net, self.term, self.slots = net, term, slots
        self.copies = [net.send(term, slots.at[i], d, bank) for i, d in enumerate(steps)]

    def finish(self):
        total = self.term[...].astype(f32)
        for i, copy in enumerate(self.copies):
            copy.wait_recv()
            total = total + self.slots[i].astype(f32)
            self.net.sent(copy)
        return total


ALONG_X, ALONG_Y, ALONG_Z = ([times(d, k) for k in (1, -1, 2)] for d in (X, Y, Z))
Y2 = times(Y, 2)

SENDS = 232
BANKS = {"ep0": 40, "ep1": 40, "ep2": 40, "tp0": 14, "tp1": 14}
BANKS |= {name + str(a): 14 for name in ("gather", "scatter") for a in range(3)}
BANKS |= {"gates": 6, "back": 6, "small": 11, "gains": 10}

ORDER = (
    (0, 0), (-1, 0), (1, 0), (0, -1),
    (0, 1), (2, 0), (0, 2), (-1, -1),
    (-1, 1), (1, -1), (1, 1), (2, -1),
    (2, 1), (-1, 2), (1, 2), (2, 2),
)
BATCH = 8


def layer_kernel(*refs, inputs, outputs, scratch):
    names = inputs + outputs + scratch
    r = dict(zip(names, refs, strict=True))

    class R:
        pass

    v = R()
    for name, ref in r.items():
        setattr(v, name, ref)
    v.totals, v.q_raw, v.d_key_t = v.grad_query, v.grad_keyval, v.grad_out
    v.d_value_t, v.x, v.cot_f = v.grad_gate, v.grad_up, v.grad_down
    net = Net(v.send_sems, v.recv_sems)
    banks, first = {}, 0
    for name, size in BANKS.items():
        banks[name] = Bank(first, size)
        first += size
    rows, width = v.output.shape
    half_rows = rows // 2
    group = rows * 8
    units = v.w_down.shape[1]
    ff = units * 8
    n_exp = v.w_router_t.shape[0]
    slots = v.places.shape[1] // 2
    full = 16 * slots
    seq_len = v.lengths[net.ep]
    factor = HEAD_DIM**-0.5

    def weight(a, j, t):
        return v.w.at[j, pl.ds(pl.multiple_of(a * ff + t * units, units), units)]

    def rows_of(i, count=1):
        return pl.ds(pl.multiple_of(i * rows, rows), rows * count)

    def half_of(t, half):
        return pl.ds(pl.multiple_of(t * rows + half * half_rows, half_rows), half_rows)

    x_load = [net.keep(v.layer_input.at[pl.ds(i * half_rows, half_rows)], v.x.at[i]) for i in (0, 1)]
    early = [
        net.keep(v.w_query, v.w_qkv.at[:, pl.ds(0, 128)]),
        net.keep(v.w_keyval, v.w_qkv.at[:, pl.ds(128, 128)]),
        net.keep(v.cosine_in, v.cosine),
        net.keep(v.sine_in, v.sine),
    ]
    cot_load = [net.keep(v.cotangent.at[pl.ds(i * half_rows, half_rows)], v.cot_f.at[i]) for i in (0, 1)]
    weight_loads = [
        net.keep(source.at[j], weight(a, j, net.tp))
        for a, source in enumerate((v.w_gate, v.w_up, v.w_down))
        for j in (0, 1)
    ]
    late = [net.keep(v.routes_in, v.routes), net.keep(v.w_out_in, v.w_out)]
    net.barrier([X, XM, X2, Y, YM, Y2, Z, ZM, Z2, C])

    for copy in x_load:
        net.kept(copy)
    x_hat, _ = normed(v.x[...].reshape(rows, width))
    v.spare[rows_of(net.tp), :] = (x_hat * v.norm_gain[...]).astype(bf16)
    tokens = GatherTp(net, banks["tp0"], lambda t, half: v.spare.at[half_of(t, half)])
    tokens.start()
    place = net.tp * rows + lax.broadcasted_iota(jnp.int32, (rows, 1), 0)
    for copy in cot_load:
        net.kept(copy)
    v.cot[net.ep] = jnp.where(place < seq_len, v.cot_f[...].reshape(rows, width), 0.0).astype(bf16)
    cots = GatherEp(net, banks["ep0"], v.cot, rows)
    net.group = "cot"
    cots.start()
    net.group = None

    for copy in early + late:
        net.kept(copy)
    v.k_gain[:, 0:HEAD_DIM] = v.key_gain[...]
    k_gain = v.k_gain[...]
    k_gain = jnp.where(low(k_gain.shape), k_gain, swap(k_gain))
    q_gain = v.query_gain[...]

    def project(dy):
        at = rows_of(net.tp_at(dy, 0) - net.c, 2)
        h = v.spare[at, :]
        parts = key_value(dot(h, v.w_qkv[...]), q_gain, k_gain, v.cosine[at, :], v.sine[at, :])
        for ref, part in zip((v.query, v.key, v.value, v.q_raw, v.k_raw), parts, strict=True):
            ref[at, :] = part
        v.h_t[:, at] = h.T

    def routing():
        for s in range(16):
            segment = v.routes[:, rows_of(s * 8 + net.tp)]
            for j in (0, 1):
                same = (segment == net.ep * 2 + j).astype(f32)
                v.hits[2 * s + j : 2 * s + j + 1, :] = jnp.max(same, 0, keepdims=True)
        before = lax.broadcasted_iota(jnp.int32, (rows, rows), 0) < lanes((rows, rows))
        rank = dot(v.hits[...].astype(bf16), before.astype(bf16))
        rank = jnp.where(v.hits[...] > 0.5, rank, -1.0)
        slot = lax.broadcasted_iota(jnp.int32, (slots, rows), 0).astype(f32)
        for s in range(16):
            for j in (0, 1):
                mine = rank[2 * s + j : 2 * s + j + 1]
                v.places[s, j * slots : (j + 1) * slots, :] = (slot == mine).astype(bf16)

    def count():
        v.counted[...] = jnp.zeros_like(v.counted)

        def one(g, _):
            segment = v.routes[:, pl.ds(pl.multiple_of(g * group, group), group)]
            segment = jnp.where(lanes(segment.shape) < v.lengths[g], segment, -1)
            for e in range(n_exp):
                hit = (segment == e).astype(f32)
                total = hit[:, 0:128]
                for i in range(1, group // 128):
                    total = total + hit[:, i * 128 : (i + 1) * 128]
                v.counted[e] += total
            return 0

        lax.fori_loop(0, 16, one, 0)

    routing()
    count()
    tokens.need(0, 1)
    project(0)
    tokens.relay()
    cots_step = lambda step, *a: (setattr(net, "group", "cot"), step(*a), setattr(net, "group", None))
    cots_step(cots.first)
    tokens.share()
    cots_step(cots.second, 0)
    tokens.need(-1, 1)
    project(-1)
    tokens.need(1, 1)
    project(1)
    cots_step(cots.far)
    tokens.spread()
    for copy in weight_loads:
        net.kept(copy)
    w_step = lambda step, *a: (setattr(net, "group", "w"), step(*a), setattr(net, "group", None))
    gate, up, down = (
        GatherTp(net, banks[f"gather{a}"], lambda t, half, a=a: weight(a, half, t)) for a in range(3)
    )
    w_step(gate.start)
    tokens.need(2, 1)
    project(2)
    tokens.finish()

    bias = jnp.where(lanes((1, group)) < seq_len, 0.0, masked_score)

    def weights_of(q, head):
        q_head = jnp.where(low(q.shape) == (head == 0), q, jnp.zeros_like(q))
        return jnp.exp(dot_nt(q_head, v.key[...]) + bias).astype(bf16)

    def attend(dy):
        def one(i, _):
            t = net.tp_at(dy, 1 - i)
            at = rows_of(t)
            q = v.query[at, :]
            first = low(q.shape)
            mixed = [dot(weights_of(q, head), v.value[...]) for head in (0, 1)]
            total = jnp.where(first, mixed[0][:, 128:], mixed[1][:, 128:])
            o = (jnp.where(first, mixed[0][:, :128], mixed[1][:, :128]) / total).astype(bf16)
            v.attn_o[at, :] = o
            v.totals[at, :] = total
            v.spare[rows_of(8 + t), :] = dot(o, v.w_out[...]).astype(bf16)
            return 0

        lax.fori_loop(0, 2, one, 0)

    def token_sums():
        return ScatterTp(
            net,
            banks["tp1"],
            lambda t, half: v.spare.at[half_of(8 + t, half)],
            lambda i, half: v.from_sib.at[i, pl.ds(half * half_rows, half_rows)],
            lambda half: v.from_far.at[half],
            lambda part, half: v.from_near.at[part, pl.ds(half * half_rows, half_rows)],
        )

    sums = token_sums()
    attend(2)
    sums.across(2)
    attend(1)
    sums.across(1)
    sums.far()
    attend(-1)
    sums.across(-1)
    cots_step(cots.second, -1)
    sums.near_first()
    attend(0)
    sums.across(0)
    sums.near_second()
    w_step(gate.relay)
    w_step(up.start)
    cots_step(cots.second, 1)
    cots_step(cots.second, 2)
    h_mid = v.output
    for half in (0, 1):
        at = pl.ds(half * half_rows, half_rows)
        h_mid[at, :] = v.x[half] + sums.last(half)
    net.finish(None)

    h_hat, h_scale = normed(h_mid[...])
    mlp_in = h_hat * v.mlp_gain[...]
    v.tok[net.ep] = mlp_in.astype(bf16)
    tokens = GatherEp(net, banks["ep1"], v.tok, rows)
    tokens.start()
    w_step(down.start)
    w_step(gate.share)
    w_step(up.relay)

    w_router_t = v.w_router_t
    logits = lax.dot_general(
        w_router_t[...], mlp_in, (((1,), (1,)), ((), ())), precision=highest, preferred_element_type=f32
    )
    token_at = net.tp * rows + lanes((1, rows))
    valid = jnp.where(token_at < seq_len, 1.0, 0.0)
    expert = lax.broadcasted_iota(jnp.int32, (n_exp, rows), 0)
    mine = v.routes[:, rows_of(net.ep * 8 + net.tp)]
    chosen = expert == mine[0:1]
    for k in range(1, mine.shape[0]):
        chosen = jnp.logical_or(chosen, expert == mine[k : k + 1])
    top = jnp.max(logits, 0, keepdims=True)
    weights = jnp.exp(logits - top)
    probs = weights / jnp.sum(weights, 0, keepdims=True)
    top = jnp.max(jnp.where(chosen, logits, masked_score), 0, keepdims=True)
    weights = jnp.where(chosen, jnp.exp(jnp.where(chosen, logits - top, 0.0)), 0.0)
    soft = weights / jnp.sum(weights, 0, keepdims=True)
    v.probs[...] = probs
    v.soft[...] = soft
    gates = soft * valid
    for e in range(16):
        v.gate_out[e // 4, e % 4, 0:2, :] = gates[2 * e : 2 * e + 2]
    to_owners = Exchange(net, banks["gates"], v.gate_out, v.gate_mid, v.gate_got)
    to_owners.start()

    cots.finish()
    net.finish("cot")
    tokens.first()
    w_step(up.share)
    w_step(gate.spread)
    to_owners.turn()
    tokens.second(0)
    w_step(down.relay)
    w_step(up.spread)
    tokens.far()
    w_step(down.share)
    to_owners.finish()
    tokens.second(-1)
    tokens.second(1)
    w_step(down.spread)
    tokens.second(2)
    for gather in (gate, up, down):
        gather.finish()
    net.finish("w")

    n = BATCH * slots

    def picked(j, at, count):
        return pl.ds(pl.multiple_of(j * full + at, slots), count)

    def d_picked(j, at, count):
        return pl.ds(pl.multiple_of((2 + j) * full + at, slots), count)

    def batch(b):
        members = []
        for i, (dx, dz) in enumerate(ORDER[b * BATCH : (b + 1) * BATCH]):
            tokens.block(dx, dz)
            s = net.ep_at(dx, dz)
            members.append((s, (net.x + dx) % 4, (net.z + dz) % 4))
            here = v.places[s]
            taken = dot(here, v.tok[s]).astype(bf16)
            taken_d = dot(here, v.cot[s]).astype(bf16)
            for j in (0, 1):
                v.big[picked(j, b * n + i * slots, slots), :] = taken[j * slots : (j + 1) * slots]
                v.big[d_picked(j, b * n + i * slots, slots), :] = taken_d[j * slots : (j + 1) * slots]

        def one(j, _):
            at, at_d = picked(j, b * n, n), d_picked(j, b * n, n)
            gate_col = []
            for s, sx, sz in members:
                here = v.places[s, pl.ds(pl.multiple_of(j * slots, slots), slots), :].astype(f32)
                gate_col.append(jnp.sum(here * v.gate_got[sx, sz, pl.ds(j, 1), :], -1, keepdims=True))
            gate_col = jnp.concatenate(gate_col, 0)
            pre = dot_nt(v.big[at, :], v.w[j, 0 : 2 * ff])
            d_hidden = dot_nt(v.big[at_d, :], v.w[j, 2 * ff :])
            g, u = pre[:, :ff], pre[:, ff:]
            sigma = 0.5 * jnp.tanh(0.5 * g) + 0.5
            act = g * sigma
            hid = act * u
            d_gate = jnp.sum(d_hidden * hid, -1, keepdims=True)
            hid = (gate_col * hid).astype(bf16)
            v.deep[pl.ds(2 * full + b * n, n), pl.ds(pl.multiple_of(j * ff, ff), ff)] = hid
            d_hidden = d_hidden * gate_col
            v.deep[at, 0:ff] = (d_hidden * u * (sigma * (1.0 + g - act))).astype(bf16)
            v.deep[at, ff:] = (d_hidden * act).astype(bf16)
            v.spare[picked(j, b * n, n), :] = dot(hid, v.w[j, 2 * ff :]).astype(bf16)
            v.row_back[j] = dot(v.deep[at, :], v.w[j, 0 : 2 * ff]).astype(bf16)
            for i, (s, sx, sz) in enumerate(members):
                here = v.places[s, pl.ds(pl.multiple_of(j * slots, slots), slots), :].astype(f32)
                d = jnp.sum(here * d_gate[i * slots : (i + 1) * slots], 0, keepdims=True)
                v.back_out[sx, sz, pl.ds(j, 1), :] = d
            return 0

        lax.fori_loop(0, 2, one, 0)
        for i, (s, _, _) in enumerate(members):
            at = pl.ds(i * slots, slots)
            both = jnp.concatenate([v.row_back[0, at, :], v.row_back[1, at, :]], 0)
            v.cot[s] = dot_tn(v.places[s], both).astype(bf16)

    row_sums = ScatterEp(
        net,
        banks["ep0"],
        lambda e, start, count: v.cot.at[e, pl.ds(start, count)],
        lambda i, start, count: v.landed.at[i, pl.ds(start, count)],
        rows,
    )
    batch(0)
    tokens.finish()
    net.finish(None)
    row_sums.far(0)
    batch(1)

    to_tokens = Exchange(net, banks["back"], v.back_out, v.back_mid, v.back_got)
    to_tokens.start()
    mix_sums = ScatterEp(
        net,
        banks["ep1"],
        lambda e, start, count: v.big.at[pl.ds(pl.multiple_of(e * rows + start, 16), count)],
        lambda i, start, count: v.tok.at[i // 2, pl.ds(i % 2 * half_rows + start, count)],
        rows,
    )
    for g in (3, 1, 2):
        row_sums.far(g)
    row_sums.near(0)

    def grads(j, _):
        v.w[j, 0 : 2 * ff] = dot_tn(
            v.deep[picked(j, 0, full), :], v.big[picked(j, 0, full), :]
        ).astype(bf16)
        hidden = v.deep[2 * full : 3 * full, pl.ds(pl.multiple_of(j * ff, ff), ff)]
        v.w[j, 2 * ff :] = dot_tn(hidden, v.big[d_picked(j, 0, full), :]).astype(bf16)
        return 0

    lax.fori_loop(0, 2, grads, 0)
    gate, up, down = (
        ScatterTp(
            net,
            banks[f"scatter{a}"],
            lambda t, half, a=a: weight(a, half, t),
            lambda i, half, a=a: v.w_sib.at[i, a, half],
            lambda half, a=a: v.w_far.at[a, half],
            lambda part, half, a=a: v.w_near.at[part, a, half],
        )
        for a in range(3)
    )
    for dy in (2, 1, -1, 0):
        for sum_ in (gate, up, down):
            w_step(sum_.across, dy)
    to_tokens.turn()
    for g in (3, 1, 2):
        row_sums.near(g)
    for sum_ in (gate, up, down):
        w_step(sum_.far)
    for sum_ in (gate, up, down):
        w_step(sum_.near_first)
    for s in range(16):
        i = net.ep_at(*ORDER[s])
        both = jnp.concatenate([v.spare[picked(j, s * slots, slots), :] for j in (0, 1)], 0)
        v.big[rows_of(i), :] = dot_tn(v.places[i], both).astype(bf16)
    row_sums.turn(3)
    row_sums.far(4)
    to_tokens.finish()

    for e in range(16):
        v.d_gates[2 * e : 2 * e + 2, :] = v.back_got[e // 4, e % 4, 0:2, :]
    probs, soft = v.probs[...], v.soft[...]
    d_gates = v.d_gates[...] * valid
    d_chosen = soft * (d_gates - jnp.sum(soft * d_gates, 0, keepdims=True))
    nvalid = jnp.int32(0)
    for e in range(16):
        nvalid = nvalid + v.lengths[e]
    nvalid = nvalid.astype(f32)
    counts = jnp.sum(jnp.sum(v.counted[...], 1), -1, keepdims=True)
    balance = n_exp * counts / (8 * nvalid * nvalid)
    d_logits = d_chosen + valid * probs * (balance - jnp.sum(probs * balance, 0, keepdims=True))
    d_mlp_in = lax.dot_general(
        d_logits, w_router_t[...], (((0,), (0,)), ((), ())), precision=highest, preferred_element_type=f32
    )
    h_hat, h_scale = normed(h_mid[...])
    mlp_in = h_hat * v.mlp_gain[...]
    small, gain = v.small, v.gain
    small[...] = jnp.dot(d_logits, mlp_in, precision=highest, preferred_element_type=f32).astype(bf16)
    gain[...] = jnp.zeros_like(gain)
    gain[16:24, 0:n_exp] = lax.dot_general(
        valid + jnp.zeros((8, rows), f32), probs, (((1,), (1,)), ((), ())), precision=highest, preferred_element_type=f32
    )
    small_first = net.send(small, v.small_sib, C, banks["small"])
    row_sums.turn(1)
    row_sums.turn(2)
    row_sums.near(4)
    row_sums.turn(0)
    d_out = jnp.where(place < seq_len, v.cot_f[...].reshape(rows, width), 0.0)
    total = jnp.concatenate([row_sums.last(4, 0), row_sums.last(4, 1)], 0)
    d_mlp_in = d_mlp_in + total
    gain_grad = jnp.sum(d_mlp_in * h_hat, 0, keepdims=True)
    for i in range(8):
        gain[8 + i : 9 + i, :] = gain_grad[:, i * 128 : (i + 1) * 128]
    d_mid = v.grad_input
    d_mid[...] = d_out + norm_back(d_mlp_in * v.mlp_gain[...], h_hat, h_scale)

    net.finish(None)

    v.d_all[net.tp] = d_mid[...].astype(bf16)
    tokens = GatherTp(net, banks["tp0"], lambda t, half: v.d_all.at[t, pl.ds(half * half_rows, half_rows)])
    tokens.start()
    net.group = "mix"
    for g in (3, 1, 2, 0):
        mix_sums.far(g)
    net.group = None
    share = small.shape[0] // 2
    v.d_key_t[...] = jnp.zeros_like(v.d_key_t)
    v.d_value_t[...] = jnp.zeros_like(v.d_value_t)

    def softmax_of(i, _):
        q = v.query[rows_of(i), :]
        for head in (0, 1):
            v.deep[rows_of(head * 8 + i), :] = weights_of(q, head)
        return 0

    lax.fori_loop(0, 4, softmax_of, 0)
    small_first.wait_recv()
    net.sent(small_first)
    mine = pl.ds(pl.multiple_of(net.c * share, share), share)
    small[mine, :] = small[mine, :] + v.small_sib[mine, :]
    tokens.relay()
    small_y = AxisSum(net, banks["small"], small.at[mine], v.small_got.at[0], ALONG_Y)
    lax.fori_loop(4, 8, softmax_of, 0)
    tokens.share()
    net.group = "mix"
    for g in (3, 1, 2, 0):
        mix_sums.near(g)
    net.group = None
    tokens.spread()
    small[mine, :] = small_y.finish().astype(bf16)
    small_x = AxisSum(net, banks["small"], small.at[mine], v.small_got.at[1], ALONG_X)
    for sum_ in (gate, up, down):
        w_step(sum_.near_second)
    tokens.finish()

    def back(i, _):
        at = rows_of(2 * i, 2)
        d_rows = jnp.concatenate([v.d_all[2 * i], v.d_all[2 * i + 1]], 0)
        d_o = dot_nt(d_rows, v.w_out[...]).astype(bf16).astype(f32) / v.totals[at, :]
        shift = pair_sums(d_o * v.attn_o[at, :].astype(f32))
        d_o = d_o.astype(bf16)
        q = v.query[at, :]
        first = low(q.shape)
        d_q = []
        for head in (0, 1):
            own = first == (head == 0)
            d_o_head = jnp.where(own, d_o, jnp.zeros_like(d_o))
            q_head = jnp.where(own, q, jnp.zeros_like(q))
            p = v.deep[rows_of(head * 8 + 2 * i, 2), :]
            d_p = dot_nt(d_o_head, v.value[:, 0:128]) - shift[:, head * HEAD_DIM : head * HEAD_DIM + 1]
            d_s = (p.astype(f32) * d_p).astype(bf16)
            d_q.append(dot(d_s, v.key[...]))
            v.d_key_t[...] += dot_tn(q_head, d_s)
            v.d_value_t[...] += dot_tn(d_o_head, p).reshape(v.d_value_t.shape)
        d_query = (jnp.where(first, d_q[0], d_q[1]) * factor).astype(bf16).astype(f32)
        d_gained = rotate_back(d_query, v.cosine[at, :], v.sine[at, :])
        hat, scale = pair_normed(v.q_raw[at, :])
        v.gain[24:25, :] += jnp.sum(d_gained * hat, 0, keepdims=True)
        v.d_qkv[at, 0:128] = pair_norm_back(d_gained * q_gain, hat, scale).astype(bf16)
        return 0

    lax.fori_loop(0, 2, back, 0)
    blocks, block = v.grad_terms.shape[0], v.grad_terms.shape[1]
    grad_o = dot_tn(v.attn_o[...], v.d_all[...].reshape(group, width)).T
    for e in range(blocks):
        v.grad_terms[e, :, 256:384] = grad_o[e * block : (e + 1) * block].astype(bf16)
    mix_sums.turn(3)
    mix_sums.far(4)
    small[mine, :] = small_x.finish().astype(bf16)
    small_z = AxisSum(net, banks["small"], small.at[mine], v.small_got.at[2], ALONG_Z)
    lax.fori_loop(2, 4, back, 0)

    d_kv = jnp.concatenate(
        [
            v.d_key_t[:HEAD_DIM] + v.d_key_t[HEAD_DIM:],
            v.d_value_t[0] + v.d_value_t[1],
        ],
        0,
    ).T
    first = low(d_kv.shape)
    d_key = jnp.where(first, d_kv, swap(d_kv)).astype(bf16).astype(f32)
    d_gained = rotate_back(d_key, v.cosine[...], v.sine[...])
    hat, scale = pair_normed(v.k_raw[...])
    v.gain[25:26, :] = jnp.sum(d_gained * hat, 0, keepdims=True)
    d_raw = pair_norm_back(d_gained * k_gain, hat, scale)
    v.d_qkv[:, 128:256] = jnp.where(first, d_raw, d_kv).astype(bf16)

    def spread(dy):
        def one(i, _):
            t = net.tp_at(dy, 1 - i)
            v.spare[rows_of(8 + t), :] = dot_nt(v.d_qkv[rows_of(t), :], v.w_qkv[...]).astype(bf16)
            return 0

        lax.fori_loop(0, 2, one, 0)

    grad_qkv = dot(v.h_t[...], v.d_qkv[...])
    for e in range(blocks):
        v.grad_terms[e, :, 0:256] = grad_qkv[e * block : (e + 1) * block].astype(bf16)
    grad_sums = ScatterEp(
        net,
        banks["ep0"],
        lambda e, start, count: v.grad_terms.at[e, pl.ds(start, count)],
        lambda i, start, count: v.grad_landed.at[i, pl.ds(start, count)],
        block,
    )
    for g in (3, 1, 2, 0):
        grad_sums.far(g)
    sums = token_sums()
    spread(2)
    sums.across(2)
    spread(1)
    sums.across(1)
    sums.far()
    spread(-1)
    sums.across(-1)
    for g in (3, 1, 2, 0):
        grad_sums.near(g)
    sums.near_first()
    spread(0)
    sums.across(0)
    mix_sums.turn(1)
    mix_sums.turn(2)
    mix_sums.near(4)
    mix_sums.turn(0)
    sums.near_second()
    grad_sums.turn(3)
    grad_sums.far(4)
    products = (grad_qkv * v.w_qkv[...].astype(f32)).astype(bf16)
    norm_sum = dot_nt(jnp.ones((16, 256), bf16), products)[0:1] / v.norm_gain[...]
    for i in range(8):
        v.gain[i : i + 1, :] = norm_sum[:, i * 128 : (i + 1) * 128]
    gain_c = AxisSum(net, banks["gains"], v.gain.at[0:24], v.gain_got.at[0, :, 0:24], [C])
    grad_sums.turn(1)
    v.gain[0:24, :] = gain_c.finish()
    gain_y = AxisSum(net, banks["gains"], v.gain.at[0:24], v.gain_got.at[1, :, 0:24], ALONG_Y)
    grad_sums.turn(2)
    grad_sums.near(4)
    grad_sums.turn(0)
    for h in (0, 1):
        part = grad_sums.last(4, h).astype(bf16)
        v.grad_all[net.ep, h * (block // 2) : (h + 1) * (block // 2), :] = part
    spread_grads = GatherEp(net, banks["ep2"], v.grad_all, block)
    spread_grads.start()
    v.gain[0:24, :] = gain_y.finish()
    gain_x = AxisSum(net, banks["gains"], v.gain, v.gain_got.at[2], ALONG_X)

    x_hat, x_scale = normed(v.x[...].reshape(rows, width))
    total = jnp.concatenate([sums.last(0), sums.last(1)], 0)
    v.grad_input[...] = d_mid[...] + norm_back(total * v.norm_gain[...], x_hat, x_scale)
    leaving = [net.keep(v.grad_input, v.grad_input_out)]

    spread_grads.first()
    spread_grads.second(0)
    spread_grads.far()
    v.gain[...] = gain_x.finish()
    gain_z = AxisSum(net, banks["gains"], v.gain, v.gain_got.at[3], ALONG_Z)
    spread_grads.second(-1)
    spread_grads.second(1)
    spread_grads.second(2)
    small[mine, :] = small_z.finish().astype(bf16)
    small_last = net.send(small.at[mine], v.small_sib.at[mine], C, banks["small"])
    mix = jnp.concatenate([mix_sums.last(4, 0), mix_sums.last(4, 1)], 0)
    v.output[...] = jnp.where(place < seq_len, h_mid[...] + mix, 0.0)
    leaving.append(net.keep(v.output, v.output_out))
    for out, to, sum_ in (
        (v.grad_gate, v.grad_gate_out, gate),
        (v.grad_up, v.grad_up_out, up),
        (v.grad_down, v.grad_down_out, down),
    ):
        for j in (0, 1):
            out[j] = sum_.last(j)
        leaving.append(net.keep(out, to))
    v.gain_out[...] = gain_z.finish()
    small_last.wait_recv()
    other = pl.ds(pl.multiple_of((1 - net.c) * share, share), share)
    v.small_out[mine, :] = small[mine, :].astype(f32)
    v.small_out[other, :] = v.small_sib[other, :].astype(f32)
    prob_total = v.gain_out[16:24, 0:n_exp]
    loss = jnp.dot(prob_total, counts, precision=highest, preferred_element_type=f32)
    v.loss[...] = loss * (n_exp / (8.0 * nvalid * nvalid)) + jnp.zeros((8, 128), f32)
    spread_grads.finish()
    leaving.append(net.keep(v.grad_all, v.grads_out))
    for copy in leaving:
        net.kept(copy)
    net.finish()


LARGE = ("output", "grad_input", "grad_gate", "grad_up", "grad_down")


def results_kernel(*refs):
    n = len(LARGE)
    large, (grads_in, loss_in, gains, small), refs = refs[:n], refs[n : n + 4], refs[n + 4 :]
    out, made, refs = refs[:n], refs[n : n + 3], refs[n + 3 :]
    (loss, norm_gain, query_gain, key_gain, mlp_gain, router), refs = refs[:6], refs[6:]
    held, grads, parts, sems = refs[:n], refs[n], refs[n + 1 : n + 4], refs[n + 4]
    grads_read = pltpu.make_async_copy(grads_in, grads, sems.at[0, n])
    grads_read.start()
    reads = [pltpu.make_async_copy(large[i], held[i], sems.at[0, i]) for i in range(n)]
    for copy in reads:
        copy.start()
    loss[...] = loss_in[0:1, 0:1]
    for i in range(8):
        norm_gain[:, i * 128 : (i + 1) * 128] = gains[i : i + 1, :]
        mlp_gain[:, i * 128 : (i + 1) * 128] = gains[8 + i : 9 + i, :]
    query_gain[...] = gains[24:25, :]
    key_gain[...] = gains[25:26, 0:HEAD_DIM]
    router[...] = small[...]
    writes = []
    for i in range(n):
        reads[i].wait()
        writes.append(pltpu.make_async_copy(held[i], out[i], sems.at[1, i]))
        writes[i].start()
    grads_read.wait()
    blocks, block, _ = grads.shape
    for i in range(3):
        part = grads[:, :, i * 128 : (i + 1) * 128].astype(f32).reshape(blocks * block, 128)
        parts[i][...] = part if i < 2 else part.T
        writes.append(pltpu.make_async_copy(parts[i], made[i], sems.at[1, n + i]))
        writes[n + i].start()
    for copy in writes:
        copy.wait()


def local(
    layer_input,
    lengths,
    routes,
    norm_gain,
    w_query,
    w_keyval,
    query_gain,
    key_gain,
    w_out,
    mlp_gain,
    w_router,
    w_gate,
    w_up,
    w_down,
    cotangent,
):
    rows, width = layer_input.shape
    group = rows * 8
    n_exp = w_router.shape[1]
    top_k = routes.shape[1]
    units = w_down.shape[1]
    ff = units * 8
    slots = 3 * rows * top_k // (2 * n_exp)
    full = 16 * slots
    n = BATCH * slots
    block = width // 16
    cosine, sine = rotary(group)
    inputs = {
        "layer_input": (layer_input, ANY),
        "lengths": (lengths, SM),
        "routes_in": (routes.T, ANY),
        "norm_gain": (norm_gain.reshape(1, -1), VM),
        "w_query": (w_query, ANY),
        "w_keyval": (w_keyval.reshape(width, -1), ANY),
        "query_gain": (query_gain.reshape(1, -1), VM),
        "key_gain": (key_gain.reshape(1, -1), VM),
        "w_out_in": (w_out, ANY),
        "mlp_gain": (mlp_gain.reshape(1, -1), VM),
        "w_router_t": (w_router.T, VM),
        "w_gate": (w_gate.transpose(0, 2, 1), ANY),
        "w_up": (w_up.transpose(0, 2, 1), ANY),
        "w_down": (w_down, ANY),
        "cotangent": (cotangent, ANY),
        "cosine_in": (jnp.asarray(cosine), ANY),
        "sine_in": (jnp.asarray(sine), ANY),
    }
    outputs = {
        "output_out": (shaped((rows, width), f32), ANY),
        "grad_input_out": (shaped((rows, width), f32), ANY),
        "grad_gate_out": (shaped((2, units, width), f32), ANY),
        "grad_up_out": (shaped((2, units, width), f32), ANY),
        "grad_down_out": (shaped((2, units, width), f32), ANY),
        "grads_out": (shaped((16, block, 384), bf16), ANY),
        "loss": (shaped((8, 128), f32), VM),
        "gain_out": (shaped((32, 128), f32), VM),
        "small_out": (shaped((n_exp, width), f32), VM),
    }
    eight = pltpu.VMEM((8, rows, width), bf16)
    sixteen = pltpu.VMEM((16, rows, width), bf16)
    row_bf = pltpu.VMEM((group, 128), bf16)
    row_f = pltpu.VMEM((group, 128), f32)
    piece = pltpu.VMEM((4, 4, 8, rows), f32)
    by_expert = pltpu.VMEM((n_exp, rows), f32)
    scratch = {
        "w_qkv": pltpu.VMEM((width, 256), bf16),
        "w_out": pltpu.VMEM((128, width), bf16),
        "cosine": row_f,
        "sine": row_f,
        "routes": pltpu.VMEM((top_k, 16 * group), jnp.int32),
        "w": pltpu.VMEM((2, 3 * ff, width), bf16),
        "k_gain": pltpu.VMEM((1, 128), f32),
        "output": pltpu.VMEM((rows, width), f32),
        "grad_input": pltpu.VMEM((rows, width), f32),
        "grad_query": row_f,
        "grad_keyval": row_f,
        "grad_out": pltpu.VMEM((128, width), f32),
        "grad_gate": pltpu.VMEM((2, units, width), f32),
        "grad_up": pltpu.VMEM((2, units, width), f32),
        "grad_down": pltpu.VMEM((2, units, width), f32),
        "h_t": pltpu.VMEM((width, group), bf16),
        "spare": pltpu.VMEM((16 * rows, width), bf16),
        "d_all": eight,
        "query": row_bf,
        "key": row_bf,
        "value": pltpu.VMEM((group, 256), bf16),
        "k_raw": row_f,
        "attn_o": row_bf,
        "from_sib": pltpu.VMEM((4, rows, width), bf16),
        "from_far": pltpu.VMEM((2, rows // 2, width), bf16),
        "from_near": pltpu.VMEM((2, rows, width), bf16),
        "tok": sixteen,
        "cot": sixteen,
        "hits": by_expert,
        "probs": by_expert,
        "soft": by_expert,
        "d_gates": by_expert,
        "places": pltpu.VMEM((16, 2 * slots, rows), bf16),
        "counted": pltpu.VMEM((n_exp, 8, 128), f32),
        "gate_out": piece,
        "gate_mid": piece,
        "gate_got": piece,
        "back_out": piece,
        "back_mid": piece,
        "back_got": piece,
        "big": pltpu.VMEM((4 * full, width), bf16),
        "deep": pltpu.VMEM((max(3 * full, 2 * group), 2 * ff), bf16),
        "row_back": pltpu.VMEM((2, n, width), bf16),
        "landed": pltpu.VMEM((30, rows // 2, width), bf16),
        "w_sib": pltpu.VMEM((4, 3, 2, units, width), bf16),
        "w_far": pltpu.VMEM((3, 2, units, width), bf16),
        "w_near": pltpu.VMEM((2, 3, 2, units, width), bf16),
        "small": pltpu.VMEM((n_exp, width), bf16),
        "small_sib": pltpu.VMEM((n_exp, width), bf16),
        "small_got": pltpu.VMEM((3, 3, n_exp // 2, width), bf16),
        "d_qkv": pltpu.VMEM((group, 256), bf16),
        "grad_terms": pltpu.VMEM((16, block, 384), bf16),
        "grad_landed": pltpu.VMEM((30, block // 2, 384), bf16),
        "grad_all": pltpu.VMEM((16, block, 384), bf16),
        "gain": pltpu.VMEM((32, 128), f32),
        "gain_got": pltpu.VMEM((4, 3, 32, 128), f32),
        "send_sems": pltpu.SemaphoreType.DMA((SENDS,)),
        "recv_sems": pltpu.SemaphoreType.DMA((sum(BANKS.values()),)),
    }
    got = pl.pallas_call(
        lambda *refs: layer_kernel(*refs, inputs=tuple(inputs), outputs=tuple(outputs), scratch=tuple(scratch)),
        name="layer",
        out_shape=tuple(shape for shape, _ in outputs.values()),
        in_specs=[spec for _, spec in inputs.values()],
        out_specs=tuple(spec for _, spec in outputs.values()),
        scratch_shapes=list(scratch.values()),
        compiler_params=params(1, 63.9),
    )(*[array for array, _ in inputs.values()])
    got = dict(zip(outputs, got, strict=True))
    large = [got[name + "_out"] for name in LARGE] + [got["grads_out"]]
    pieces = [got[name] for name in ("loss", "gain_out", "small_out")]
    made = [(width, 128), (width, 128), (128, width)]
    sizes = [(1, 1), (1, width), (1, 128), (1, HEAD_DIM), (1, width), (n_exp, width)]
    got = pl.pallas_call(
        results_kernel,
        name="results",
        out_shape=tuple(shaped(a.shape, f32) for a in large[:-1]) + tuple(shaped(size, f32) for size in made + sizes),
        in_specs=[pl.BlockSpec(memory_space=pltpu.HBM)] * len(large) + [VM] * len(pieces),
        out_specs=(ANY,) * (len(LARGE) + len(made)) + (VM,) * len(sizes),
        scratch_shapes=[pltpu.VMEM(a.shape, a.dtype) for a in large]
        + [pltpu.VMEM(size, f32) for size in made]
        + [pltpu.SemaphoreType.DMA((2, len(large) + len(made)))],
        compiler_params=pltpu.CompilerParams(vmem_limit_bytes=62 * MIB),
    )(*large, *pieces)
    large = dict(zip(LARGE + ("grad_query", "grad_keyval", "grad_out"), got, strict=False))
    loss, grad_norm_gain, grad_query_gain, grad_key_gain, grad_mlp_gain, grad_router = got[len(large) :]
    return (
        large["output"],
        large["grad_input"],
        loss.reshape(()),
        grad_norm_gain.reshape(-1),
        large["grad_query"],
        large["grad_keyval"].reshape(w_keyval.shape),
        grad_query_gain.reshape(-1),
        grad_key_gain.reshape(-1),
        large["grad_out"],
        grad_mlp_gain.reshape(-1),
        grad_router.T,
        large["grad_gate"].transpose(0, 2, 1),
        large["grad_up"].transpose(0, 2, 1),
        large["grad_down"],
    )


def solution(mesh):
    in_specs = (
        P(("ep", "tp"), None),
        P(),
        P(),
        P(),
        P(None, "tp"),
        P(None, "tp", None),
        P("tp"),
        P("tp"),
        P("tp", None),
        P(),
        P(),
        P("ep", None, "tp"),
        P("ep", None, "tp"),
        P("ep", "tp", None),
        P(("ep", "tp"), None),
    )
    out_specs = (
        P(("ep", "tp"), None),
        P(("ep", "tp"), None),
        P(),
        P(),
        P(None, "tp"),
        P(None, "tp", None),
        P("tp"),
        P("tp"),
        P("tp", None),
        P(),
        P(),
        P("ep", None, "tp"),
        P("ep", None, "tp"),
        P("ep", "tp", None),
    )
    return jax.shard_map(local, mesh=mesh, in_specs=in_specs, out_specs=out_specs, check_vma=False)
```
